256 devices in a mesh: plan: 32 (over z_hi, x, core), layer: 8 (over z_lo, y).
Axes of the slice: x: 4, y: 4, z: 8 (z_hi: 4, z_lo: 2; z = z_hi * 2 + z_lo), core: 2. Of those that a mesh axis runs over, the one named last changes fastest.
Arguments:
- dual_block: float32 [8, 32, 1024, 1024], P('layer', 'plan'), may hold values from -1 to 6, as said below
- start: float32 [8, 32, 8, 1024], P('layer', 'plan'), may hold values from -6 to 6
- load: float32 [8, 32, 8, 1024], P('layer', 'plan'), may hold values from -40 to 40
- partners: int32 [32, 6], P('plan'), may hold values from 0 to 31, as said below
- jump_rows: int32 [8, 32, 6, 32], P('layer', 'plan'), may hold values from 128 to 895, as said below
- counts: int32 [8, 32, 6], P('layer', 'plan'), may hold values from 16 to 32, as said below
- contact: int32 [8, 32, 1024], P('layer', 'plan'), may hold values 0 or 1
Outputs:
- multipliers: float32 [8, 32, 8, 1024], P('layer', 'plan')
- gradient: float32 [8, 32, 8, 1024], P('layer', 'plan')
The draws below stay inside these ranges and needn't reach their ends.
Inputs may be any that keep to these rules, and one draw needn't show every extreme that they name: `dual_block`: every block is symmetric positive definite. In every round the partners form a perfect matching of the 32 subdomains with nobody paired to itself, and no pair meets in two rounds. `jump_rows`: the 192 rows of one subdomain are distinct and lie outside its first and last 128 rows; row k of a subdomain's block for round r meets row k of its partner's block. `counts`: both partners of a round have the same count; rows at position count or beyond are padding; every count of round 0 is 32.
All inputs are finite; a program needn't handle non-finite values. No bound on the sum of `contact` on one device may be relied on, other than what follows from the above.
Results may differ from the reference program's by a relative error of at most 0.0001.
Values sent between devices are 32-bit elements; how exact they have to be, the bound alone decides.
No kernel may reach another device: no remote copies, remote signals or barrier semaphores. Data moves between devices by JAX's collectives and lax.ppermute only.
A program may use at most 64 MiB of HBM per device.

```python
import jax
import jax.numpy as jnp
from jax import lax

M = 1024
LOADS = 8
FACE = 128
JR = 32
ROUNDS = 6
ITERS = 4
PLANS = 32
LAYERS = 8


def matching_table(key):
    relabel = jax.random.permutation(jax.random.fold_in(key, 11), PLANS).astype(jnp.int32)
    chosen = jax.random.permutation(jax.random.fold_in(key, 12), PLANS - 1)[:ROUNDS].astype(jnp.int32)
    inverse = jnp.argsort(relabel, stable=True).astype(jnp.int32)
    slots = inverse[:, None]
    pivot = chosen[None, :]
    mirror = jnp.mod(2 * pivot - slots, PLANS - 1)
    position = jnp.where(slots == PLANS - 1, pivot, jnp.where(slots == pivot, PLANS - 1, mirror))
    return relabel[position].astype(jnp.int32)


def draw_partners(key, part):
    return matching_table(key)


def draw_counts(key, part):
    partner_ids = matching_table(key)
    lower = jnp.minimum(jnp.arange(PLANS, dtype=jnp.int32)[:, None], partner_ids)
    drawn = jax.random.randint(jax.random.fold_in(key, 13), (LAYERS, ROUNDS, PLANS), JR // 2, JR + 1)
    picked = drawn[:, jnp.arange(ROUNDS)[None, :], lower]
    return picked.at[:, :, 0].set(JR).astype(jnp.int32)


def draw_jump_rows(key, part):
    keys = jax.random.split(jax.random.fold_in(key, 14), LAYERS * PLANS)
    chosen = jax.vmap(lambda one_key: jax.random.permutation(one_key, M - 2 * FACE)[:ROUNDS * JR])(keys)
    return (chosen + FACE).reshape(LAYERS, PLANS, ROUNDS, JR).astype(jnp.int32)


def draw_dual_block(key, part):
    normal_part = jax.random.normal(jax.random.fold_in(key, 21), (LAYERS, PLANS, M, M), jnp.float32)
    symmetric = (normal_part + jnp.swapaxes(normal_part, 2, 3)) / jnp.sqrt(2.0)
    off_scale = 0.7
    diagonal = jax.random.uniform(jax.random.fold_in(key, 22), (LAYERS, PLANS, M), jnp.float32, 2.0, 4.0)
    identity = jnp.eye(M, dtype=jnp.float32)
    off_diag = symmetric * (off_scale / jnp.sqrt(1.0 * M)) * (1.0 - identity)
    return off_diag + diagonal[:, :, :, None] * identity


def draw_load(key, part):
    depth = jnp.arange(LAYERS, dtype=jnp.float32) / max(LAYERS - 1, 1)
    ramp = (1.0 + 2.0 * depth)[:, None, None, None]
    values = jnp.clip(jax.random.normal(jax.random.fold_in(key, 31), (LAYERS, PLANS, LOADS, M), jnp.float32), -4.0, 4.0)
    return values * ramp


def touch_ends(result, key, smallest, top_value):
    place = [jax.random.randint(jax.random.fold_in(key, axis), (), 0, length) for axis, length in enumerate(result.shape)]
    widest = result.shape.index(max(result.shape))
    beside = place[:widest] + [(place[widest] + 1) % result.shape[widest]] + place[widest + 1:]
    return result.at[tuple(place)].set(smallest).at[tuple(beside)].set(top_value)


def levels(key, dims, cuts, low, high):
    gain = 1.0
    for axis_at, blocks in cuts:
        steps = jax.random.uniform(jax.random.fold_in(jax.random.fold_in(key, 6), axis_at), (blocks,), jnp.float32, low / len(cuts), high / len(cuts))
        gain = gain * jnp.repeat(jnp.exp(steps), dims[axis_at] // blocks).reshape((-1,) + (1,) * (len(dims) - 1 - axis_at))
    return gain


def scatter_about(rng, dims, scale, most, shards=(), held_as=jnp.bfloat16):
    entries = jax.random.normal(rng, dims, jnp.float32) * scale
    if len(shards) > 0:
        entries = levels(rng, dims, shards, -0.22, 0.18) * entries
    return jnp.clip(entries, min=-most, max=most).astype(held_as)


def setup_inputs(seed: int = 0) -> dict:
    arg_keys = jax.random.split(jax.random.key(seed), 8)
    return {
        "dual_block": draw_dual_block(jax.random.fold_in(arg_keys[7], 71), 0),
        "start": scatter_about(arg_keys[1], (LAYERS, PLANS, LOADS, M), 1.0, 6.0, ((0, 8), (1, 32)), jnp.float32),
        "load": draw_load(jax.random.fold_in(arg_keys[7], 71), 0),
        "partners": draw_partners(jax.random.fold_in(arg_keys[7], 71), 0),
        "jump_rows": draw_jump_rows(jax.random.fold_in(arg_keys[7], 71), 0),
        "counts": draw_counts(jax.random.fold_in(arg_keys[7], 71), 0),
        "contact": touch_ends((jax.random.randint(arg_keys[6], (LAYERS, PLANS, M), 0, 2) < 1).astype(jnp.int32), jax.random.fold_in(arg_keys[6], 1), 0, 1),
    }


highest = lax.Precision.HIGHEST
coupling = 1.0


def add_rows(total, indices, values):
    return total.at[:, indices].add(values)


def apply_dual(field, dual_block, partners, jump_rows, valid_mask):
    local_term = jnp.einsum("lpnm,lpmk->lpnk", field, dual_block, precision=highest)
    layer_count, plan_count, load_count, width = field.shape
    zeros_edge = jnp.zeros_like(field[:1, :, :, :FACE])
    from_below = jnp.concatenate([zeros_edge, field[:-1, :, :, width - FACE:]], axis=0)
    from_above = jnp.concatenate([field[1:, :, :, :FACE], zeros_edge], axis=0)
    middle = jnp.zeros((layer_count, plan_count, load_count, width - 2 * FACE), jnp.float32)
    neighbour = jnp.concatenate([from_below, middle, from_above], axis=3)
    positions = jnp.arange(width)
    edge_mask = (positions < FACE) | (positions >= width - FACE)
    face_term = jnp.where(edge_mask, field, 0.0) - neighbour
    flat_rows = jump_rows.reshape(layer_count, plan_count, 1, ROUNDS * JR).astype(jnp.int32)
    flat_rows = jnp.broadcast_to(flat_rows, (layer_count, plan_count, load_count, ROUNDS * JR))
    gathered = jnp.take_along_axis(field, flat_rows, axis=3).reshape(layer_count, plan_count, load_count, ROUNDS, JR)
    partner_vals = jnp.stack(
        [jnp.take(gathered[:, :, :, r, :], partners[:, r].astype(jnp.int32), axis=1) for r in range(ROUNDS)],
        axis=3)
    jump_diff = (gathered - partner_vals) * valid_mask[:, :, None, :, :]
    jump_term = jax.vmap(jax.vmap(add_rows))(
        jnp.zeros_like(field),
        jump_rows.reshape(layer_count, plan_count, ROUNDS * JR).astype(jnp.int32),
        jump_diff.reshape(layer_count, plan_count, load_count, ROUNDS * JR))
    return local_term + coupling * (face_term + jump_term)


def reference(dual_block, start, load, partners, jump_rows, counts, contact):
    valid_mask = (jnp.arange(JR)[None, None, None, :] < counts[:, :, :, None]).astype(jnp.float32)
    is_contact = (contact == 1)[:, :, None, :]
    multipliers = start
    gradient = start
    for iteration in range(ITERS):
        gradient = apply_dual(multipliers, dual_block, partners, jump_rows, valid_mask) - load
        image = apply_dual(gradient, dual_block, partners, jump_rows, valid_mask)
        grad_sq = jnp.sum(gradient * gradient, axis=(0, 1, 3))
        curvature = jnp.sum(gradient * image, axis=(0, 1, 3))
        step_size = (grad_sq + 1e-6) / (curvature + 1e-6)
        moved = multipliers - step_size[None, None, :, None] * gradient
        multipliers = jnp.where(is_contact, jnp.maximum(moved, 0.0), moved)
    return multipliers, gradient
```

```python
import functools

import jax
import jax.numpy as jnp
from jax import lax
from jax.experimental import pallas as pl
from jax.experimental.pallas import tpu as pltpu
from jax.sharding import PartitionSpec as P

FACE = 128
JR = 32
ROUNDS = 6
ITERS = 4
LANES = 128
JW = 256
F32 = jnp.float32
BF16 = jnp.bfloat16

VMEM = pl.BlockSpec(memory_space=pltpu.VMEM)
SMEM = pl.BlockSpec(memory_space=pltpu.SMEM)


def shape(*dims, dtype=F32):
    return jax.ShapeDtypeStruct(dims, dtype)


def call(body, name, outs, specs, limit, flops=0, moved=0):
    return pl.pallas_call(
        body,
        name=name,
        out_shape=outs,
        in_specs=specs,
        out_specs=jax.tree.map(lambda _: VMEM, outs),
        compiler_params=pltpu.CompilerParams(vmem_limit_bytes=limit * 2**20),
        cost_estimate=pl.CostEstimate(flops=flops, bytes_accessed=moved, transcendentals=0),
    )


def pieces(value, count):
    parts = []
    for _ in range(count):
        part = value.astype(BF16).astype(F32)
        parts.append(part)
        value = value - part
    return parts


def dense(field, high, low):
    lhs = jnp.concatenate(pieces(field, 2), axis=0).astype(BF16)
    total = jnp.dot(lhs, high, preferred_element_type=F32)
    total = total + jnp.dot(lhs, low, preferred_element_type=F32)
    return total[:8] + total[8:]


def pick(field, onehot, *extra):
    lhs = jnp.concatenate(pieces(field, 3) + list(extra), axis=0).astype(BF16)
    out = jnp.dot(lhs, onehot, preferred_element_type=F32)
    return [out[:8] + out[8:16] + out[16:24]] + [
        out[24 + 8 * i : 32 + 8 * i] for i in range(len(extra))
    ]


def spread(jumps, onehot):
    lhs = jnp.concatenate(pieces(jumps, 3), axis=0).astype(BF16)
    out = lax.dot_general(lhs, onehot, (((1,), (1,)), ((), ())), preferred_element_type=F32)
    return out[:8] + out[8:16] + out[16:24]


def address(out_ref, partners_ref, *jumps):
    out_ref[...] = jnp.zeros_like(out_ref)
    for r in range(ROUNDS):
        group = (r * JR) // LANES
        block = jnp.concatenate(
            [jump[:, group * LANES : (group + 1) * LANES] for jump in jumps], axis=0
        )
        out_ref[pl.ds(partners_ref[0, r], 1)] = block[None]


def arrived(in_ref, partners_ref):
    height = in_ref.shape[1]
    place = lax.broadcasted_iota(jnp.int32, (height, LANES), 1) // JR
    groups = []
    for first in range(0, JW // JR, LANES // JR):
        total = jnp.zeros((height, LANES), F32)
        for r in range(first, min(first + LANES // JR, ROUNDS)):
            block = in_ref[pl.ds(partners_ref[0, r], 1)][0]
            total = jnp.where(place == r - first, block, total)
        groups.append(total)
    return jnp.concatenate(groups, axis=1)


def prepare(x_ref, contact_ref, rows_ref, partners_ref, counts_ref,
            onehot_ref, valid_ref, own_ref, out_ref, first_ref, last_ref):
    x = x_ref[...]
    rows = jnp.concatenate(
        [rows_ref[r : r + 1, :] for r in range(ROUNDS)]
        + [jnp.full((1, JW - ROUNDS * JR), -1, jnp.int32)],
        axis=1,
    )
    hit = lax.broadcasted_iota(jnp.int32, (x.shape[1], JW), 0) == rows
    onehot = jnp.where(hit, 1.0, 0.0).astype(BF16)
    onehot_ref[...] = onehot
    lane = lax.broadcasted_iota(jnp.int32, (8, JW), 1)
    valid = jnp.zeros((8, JW), F32)
    for r in range(ROUNDS):
        inside = (lane >= r * JR) & (lane < r * JR + counts_ref[0, r])
        valid = jnp.where(inside, 1.0, valid)
    valid_ref[...] = valid
    contact = jnp.broadcast_to(jnp.where(contact_ref[...] == 1, 1.0, 0.0), x.shape)
    own, own_contact = pick(x, onehot, contact)
    own_ref[...] = jnp.concatenate([own, own_contact], axis=0)
    address(out_ref, partners_ref, own, own_contact)
    both = jnp.concatenate([x, contact], axis=0)
    first_ref[...] = both[:, :FACE]
    last_ref[...] = both[:, x.shape[1] - FACE :]


def split_dense(block_ref, x_ref, high_ref, low_ref, image_ref):
    block = block_ref[...]
    high = block.astype(BF16)
    low = (block - high.astype(F32)).astype(BF16)
    high_ref[...] = high
    low_ref[...] = low
    image_ref[...] = dense(x_ref[...], high, low)


def with_coupling(image, x, load, own, far, below, above, valid, onehot):
    width = x.shape[1]
    total = image + spread(valid * (own - far), onehot) - load
    head = total[:, :FACE] + (x[:, :FACE] - below)
    tail = total[:, width - FACE :] + (x[:, width - FACE :] - above)
    return jnp.concatenate([head, total[:, FACE : width - FACE], tail], axis=1)


def give_gradient(gradient, onehot, partners_ref, g_ref, gown_ref, out_ref, first_ref, last_ref):
    width = gradient.shape[1]
    g_ref[...] = gradient
    first_ref[...] = gradient[:, :FACE]
    last_ref[...] = gradient[:, width - FACE :]
    (own,) = pick(gradient, onehot)
    gown_ref[...] = own
    address(out_ref, partners_ref, own)


def first_gradient(partners_ref, image_ref, x_ref, load_ref, own_ref, in_ref, below_ref, above_ref,
                   valid_ref, onehot_ref,
                   g_ref, gown_ref, out_ref, first_ref, last_ref, far_ref):
    far = arrived(in_ref, partners_ref)
    far_ref[...] = far
    onehot = onehot_ref[...]
    gradient = with_coupling(
        image_ref[...], x_ref[...], load_ref[...], own_ref[:8], far[:8], below_ref[:8],
        above_ref[:8], valid_ref[...], onehot,
    )
    give_gradient(gradient, onehot, partners_ref, g_ref, gown_ref, out_ref, first_ref, last_ref)


def local_sums(g_ref, high_ref, low_ref, sums_ref):
    g = g_ref[...]
    image = dense(g, high_ref[...], low_ref[...])
    square = jnp.sum(g * g, axis=1, keepdims=True)
    curvature = jnp.sum(g * image, axis=1, keepdims=True)
    sums_ref[...] = jnp.concatenate(
        [jnp.broadcast_to(square, (8, LANES)), jnp.broadcast_to(curvature, (8, LANES))], axis=0
    )


def add_coupling(partners_ref, sums_ref, gown_ref, in_ref, first_ref, last_ref, below_ref,
                 above_ref, valid_ref, all_ref, gfar_ref):
    far = arrived(in_ref, partners_ref)
    gfar_ref[...] = far
    own = gown_ref[...]
    first, last = first_ref[...], last_ref[...]
    jump = valid_ref[...] * own * (own - far)
    terms = first * (first - below_ref[...]) + last * (last - above_ref[...])
    terms = terms + jump[:, :LANES] + jump[:, LANES:]
    curvature = sums_ref[8:] + jnp.sum(terms, axis=1, keepdims=True)
    lane = lax.broadcasted_iota(jnp.int32, (8, LANES), 1)
    row = lax.broadcasted_iota(jnp.int32, (8, LANES), 0)
    both = jnp.where(lane == row, sums_ref[:8], 0.0) + jnp.where(lane == row + 8, curvature, 0.0)
    line = jnp.sum(both, axis=0, keepdims=True)
    all_ref[...] = jnp.broadcast_to(line, all_ref.shape)


def step_of(all_ref):
    line = jnp.sum(all_ref[...], axis=0, keepdims=True)
    line = jnp.broadcast_to(line, (8, LANES))
    lane = lax.broadcasted_iota(jnp.int32, (8, LANES), 1)
    row = lax.broadcasted_iota(jnp.int32, (8, LANES), 0)
    square = jnp.sum(jnp.where(lane == row, line, 0.0), axis=1, keepdims=True)
    curvature = jnp.sum(jnp.where(lane == row + 8, line, 0.0), axis=1, keepdims=True)
    return (square + 1e-6) / (curvature + 1e-6)


def moved(x, g, step, contact):
    out = x - step * g
    return jnp.where(contact == 1, jnp.maximum(out, 0.0), out)


def advance(partners_ref, all_ref, x_ref, g_ref, contact_ref, load_ref,
            own_ref, gown_ref, far_ref, gfar_ref, below_ref, gbelow_ref, above_ref, gabove_ref,
            valid_ref, onehot_ref, high_ref, low_ref,
            g_out, gown_out, out_ref, first_ref, last_ref,
            x_out, own_out, far_out, below_out, above_out):
    step = step_of(all_ref)
    x = moved(x_ref[...], g_ref[...], step, contact_ref[...])
    x_out[...] = x
    halo = []
    for held_ref, slope_ref, held_out in (
        (own_ref, gown_ref, own_out), (far_ref, gfar_ref, far_out),
        (below_ref, gbelow_ref, below_out), (above_ref, gabove_ref, above_out),
    ):
        flags = held_ref[8:]
        value = moved(held_ref[:8], slope_ref[...], step, flags)
        held_out[...] = jnp.concatenate([value, flags], axis=0)
        halo.append(value)
    onehot = onehot_ref[...]
    image = dense(x, high_ref[...], low_ref[...])
    gradient = with_coupling(image, x, load_ref[...], *halo, valid_ref[...], onehot)
    give_gradient(gradient, onehot, partners_ref, g_out, gown_out, out_ref, first_ref, last_ref)


def finish(all_ref, x_ref, g_ref, contact_ref, x_out):
    x_out[...] = moved(x_ref[...], g_ref[...], step_of(all_ref), contact_ref[...])


def swap(outgoing):
    return lax.all_to_all(outgoing, "plan", split_axis=0, concat_axis=0, tiled=True)


def neighbours(first, last):
    layers = lax.axis_size("layer")
    up = [(i, i + 1) for i in range(layers - 1)]
    down = [(j, i) for i, j in up]
    return lax.ppermute(last, "layer", up), lax.ppermute(first, "layer", down)


def shards(dual_block, start, load, partners, jump_rows, counts, contact):
    block, x, target = dual_block[0, 0], start[0, 0], load[0, 0]
    rows, amounts, flags = jump_rows[0, 0], counts[0], contact[0]
    loads, width = x.shape
    plans = lax.axis_size("plan")
    devices = plans * lax.axis_size("layer")
    field, jump, face = shape(loads, width), shape(loads, JW), shape(loads, FACE)
    parcel = shape(plans, loads, LANES)
    jump2, face2, parcel2 = shape(2 * loads, JW), shape(2 * loads, FACE), shape(plans, 2 * loads, LANES)
    half = shape(width, width, dtype=BF16)
    flops = 4 * 16 * width * width

    onehot, valid, own, out, first, last = call(
        prepare, "prepare",
        (shape(width, JW, dtype=BF16), jump, jump2, parcel2, face2, face2),
        [VMEM, VMEM, VMEM, SMEM, SMEM], 8,
    )(x, flags, rows, partners, amounts)
    incoming = swap(out)
    below, above = neighbours(first, last)
    high, low, image = call(
        split_dense, "split_dense", (half, half, field), [VMEM, VMEM], 24, flops, 12 * width * width,
    )(block, x)
    g, gown, out, first, last, far = call(
        first_gradient, "first_gradient", (field, jump, parcel, face, face, jump2),
        [SMEM] + [VMEM] * 9, 8,
    )(partners, image, x, target, own, incoming, below, above, valid, onehot)

    for iteration in range(ITERS):
        incoming = swap(out)
        gbelow, gabove = neighbours(first, last)
        sums = call(
            local_sums, "local_sums", shape(2 * loads, LANES), [VMEM] * 3, 16, flops, 4 * width * width,
        )(g, high, low)
        everyone, gfar = call(
            add_coupling, "add_coupling", (shape(devices, LANES), jump), [SMEM] + [VMEM] * 8, 8,
        )(partners, sums, gown, incoming, first, last, gbelow, gabove, valid)
        everyone = lax.all_to_all(everyone, ("plan", "layer"), split_axis=0, concat_axis=0, tiled=True)
        if iteration == ITERS - 1:
            x = call(finish, "finish", field, [VMEM] * 4, 8)(everyone, x, g, flags)
            break
        g, gown, out, first, last, x, own, far, below, above = call(
            advance, "advance",
            (field, jump, parcel, face, face, field, jump2, jump2, face2, face2),
            [SMEM] + [VMEM] * 17, 16, flops, 4 * width * width,
        )(partners, everyone, x, g, flags, target, own, gown, far, gfar, below, gbelow, above, gabove,
          valid, onehot, high, low)
    return x[None, None], g[None, None]


def solution(mesh):
    in_specs = (
        P("layer", "plan", None, None),
        P("layer", "plan", None, None),
        P("layer", "plan", None, None),
        P("plan", None),
        P("layer", "plan", None, None),
        P("layer", "plan", None),
        P("layer", "plan", None),
    )
    out_specs = (P("layer", "plan", None, None), P("layer", "plan", None, None))
    return jax.shard_map(shards, mesh=mesh, in_specs=in_specs, out_specs=out_specs, check_vma=False)
```

```python
import functools

import jax
import jax.numpy as jnp
from jax import lax
from jax.experimental import pallas as pl
from jax.experimental.pallas import tpu as pltpu
from jax.sharding import PartitionSpec as P

FACE = 128
JR = 32
ROUNDS = 6
ITERS = 4
LANES = 128
JW = 256
SQUARE, CURVATURE = 64, 65
F32 = jnp.float32
BF16 = jnp.bfloat16

VMEM = pl.BlockSpec(memory_space=pltpu.VMEM)
SMEM = pl.BlockSpec(memory_space=pltpu.SMEM)


def shape(*dims, dtype=F32):
    return jax.ShapeDtypeStruct(dims, dtype)


def call(body, name, outs, specs, limit, flops=0, moved=0):
    return pl.pallas_call(
        body,
        name=name,
        out_shape=outs,
        in_specs=specs,
        out_specs=jax.tree.map(lambda _: VMEM, outs),
        compiler_params=pltpu.CompilerParams(vmem_limit_bytes=limit * 2**20),
        cost_estimate=pl.CostEstimate(flops=flops, bytes_accessed=moved, transcendentals=0),
    )


def pieces(value, count):
    parts = []
    for _ in range(count):
        part = value.astype(BF16).astype(F32)
        parts.append(part)
        value = value - part
    return parts


def dense(field, high, low):
    lhs = jnp.concatenate(pieces(field, 2), axis=0).astype(BF16)
    total = jnp.dot(lhs, high, preferred_element_type=F32)
    total = total + jnp.dot(lhs, low, preferred_element_type=F32)
    return total[:8] + total[8:]


def pick(field, onehot, *extra):
    lhs = jnp.concatenate(pieces(field, 3) + list(extra), axis=0).astype(BF16)
    out = jnp.dot(lhs, onehot, preferred_element_type=F32)
    return [out[:8] + out[8:16] + out[16:24]] + [
        out[24 + 8 * i : 32 + 8 * i] for i in range(len(extra))
    ]


def spread(jumps, onehot):
    lhs = jnp.concatenate(pieces(jumps, 3), axis=0).astype(BF16)
    out = lax.dot_general(lhs, onehot, (((1,), (1,)), ((), ())), preferred_element_type=F32)
    return out[:8] + out[8:16] + out[16:24]


def arrived(in_ref, partners_ref, wide):
    height = in_ref.shape[1]
    place = lax.broadcasted_iota(jnp.int32, (height, LANES), 1) // JR
    groups = []
    for first in range(0, JW // JR, LANES // JR):
        total = jnp.zeros((height, LANES), F32)
        at = first * JR if wide else 0
        for r in range(first, min(first + LANES // JR, ROUNDS)):
            block = in_ref[partners_ref[0, r], :, at : at + LANES]
            total = jnp.where(place == r - first, block, total)
        groups.append(total)
    return jnp.concatenate(groups, axis=1)


def prepare(x_ref, contact_ref, rows_ref, partners_ref, counts_ref,
            onehot_ref, valid_ref, own_ref, out_ref, first_ref, last_ref):
    x = x_ref[...]
    rows = jnp.concatenate(
        [rows_ref[r : r + 1, :] for r in range(ROUNDS)]
        + [jnp.full((1, JW - ROUNDS * JR), -1, jnp.int32)],
        axis=1,
    )
    hit = lax.broadcasted_iota(jnp.int32, (x.shape[1], JW), 0) == rows
    onehot = jnp.where(hit, 1.0, 0.0).astype(BF16)
    onehot_ref[...] = onehot
    lane = lax.broadcasted_iota(jnp.int32, (8, JW), 1)
    valid = jnp.zeros((8, JW), F32)
    for r in range(ROUNDS):
        inside = (lane >= r * JR) & (lane < r * JR + counts_ref[0, r])
        valid = jnp.where(inside, 1.0, valid)
    valid_ref[...] = valid
    contact = jnp.broadcast_to(jnp.where(contact_ref[...] == 1, 1.0, 0.0), x.shape)
    own, own_contact = pick(x, onehot, contact)
    own_ref[...] = jnp.concatenate([own, own_contact], axis=0)
    short = lax.broadcasted_iota(jnp.int32, (8, LANES), 1)
    names = jnp.zeros((8, LANES), jnp.int32)
    for r in range(ROUNDS):
        names = jnp.where(short == r, partners_ref[0, r], names)
    names = names.astype(F32)
    row = lax.broadcasted_iota(jnp.int32, (8, LANES), 0)
    out_ref[...] = jnp.broadcast_to(
        jnp.concatenate([jnp.zeros((8, LANES), F32), names], axis=0)[None], out_ref.shape
    )
    for r in range(ROUNDS):
        group = (r * JR) // LANES
        at = slice(group * LANES, (group + 1) * LANES)
        low = jnp.where(row == 7, names, own_contact[:, at])
        out_ref[pl.ds(partners_ref[0, r], 1)] = jnp.concatenate([own[:, at], low], axis=0)[None]
    both = jnp.concatenate([x, contact], axis=0)
    first_ref[...] = both[:, :FACE]
    last_ref[...] = both[:, x.shape[1] - FACE :]


def split_dense(block_ref, x_ref, halves_ref, image_ref):
    block = block_ref[...]
    high = block.astype(BF16)
    low = (block - high.astype(F32)).astype(BF16)
    halves_ref[0] = high
    halves_ref[1] = low
    image_ref[...] = dense(x_ref[...], high, low)


def with_coupling(image, x, load, own, far, below, above, valid, onehot):
    width = x.shape[1]
    total = image + spread(valid * (own - far), onehot) - load
    head = total[:, :FACE] + (x[:, :FACE] - below)
    tail = total[:, width - FACE :] + (x[:, width - FACE :] - above)
    return jnp.concatenate([head, total[:, FACE : width - FACE], tail], axis=1)


def give_gradient(gradient, onehot, g_ref, gown_ref, last_ref):
    g_ref[...] = gradient
    last_ref[...] = gradient[:, gradient.shape[1] - FACE :]
    gown_ref[...] = pick(gradient, onehot)[0]


def first_gradient(partners_ref, image_ref, x_ref, load_ref, own_ref, in_ref, below_ref, above_ref,
                   valid_ref, onehot_ref, g_ref, gown_ref, last_ref, far_ref, table_ref):
    far = arrived(in_ref, partners_ref, False)
    flags = jnp.broadcast_to(far[8:9], far[8:].shape)
    far_ref[...] = jnp.concatenate([far[:8], flags], axis=0)
    for p in range(table_ref.shape[0]):
        table_ref[p : p + 1, :] = in_ref[p, 15:16, :8].astype(jnp.int32)
    onehot = onehot_ref[...]
    gradient = with_coupling(
        image_ref[...], x_ref[...], load_ref[...], own_ref[:8], far[:8], below_ref[:8],
        above_ref[:8], valid_ref[...], onehot,
    )
    give_gradient(gradient, onehot, g_ref, gown_ref, last_ref)


def local_sums(g_ref, halves_ref, sums_ref):
    g = g_ref[...]
    image = dense(g, halves_ref[0], halves_ref[1])
    width = g.shape[1]
    terms = g * image
    edges = g[:, :FACE] * g[:, :FACE] + g[:, width - FACE :] * g[:, width - FACE :]
    square = jnp.sum(g * g, axis=1, keepdims=True)
    curvature = jnp.sum(terms, axis=1, keepdims=True) + jnp.sum(edges, axis=1, keepdims=True)
    lane = lax.broadcasted_iota(jnp.int32, (8, LANES), 1)
    sums_ref[...] = jnp.where(lane == SQUARE, square, jnp.where(lane == CURVATURE, curvature, 0.0))


def announce(sums_ref, g_ref, gown_ref, valid_ref, below_ref, out_ref):
    own = valid_ref[...] * gown_ref[...]
    squares = own * own
    pairs = g_ref[:, :FACE] * below_ref[...]
    terms = squares[:, :LANES] + squares[:, LANES:] - 2.0 * pairs
    more = jnp.sum(terms, axis=1, keepdims=True)
    lane = lax.broadcasted_iota(jnp.int32, (8, LANES), 1)
    extra = sums_ref[...] + jnp.where(lane == CURVATURE, more, 0.0)
    parcel = jnp.concatenate([own[:, :LANES], own[:, LANES:] + extra], axis=1)
    out_ref[...] = jnp.broadcast_to(parcel[None], out_ref.shape)


def layer_sums(partners_ref, table_ref, in_ref, g_ref, gfar_ref, out_ref):
    gfar_ref[...] = arrived(in_ref, partners_ref, True)
    place = lax.broadcasted_iota(jnp.int32, (8, LANES), 1) // JR
    nothing = jnp.zeros((8, LANES), F32)
    products, sums = [nothing, nothing], nothing
    for p in range(in_ref.shape[0]):
        near = [in_ref[p, :, :LANES], in_ref[p, :, LANES:]]
        sums = sums + near[1]
        for group in range(2):
            far = nothing
            for r in range(4 * group, min(4 * group + 4, ROUNDS)):
                block = in_ref[table_ref[p, r], :, group * LANES : (group + 1) * LANES]
                far = jnp.where(place == r - 4 * group, block, far)
            products[group] = products[group] + near[group] * far
    cross = jnp.sum(products[0] + products[1], axis=1, keepdims=True)
    lane = lax.broadcasted_iota(jnp.int32, (8, LANES), 1)
    sums = sums - jnp.where(lane == CURVATURE, cross, 0.0)
    parcel = jnp.concatenate([g_ref[:, :FACE], sums], axis=1)
    out_ref[...] = jnp.broadcast_to(parcel[None], out_ref.shape)


def step_of(in_ref):
    total = in_ref[0, :, LANES:]
    for layer in range(1, in_ref.shape[0]):
        total = total + in_ref[layer, :, LANES:]
    square = total[:, SQUARE : SQUARE + 1]
    curvature = total[:, CURVATURE : CURVATURE + 1]
    return (square + 1e-6) / (curvature + 1e-6)


def moved(x, g, step, contact):
    out = x - step * g
    return jnp.where(contact == 1, jnp.maximum(out, 0.0), out)


def advance(layer_ref, in_ref, x_ref, g_ref, contact_ref, load_ref,
            own_ref, gown_ref, far_ref, gfar_ref, below_ref, gbelow_ref, above_ref,
            valid_ref, onehot_ref, halves_ref,
            g_out, gown_out, last_out, x_out, own_out, far_out, below_out, above_out):
    step = step_of(in_ref)
    x = moved(x_ref[...], g_ref[...], step, contact_ref[...])
    x_out[...] = x
    layers = in_ref.shape[0]
    layer = layer_ref[0, 0]
    gabove = in_ref[jnp.minimum(layer + 1, layers - 1), :, :FACE]
    gabove = jnp.where(layer < layers - 1, gabove, 0.0)
    halo = []
    for held_ref, slope, held_out in (
        (own_ref, gown_ref[...], own_out), (far_ref, gfar_ref[...], far_out),
        (below_ref, gbelow_ref[...], below_out), (above_ref, gabove, above_out),
    ):
        flags = held_ref[8:]
        value = moved(held_ref[:8], slope, step, flags)
        held_out[...] = jnp.concatenate([value, flags], axis=0)
        halo.append(value)
    onehot = onehot_ref[...]
    image = dense(x, halves_ref[0], halves_ref[1])
    gradient = with_coupling(image, x, load_ref[...], *halo, valid_ref[...], onehot)
    give_gradient(gradient, onehot, g_out, gown_out, last_out)


def finish(in_ref, x_ref, g_ref, contact_ref, x_out):
    x_out[...] = moved(x_ref[...], g_ref[...], step_of(in_ref), contact_ref[...])


def swap(outgoing, axis):
    return lax.all_to_all(outgoing, axis, split_axis=0, concat_axis=0, tiled=True)


def lift(face, step):
    layers = lax.axis_size("layer")
    return lax.ppermute(
        face, "layer", [(i, i + step) for i in range(layers) if 0 <= i + step < layers]
    )


def shards(dual_block, start, load, partners, jump_rows, counts, contact):
    block, x, target = dual_block[0, 0], start[0, 0], load[0, 0]
    rows, amounts, flags = jump_rows[0, 0], counts[0], contact[0]
    loads, width = x.shape
    plans, layers = lax.axis_size("plan"), lax.axis_size("layer")
    field, jump, face = shape(loads, width), shape(loads, JW), shape(loads, FACE)
    jump2, face2 = shape(2 * loads, JW), shape(2 * loads, FACE)
    halves_shape = shape(2, width, width, dtype=BF16)
    flops = 4 * 16 * width * width
    layer = lax.axis_index("layer").astype(jnp.int32).reshape(1, 1)

    onehot, valid, own, out, first, last = call(
        prepare, "prepare",
        (shape(width, JW, dtype=BF16), jump, jump2, shape(plans, 2 * loads, LANES), face2, face2),
        [VMEM, VMEM, VMEM, SMEM, SMEM], 8,
    )(x, flags, rows, partners, amounts)
    incoming = swap(out, "plan")
    below, above = lift(last, 1), lift(first, -1)
    halves, image = call(
        split_dense, "split_dense", (halves_shape, field), [VMEM, VMEM], 20, flops, 12 * width * width,
    )(block, x)
    g, gown, last, far, table = call(
        first_gradient, "first_gradient",
        (field, jump, face, jump2, shape(plans, 8, dtype=jnp.int32)), [SMEM] + [VMEM] * 9, 8,
    )(partners, image, x, target, own, incoming, below, above, valid, onehot)

    for iteration in range(ITERS):
        gbelow = lift(last, 1)
        sums = call(
            local_sums, "local_sums", face, [VMEM] * 2, 12, flops, 4 * width * width,
        )(g, halves)
        out = call(announce, "announce", shape(plans, loads, JW), [VMEM] * 5, 8)(
            sums, g, gown, valid, gbelow
        )
        gfar, out = call(
            layer_sums, "layer_sums", (jump, shape(layers, loads, FACE + LANES)),
            [SMEM] * 2 + [VMEM] * 2, 8,
        )(partners, table, swap(out, "plan"), g)
        incoming = swap(out, "layer")
        if iteration == ITERS - 1:
            x = call(finish, "finish", field, [VMEM] * 4, 8)(incoming, x, g, flags)
            break
        g, gown, last, x, own, far, below, above = call(
            advance, "advance", (field, jump, face, field, jump2, jump2, face2, face2),
            [SMEM] + [VMEM] * 15, 12, flops, 4 * width * width,
        )(layer, incoming, x, g, flags, target, own, gown, far, gfar, below, gbelow, above,
          valid, onehot, halves)
    return x[None, None], g[None, None]


def solution(mesh):
    in_specs = (
        P("layer", "plan", None, None),
        P("layer", "plan", None, None),
        P("layer", "plan", None, None),
        P("plan", None),
        P("layer", "plan", None, None),
        P("layer", "plan", None),
        P("layer", "plan", None),
    )
    out_specs = (P("layer", "plan", None, None), P("layer", "plan", None, None))
    return jax.shard_map(shards, mesh=mesh, in_specs=in_specs, out_specs=out_specs, check_vma=False)
```

```python
import jax
import jax.numpy as jnp
from jax import lax
from jax.experimental import pallas as pl
from jax.experimental.pallas import tpu as pltpu
from jax.sharding import PartitionSpec as P

FACE = 128
JR = 32
ROUNDS = 6
ITERS = 4
LANES = 128
JW = 256
CHUNKS = 4
NAMES = 16
SQUARE, CURVATURE = 64, 65
F32 = jnp.float32
BF16 = jnp.bfloat16

VMEM = pl.BlockSpec(memory_space=pltpu.VMEM)
SMEM = pl.BlockSpec(memory_space=pltpu.SMEM)
HBM = pl.BlockSpec(memory_space=pltpu.HBM)


def shape(*dims, dtype=F32):
    return jax.ShapeDtypeStruct(dims, dtype)


def call(body, name, outs, specs, limit, flops=0, traffic=0, scratch=()):
    return pl.pallas_call(
        body,
        name=name,
        out_shape=outs,
        in_specs=specs,
        scratch_shapes=scratch,
        out_specs=jax.tree.map(lambda _: VMEM, outs),
        compiler_params=pltpu.CompilerParams(vmem_limit_bytes=limit * 2**20),
        cost_estimate=pl.CostEstimate(flops=flops, bytes_accessed=traffic, transcendentals=0),
    )


def pieces(value, count):
    parts = []
    for _ in range(count):
        part = value.astype(BF16).astype(F32)
        parts.append(part)
        value = value - part
    return parts


def dense(field, high, low):
    lhs = jnp.concatenate(pieces(field, 2), axis=0).astype(BF16)
    total = jnp.dot(lhs, high, preferred_element_type=F32)
    total = total + jnp.dot(lhs, low, preferred_element_type=F32)
    return total[:8] + total[8:]


def pick(field, onehot, *extra):
    lhs = jnp.concatenate(pieces(field, 3) + list(extra), axis=0).astype(BF16)
    out = jnp.dot(lhs, onehot, preferred_element_type=F32)
    return [out[:8] + out[8:16] + out[16:24]] + [
        out[24 + 8 * i : 32 + 8 * i] for i in range(len(extra))
    ]


def spread(jumps, onehot):
    lhs = jnp.concatenate(pieces(jumps, 3), axis=0).astype(BF16)
    out = lax.dot_general(lhs, onehot, (((1,), (1,)), ((), ())), preferred_element_type=F32)
    return out[:8] + out[8:16] + out[16:24]


def arrived(in_ref, partners_ref):
    place = lax.broadcasted_iota(jnp.int32, (8, LANES), 1) // JR
    groups = []
    for first in range(0, JW // JR, LANES // JR):
        total = jnp.zeros((8, LANES), F32)
        at = first * JR
        for r in range(first, min(first + LANES // JR, ROUNDS)):
            block = in_ref[partners_ref[0, r], :, at : at + LANES]
            total = jnp.where(place == r - first, block, total)
        groups.append(total)
    return jnp.concatenate(groups, axis=1)


def stream_dense(field, block_ref, rows_ref, sems, keep=None):
    lhs = jnp.concatenate(pieces(field, 2), axis=0).astype(BF16)
    depth = rows_ref.shape[0] // CHUNKS
    total = jnp.zeros((lhs.shape[0], rows_ref.shape[1]), F32)
    for chunk in range(CHUNKS):
        at = slice(chunk * depth, (chunk + 1) * depth)
        chunk_copy(block_ref, rows_ref, sems, chunk).wait()
        rows = rows_ref[at, :]
        high = rows.astype(BF16)
        low = (rows - high.astype(F32)).astype(BF16)
        if keep is not None:
            keep[0, at, :] = high
            keep[1, at, :] = low
        total = total + jnp.dot(lhs[:, at], high, preferred_element_type=F32)
        total = total + jnp.dot(lhs[:, at], low, preferred_element_type=F32)
    return total[:8] + total[8:]


def chunk_copy(block_ref, rows_ref, sems, chunk):
    depth = rows_ref.shape[0] // CHUNKS
    at = pl.ds(chunk * depth, depth)
    return pltpu.make_async_copy(block_ref.at[at, :], rows_ref.at[at, :], sems.at[chunk])


def prepare(block_ref, x_hbm, load_hbm, contact_hbm, rows_hbm, partners_hbm, counts_hbm,
            onehot_ref, valid_ref, own_ref, hown_ref, h_ref, out_ref, first_ref, last_ref,
            held_ref, x_ref, load_ref, contact_ref, rows_ref, partners_ref, counts_ref, sems, more_sems):
    small = [
        pltpu.make_async_copy(source, target, more_sems.at[i])
        for i, (source, target) in enumerate((
            (rows_hbm, rows_ref), (counts_hbm, counts_ref), (x_hbm, x_ref),
            (contact_hbm, contact_ref), (partners_hbm, partners_ref), (load_hbm, load_ref),
        ))
    ]
    for copy in small:
        copy.start()
    for chunk in range(CHUNKS):
        chunk_copy(block_ref, held_ref, sems, chunk).start()
    for copy in small:
        copy.wait()
    x = x_ref[...]
    width = x.shape[1]
    rows = jnp.concatenate(
        [rows_ref[r : r + 1, :] for r in range(ROUNDS)]
        + [jnp.full((1, JW - ROUNDS * JR), -1, jnp.int32)],
        axis=1,
    )
    hit = lax.broadcasted_iota(jnp.int32, (width, JW), 0) == rows
    onehot = jnp.where(hit, 1.0, 0.0).astype(BF16)
    onehot_ref[...] = onehot
    lane = lax.broadcasted_iota(jnp.int32, (8, JW), 1)
    valid = jnp.zeros((8, JW), F32)
    for r in range(ROUNDS):
        inside = (lane >= r * JR) & (lane < r * JR + counts_ref[0, r])
        valid = jnp.where(inside, 1.0, valid)
    valid_ref[...] = valid
    contact = jnp.broadcast_to(jnp.where(contact_ref[...] == 1, 1.0, 0.0), x.shape)
    own, own_contact = pick(x, onehot, contact)
    own_ref[...] = jnp.concatenate([own, own_contact], axis=0)
    position = lax.broadcasted_iota(jnp.int32, x.shape, 1)
    edge = (position < FACE) | (position >= width - FACE)
    h = spread(valid * own, onehot) + jnp.where(edge, x, 0.0) - load_ref[...]
    h = h + stream_dense(x, block_ref, held_ref, sems)
    h_ref[...] = h
    (hown,) = pick(h, onehot)
    hown_ref[...] = hown
    out_ref[...] = jnp.zeros_like(out_ref)
    place = lax.broadcasted_iota(jnp.int32, (8, LANES), 1) // JR
    for r in range(ROUNDS):
        group, slot = divmod(r * JR, LANES)
        at = slice(group * LANES, (group + 1) * LANES)
        parcel = jnp.zeros((8, LANES), F32)
        for i, jump in enumerate((own, hown, own_contact)):
            block = pltpu.roll(jump[:, at], (i * JR) % LANES, 1) if i else jump[:, at]
            parcel = jnp.where(place == (slot // JR + i) % (LANES // JR), block, parcel)
        out_ref[partners_ref[0, r]] = parcel
    both = jnp.concatenate([x, h, contact], axis=0)
    first_ref[...] = both[:, :FACE]
    last_ref[...] = both[:, width - FACE :]


def with_coupling(image, x, load, own, far, below, above, valid, onehot):
    width = x.shape[1]
    total = image + spread(valid * (own - far), onehot) - load
    head = total[:, :FACE] + (x[:, :FACE] - below)
    tail = total[:, width - FACE :] + (x[:, width - FACE :] - above)
    return jnp.concatenate([head, total[:, FACE : width - FACE], tail], axis=1)


def lane_sum(value):
    return jnp.sum(value, axis=1, keepdims=True)


def first_gradient(partners_ref, layer_ref, block_ref, x_ref, h_ref, own_ref, hown_ref, in_ref,
                   below_in, above_in, valid_ref, onehot_ref,
                   g_ref, gown_ref, far_ref, gfar_ref, below_ref, gbelow_ref, above_ref, gabove_ref,
                   halves_ref, all_ref, held_ref, sems):
    for chunk in range(CHUNKS):
        chunk_copy(block_ref, held_ref, sems, chunk).start()
    width = x_ref.shape[1]
    place = lax.broadcasted_iota(jnp.int32, (8, LANES), 1) // JR
    parts = [[jnp.zeros((8, LANES), F32)] * 2 for _ in range(3)]
    for r in range(ROUNDS):
        group, slot = divmod(r * JR, LANES)
        parcel = in_ref[partners_ref[0, r]]
        for i in range(3):
            block = pltpu.roll(parcel, LANES - i * JR, 1) if i else parcel
            parts[i][group] = jnp.where(place == slot // JR, block, parts[i][group])
    far, hfar, far_contact = (jnp.concatenate(part, axis=1) for part in parts)
    valid = valid_ref[...]
    own = own_ref[:8]
    far_ref[...] = jnp.concatenate([far, far_contact], axis=0)
    gown = hown_ref[...] - valid * far
    gfar = hfar - valid * own
    gown_ref[...] = gown
    gfar_ref[...] = gfar
    below, above = below_in[...], above_in[...]
    below_ref[...] = jnp.concatenate([below[:8], below[16:]], axis=0)
    above_ref[...] = jnp.concatenate([above[:8], above[16:]], axis=0)
    layer = layer_ref[0, 0]
    gbelow = jnp.where(layer > 0, below[8:16] - x_ref[:, :FACE], 0.0)
    gabove = jnp.where(layer < layer_ref[0, 1] - 1, above[8:16] - x_ref[:, width - FACE :], 0.0)
    gbelow_ref[...] = gbelow
    gabove_ref[...] = gabove
    h = h_ref[...] - spread(valid * far, onehot_ref[...])
    first = h[:, :FACE] - below[:8]
    last = h[:, width - FACE :] - above[:8]
    g = jnp.concatenate([first, h[:, FACE : width - FACE], last], axis=1)
    g_ref[...] = g
    jumps = valid * gown * (gown - gfar)
    terms = first * (first - gbelow) + last * (last - gabove) + jumps[:, :LANES] + jumps[:, LANES:]
    square = lane_sum(g * g)
    curvature = lane_sum(terms) + lane_sum(g * stream_dense(g, block_ref, held_ref, sems, halves_ref))
    lane = lax.broadcasted_iota(jnp.int32, (8, LANES), 1)
    row = lax.broadcasted_iota(jnp.int32, (8, LANES), 0)
    line = jnp.where(lane == row, square, 0.0) + jnp.where(lane == row + 8, curvature, 0.0)
    line = jnp.sum(line, axis=0, keepdims=True)
    short = lax.broadcasted_iota(jnp.int32, (1, LANES), 1)
    for r in range(ROUNDS):
        name = jnp.full((1, LANES), partners_ref[0, r], jnp.int32).astype(F32)
        line = jnp.where(short == NAMES + r, name, line)
    all_ref[...] = jnp.broadcast_to(line, all_ref.shape)


def give_gradient(gradient, onehot, g_ref, gown_ref, last_ref):
    g_ref[...] = gradient
    last_ref[...] = gradient[:, gradient.shape[1] - FACE :]
    gown_ref[...] = pick(gradient, onehot)[0]


def local_sums(g_ref, halves_ref, sums_ref):
    g = g_ref[...]
    image = dense(g, halves_ref[0], halves_ref[1])
    width = g.shape[1]
    terms = g * image
    edges = g[:, :FACE] * g[:, :FACE] + g[:, width - FACE :] * g[:, width - FACE :]
    square = jnp.sum(g * g, axis=1, keepdims=True)
    curvature = jnp.sum(terms, axis=1, keepdims=True) + jnp.sum(edges, axis=1, keepdims=True)
    lane = lax.broadcasted_iota(jnp.int32, (8, LANES), 1)
    sums_ref[...] = jnp.where(lane == SQUARE, square, jnp.where(lane == CURVATURE, curvature, 0.0))


def announce(sums_ref, g_ref, gown_ref, valid_ref, below_ref, out_ref):
    own = valid_ref[...] * gown_ref[...]
    squares = own * own
    pairs = g_ref[:, :FACE] * below_ref[...]
    terms = squares[:, :LANES] + squares[:, LANES:] - 2.0 * pairs
    more = jnp.sum(terms, axis=1, keepdims=True)
    lane = lax.broadcasted_iota(jnp.int32, (8, LANES), 1)
    extra = sums_ref[...] + jnp.where(lane == CURVATURE, more, 0.0)
    parcel = jnp.concatenate([own[:, :LANES], own[:, LANES:] + extra], axis=1)
    out_ref[...] = jnp.broadcast_to(parcel[None], out_ref.shape)


def layer_sums(partners_ref, table_ref, in_ref, g_ref, gfar_ref, out_ref):
    gfar_ref[...] = arrived(in_ref, partners_ref)
    place = lax.broadcasted_iota(jnp.int32, (8, LANES), 1) // JR
    nothing = jnp.zeros((8, LANES), F32)
    products, sums = [nothing, nothing], nothing
    for p in range(in_ref.shape[0]):
        near = [in_ref[p, :, :LANES], in_ref[p, :, LANES:]]
        sums = sums + near[1]
        for group in range(2):
            far = nothing
            for r in range(4 * group, min(4 * group + 4, ROUNDS)):
                block = in_ref[table_ref[p, r], :, group * LANES : (group + 1) * LANES]
                far = jnp.where(place == r - 4 * group, block, far)
            products[group] = products[group] + near[group] * far
    cross = jnp.sum(products[0] + products[1], axis=1, keepdims=True)
    lane = lax.broadcasted_iota(jnp.int32, (8, LANES), 1)
    sums = sums - jnp.where(lane == CURVATURE, cross, 0.0)
    parcel = jnp.concatenate([g_ref[:, :FACE], sums], axis=1)
    out_ref[...] = jnp.broadcast_to(parcel[None], out_ref.shape)


def step_of(in_ref):
    total = in_ref[0, :, LANES:]
    for layer in range(1, in_ref.shape[0]):
        total = total + in_ref[layer, :, LANES:]
    square = total[:, SQUARE : SQUARE + 1]
    curvature = total[:, CURVATURE : CURVATURE + 1]
    return (square + 1e-6) / (curvature + 1e-6)


def moved(x, g, step, contact):
    out = x - step * g
    return jnp.where(contact == 1, jnp.maximum(out, 0.0), out)


def first_step(in_ref):
    line = jnp.sum(in_ref[...], axis=0, keepdims=True)
    line = jnp.broadcast_to(line, (8, LANES))
    lane = lax.broadcasted_iota(jnp.int32, (8, LANES), 1)
    row = lax.broadcasted_iota(jnp.int32, (8, LANES), 0)
    square = lane_sum(jnp.where(lane == row, line, 0.0))
    curvature = lane_sum(jnp.where(lane == row + 8, line, 0.0))
    return (square + 1e-6) / (curvature + 1e-6)


def first_advance(in_ref, *refs):
    *refs, table_ref = refs
    plans = table_ref.shape[0]
    lines = in_ref[pl.ds(0, plans, stride=in_ref.shape[0] // plans), :]
    table_ref[...] = pltpu.roll(lines, LANES - NAMES, 1)[:, :8].astype(jnp.int32)
    gabove_ref, *refs = refs
    advance_by(first_step(in_ref), gabove_ref[...], *refs)


def advance(layer_ref, in_ref, *refs):
    layers = in_ref.shape[0]
    layer = layer_ref[0, 0]
    gabove = in_ref[jnp.minimum(layer + 1, layers - 1), :, :FACE]
    gabove = jnp.where(layer < layers - 1, gabove, 0.0)
    advance_by(step_of(in_ref), gabove, *refs)


def advance_by(step, gabove, x_ref, g_ref, contact_ref, load_ref,
               own_ref, gown_ref, far_ref, gfar_ref, below_ref, gbelow_ref, above_ref,
               valid_ref, onehot_ref, halves_ref,
               g_out, gown_out, last_out, x_out, own_out, far_out, below_out, above_out):
    x = moved(x_ref[...], g_ref[...], step, contact_ref[...])
    x_out[...] = x
    halo = []
    for held_ref, slope, held_out in (
        (own_ref, gown_ref[...], own_out), (far_ref, gfar_ref[...], far_out),
        (below_ref, gbelow_ref[...], below_out), (above_ref, gabove, above_out),
    ):
        flags = held_ref[8:]
        value = moved(held_ref[:8], slope, step, flags)
        held_out[...] = jnp.concatenate([value, flags], axis=0)
        halo.append(value)
    onehot = onehot_ref[...]
    image = dense(x, halves_ref[0], halves_ref[1])
    gradient = with_coupling(image, x, load_ref[...], *halo, valid_ref[...], onehot)
    give_gradient(gradient, onehot, g_out, gown_out, last_out)


def finish(in_ref, x_ref, g_ref, contact_ref, x_out):
    x_out[...] = moved(x_ref[...], g_ref[...], step_of(in_ref), contact_ref[...])


def swap(outgoing, axis):
    return lax.all_to_all(outgoing, axis, split_axis=0, concat_axis=0, tiled=True)


def lift(face, step):
    layers = lax.axis_size("layer")
    return lax.ppermute(
        face, "layer", [(i, i + step) for i in range(layers) if 0 <= i + step < layers]
    )


def shards(dual_block, start, load, partners, jump_rows, counts, contact):
    block, x, target = dual_block[0, 0], start[0, 0], load[0, 0]
    rows, amounts, flags = jump_rows[0, 0], counts[0], contact[0]
    loads, width = x.shape
    plans, layers = lax.axis_size("plan"), lax.axis_size("layer")
    field, jump, face = shape(loads, width), shape(loads, JW), shape(loads, FACE)
    jump2, face2, face3 = shape(2 * loads, JW), shape(2 * loads, FACE), shape(3 * loads, FACE)
    flops = 4 * 16 * width * width
    layer = jnp.stack([lax.axis_index("layer"), layers]).astype(jnp.int32).reshape(1, 2)
    held = pltpu.VMEM((width, width), F32)
    chunk_sems = pltpu.SemaphoreType.DMA((CHUNKS,))

    onehot, valid, own, hown, h, out, first, last = call(
        prepare, "prepare",
        (shape(width, JW, dtype=BF16), jump, jump2, jump, field, shape(plans, loads, LANES), face3, face3),
        [HBM] * 7, 53, flops, 4 * width * width,
        [
            held, pltpu.VMEM(x.shape, F32), pltpu.VMEM(target.shape, F32),
            pltpu.VMEM(flags.shape, jnp.int32), pltpu.VMEM(rows.shape, jnp.int32),
            pltpu.SMEM(partners.shape, jnp.int32), pltpu.SMEM(amounts.shape, jnp.int32),
            chunk_sems, pltpu.SemaphoreType.DMA((6,)),
        ],
    )(block, x, target, flags, rows, partners, amounts)
    incoming = swap(out, "plan")
    below, above = lift(last, 1), lift(first, -1)
    g, gown, far, gfar, below, gbelow, above, gabove, halves, out = call(
        first_gradient, "first_gradient",
        (field, jump, jump2, jump, face2, face, face2, face,
         shape(2, width, width, dtype=BF16), shape(plans * layers, LANES)),
        [SMEM] * 2 + [HBM] + [VMEM] * 9, 48, flops, 4 * width * width, [held, chunk_sems],
    )(partners, layer, block, x, h, own, hown, incoming, below, above, valid, onehot)
    incoming = swap(out, ("plan", "layer"))

    after = (field, jump, face, field, jump2, jump2, face2, face2)
    g, gown, last, x, own, far, below, above, table = call(
        first_advance, "first_advance", after + (shape(plans, 8, dtype=jnp.int32),),
        [VMEM] * 16, 12, flops, 4 * width * width,
    )(incoming, gabove, x, g, flags, target, own, gown, far, gfar, below, gbelow, above,
      valid, onehot, halves)

    for iteration in range(1, ITERS):
        gbelow = lift(last, 1)
        sums = call(
            local_sums, "local_sums", face, [VMEM] * 2, 12, flops, 4 * width * width,
        )(g, halves)
        out = call(announce, "announce", shape(plans, loads, JW), [VMEM] * 5, 8)(
            sums, g, gown, valid, gbelow
        )
        gfar, out = call(
            layer_sums, "layer_sums", (jump, shape(layers, loads, FACE + LANES)),
            [SMEM] * 2 + [VMEM] * 2, 8,
        )(partners, table, swap(out, "plan"), g)
        incoming = swap(out, "layer")
        if iteration == ITERS - 1:
            x = call(finish, "finish", field, [VMEM] * 4, 8)(incoming, x, g, flags)
            break
        g, gown, last, x, own, far, below, above = call(
            advance, "advance", after, [SMEM] + [VMEM] * 15, 12, flops, 4 * width * width,
        )(layer, incoming, x, g, flags, target, own, gown, far, gfar, below, gbelow, above,
          valid, onehot, halves)
    return x[None, None], g[None, None]


def solution(mesh):
    in_specs = (
        P("layer", "plan", None, None),
        P("layer", "plan", None, None),
        P("layer", "plan", None, None),
        P("plan", None),
        P("layer", "plan", None, None),
        P("layer", "plan", None),
        P("layer", "plan", None),
    )
    out_specs = (P("layer", "plan", None, None), P("layer", "plan", None, None))
    return jax.shard_map(shards, mesh=mesh, in_specs=in_specs, out_specs=out_specs, check_vma=False)
```

```python
import jax
import jax.numpy as jnp
from jax import lax
from jax.experimental import pallas as pl
from jax.experimental.pallas import tpu as pltpu
from jax.sharding import PartitionSpec as P

FACE = 128
JR = 32
ROUNDS = 6
ITERS = 4
LANES = 128
JW = 256
CHUNKS = 4
NAMES = 16
SQUARE, CURVATURE = 64, 65
F32 = jnp.float32
BF16 = jnp.bfloat16

VMEM = pl.BlockSpec(memory_space=pltpu.VMEM)
SMEM = pl.BlockSpec(memory_space=pltpu.SMEM)
HBM = pl.BlockSpec(memory_space=pltpu.HBM)


def shape(*dims, dtype=F32):
    return jax.ShapeDtypeStruct(dims, dtype)


def call(body, name, outs, specs, limit, flops=0, traffic=0, scratch=()):
    return pl.pallas_call(
        body,
        name=name,
        out_shape=outs,
        in_specs=specs,
        scratch_shapes=scratch,
        out_specs=jax.tree.map(lambda _: VMEM, outs),
        compiler_params=pltpu.CompilerParams(vmem_limit_bytes=limit * 2**20),
        cost_estimate=pl.CostEstimate(flops=flops, bytes_accessed=traffic, transcendentals=0),
    )


def pieces(value, count):
    parts = []
    for _ in range(count):
        part = value.astype(BF16).astype(F32)
        parts.append(part)
        value = value - part
    return parts


def dense(field, high, low):
    lhs = jnp.concatenate(pieces(field, 2), axis=0).astype(BF16)
    total = jnp.dot(lhs, high, preferred_element_type=F32)
    total = total + jnp.dot(lhs, low, preferred_element_type=F32)
    return total[:8] + total[8:]


def pick(field, onehot, *extra):
    lhs = jnp.concatenate(pieces(field, 3) + list(extra), axis=0).astype(BF16)
    out = jnp.dot(lhs, onehot, preferred_element_type=F32)
    return [out[:8] + out[8:16] + out[16:24]] + [
        out[24 + 8 * i : 32 + 8 * i] for i in range(len(extra))
    ]


def spread(jumps, onehot):
    lhs = jnp.concatenate(pieces(jumps, 3), axis=0).astype(BF16)
    out = lax.dot_general(lhs, onehot, (((1,), (1,)), ((), ())), preferred_element_type=F32)
    return out[:8] + out[8:16] + out[16:24]


def arrived(in_ref, partners_ref):
    place = lax.broadcasted_iota(jnp.int32, (8, LANES), 1) // JR
    groups = []
    for first in range(0, JW // JR, LANES // JR):
        total = jnp.zeros((8, LANES), F32)
        at = first * JR
        for r in range(first, min(first + LANES // JR, ROUNDS)):
            block = in_ref[partners_ref[0, r], :, at : at + LANES]
            total = jnp.where(place == r - first, block, total)
        groups.append(total)
    return jnp.concatenate(groups, axis=1)


def stream_dense(field, block_ref, rows_ref, sems, keep):
    lhs = jnp.concatenate(pieces(field, 2), axis=0).astype(BF16)
    depth = rows_ref.shape[0] // CHUNKS
    total = jnp.zeros((lhs.shape[0], rows_ref.shape[1]), F32)
    for chunk in range(CHUNKS):
        at = slice(chunk * depth, (chunk + 1) * depth)
        chunk_copy(block_ref, rows_ref, sems, chunk).wait()
        rows = rows_ref[at, :]
        high = rows.astype(BF16)
        low = (rows - high.astype(F32)).astype(BF16)
        keep[0, at, :] = high
        keep[1, at, :] = low
        total = total + jnp.dot(lhs[:, at], high, preferred_element_type=F32)
        total = total + jnp.dot(lhs[:, at], low, preferred_element_type=F32)
    return total[:8] + total[8:]


def chunk_copy(block_ref, rows_ref, sems, chunk):
    depth = rows_ref.shape[0] // CHUNKS
    at = pl.ds(chunk * depth, depth)
    return pltpu.make_async_copy(block_ref.at[at, :], rows_ref.at[at, :], sems.at[chunk])


def prepare(block_ref, x_hbm, load_hbm, contact_hbm, rows_hbm, partners_hbm, counts_hbm,
            onehot_ref, valid_ref, own_ref, hown_ref, h_ref, out_ref, first_ref, last_ref, halves_ref,
            held_ref, x_ref, load_ref, contact_ref, rows_ref, partners_ref, counts_ref, sems, more_sems):
    small = [
        pltpu.make_async_copy(source, target, more_sems.at[i])
        for i, (source, target) in enumerate((
            (rows_hbm, rows_ref), (counts_hbm, counts_ref), (x_hbm, x_ref),
            (contact_hbm, contact_ref), (partners_hbm, partners_ref), (load_hbm, load_ref),
        ))
    ]
    for copy in small:
        copy.start()
    for chunk in range(CHUNKS):
        chunk_copy(block_ref, held_ref, sems, chunk).start()
    for copy in small:
        copy.wait()
    x = x_ref[...]
    width = x.shape[1]
    rows = jnp.concatenate(
        [rows_ref[r] for r in range(ROUNDS)]
        + [jnp.full((1, JW - ROUNDS * JR), -1, jnp.int32)],
        axis=1,
    )
    hit = lax.broadcasted_iota(jnp.int32, (width, JW), 0) == rows
    onehot = jnp.where(hit, 1.0, 0.0).astype(BF16)
    onehot_ref[...] = onehot
    lane = lax.broadcasted_iota(jnp.int32, (8, JW), 1)
    valid = jnp.zeros((8, JW), F32)
    for r in range(ROUNDS):
        inside = (lane >= r * JR) & (lane < r * JR + counts_ref[0, r])
        valid = jnp.where(inside, 1.0, valid)
    valid_ref[...] = valid
    contact = jnp.broadcast_to(jnp.where(contact_ref[...] == 1, 1.0, 0.0), x.shape)
    own, own_contact = pick(x, onehot, contact)
    own_ref[...] = jnp.concatenate([own, own_contact], axis=0)
    position = lax.broadcasted_iota(jnp.int32, x.shape, 1)
    edge = (position < FACE) | (position >= width - FACE)
    h = spread(valid * own, onehot) + jnp.where(edge, x, 0.0) - load_ref[...]
    h = h + stream_dense(x, block_ref, held_ref, sems, halves_ref)
    h_ref[...] = h
    (hown,) = pick(h, onehot)
    hown_ref[...] = hown
    out_ref[...] = jnp.zeros_like(out_ref)
    place = lax.broadcasted_iota(jnp.int32, (8, LANES), 1) // JR
    for r in range(ROUNDS):
        group, slot = divmod(r * JR, LANES)
        at = slice(group * LANES, (group + 1) * LANES)
        parcel = jnp.zeros((8, LANES), F32)
        for i, jump in enumerate((own, hown, own_contact)):
            block = pltpu.roll(jump[:, at], (i * JR) % LANES, 1) if i else jump[:, at]
            parcel = jnp.where(place == (slot // JR + i) % (LANES // JR), block, parcel)
        out_ref[partners_ref[0, r]] = parcel
    both = jnp.concatenate([x, h, contact], axis=0)
    first_ref[...] = both[:, :FACE]
    last_ref[...] = both[:, width - FACE :]


def with_coupling(image, x, load, own, far, below, above, valid, onehot):
    width = x.shape[1]
    total = image + spread(valid * (own - far), onehot) - load
    head = total[:, :FACE] + (x[:, :FACE] - below)
    tail = total[:, width - FACE :] + (x[:, width - FACE :] - above)
    return jnp.concatenate([head, total[:, FACE : width - FACE], tail], axis=1)


def lane_sum(value):
    return jnp.sum(value, axis=1, keepdims=True)


def first_gradient(partners_ref, layer_ref, halves_ref, x_ref, h_ref, own_ref, hown_ref, in_ref,
                   below_in, above_in, valid_ref, onehot_ref,
                   g_ref, gown_ref, far_ref, gfar_ref, below_ref, gbelow_ref, above_ref, gabove_ref,
                   all_ref):
    width = x_ref.shape[1]
    place = lax.broadcasted_iota(jnp.int32, (8, LANES), 1) // JR
    parts = [[jnp.zeros((8, LANES), F32)] * 2 for _ in range(3)]
    for r in range(ROUNDS):
        group, slot = divmod(r * JR, LANES)
        parcel = in_ref[partners_ref[0, r]]
        for i in range(3):
            block = pltpu.roll(parcel, LANES - i * JR, 1) if i else parcel
            parts[i][group] = jnp.where(place == slot // JR, block, parts[i][group])
    far, hfar, far_contact = (jnp.concatenate(part, axis=1) for part in parts)
    valid = valid_ref[...]
    own = own_ref[:8]
    far_ref[...] = jnp.concatenate([far, far_contact], axis=0)
    gown = hown_ref[...] - valid * far
    gfar = hfar - valid * own
    gown_ref[...] = gown
    gfar_ref[...] = gfar
    below, above = below_in[...], above_in[...]
    below_ref[...] = jnp.concatenate([below[:8], below[16:]], axis=0)
    above_ref[...] = jnp.concatenate([above[:8], above[16:]], axis=0)
    layer = layer_ref[0, 0]
    gbelow = jnp.where(layer > 0, below[8:16] - x_ref[:, :FACE], 0.0)
    gabove = jnp.where(layer < layer_ref[0, 1] - 1, above[8:16] - x_ref[:, width - FACE :], 0.0)
    gbelow_ref[...] = gbelow
    gabove_ref[...] = gabove
    h = h_ref[...] - spread(valid * far, onehot_ref[...])
    first = h[:, :FACE] - below[:8]
    last = h[:, width - FACE :] - above[:8]
    g = jnp.concatenate([first, h[:, FACE : width - FACE], last], axis=1)
    g_ref[...] = g
    jumps = valid * gown * (gown - gfar)
    terms = first * (first - gbelow) + last * (last - gabove) + jumps[:, :LANES] + jumps[:, LANES:]
    square = lane_sum(g * g)
    curvature = lane_sum(terms) + lane_sum(g * dense(g, halves_ref[0], halves_ref[1]))
    lane = lax.broadcasted_iota(jnp.int32, (8, LANES), 1)
    row = lax.broadcasted_iota(jnp.int32, (8, LANES), 0)
    line = jnp.where(lane == row, square, 0.0) + jnp.where(lane == row + 8, curvature, 0.0)
    line = jnp.sum(line, axis=0, keepdims=True)
    short = lax.broadcasted_iota(jnp.int32, (1, LANES), 1)
    for r in range(ROUNDS):
        name = jnp.full((1, LANES), partners_ref[0, r], jnp.int32).astype(F32)
        line = jnp.where(short == NAMES + r, name, line)
    all_ref[...] = jnp.broadcast_to(line, all_ref.shape)


def give_gradient(gradient, onehot, g_ref, gown_ref, last_ref):
    g_ref[...] = gradient
    last_ref[...] = gradient[:, gradient.shape[1] - FACE :]
    gown_ref[...] = pick(gradient, onehot)[0]


def local_sums(g_ref, halves_ref, sums_ref):
    g = g_ref[...]
    image = dense(g, halves_ref[0], halves_ref[1])
    width = g.shape[1]
    terms = g * image
    edges = g[:, :FACE] * g[:, :FACE] + g[:, width - FACE :] * g[:, width - FACE :]
    square = jnp.sum(g * g, axis=1, keepdims=True)
    curvature = jnp.sum(terms, axis=1, keepdims=True) + jnp.sum(edges, axis=1, keepdims=True)
    lane = lax.broadcasted_iota(jnp.int32, (8, LANES), 1)
    sums_ref[...] = jnp.where(lane == SQUARE, square, jnp.where(lane == CURVATURE, curvature, 0.0))


def announce(sums_ref, g_ref, gown_ref, valid_ref, below_ref, out_ref):
    own = valid_ref[...] * gown_ref[...]
    squares = own * own
    pairs = g_ref[:, :FACE] * below_ref[...]
    terms = squares[:, :LANES] + squares[:, LANES:] - 2.0 * pairs
    more = jnp.sum(terms, axis=1, keepdims=True)
    lane = lax.broadcasted_iota(jnp.int32, (8, LANES), 1)
    extra = sums_ref[...] + jnp.where(lane == CURVATURE, more, 0.0)
    parcel = jnp.concatenate([own[:, :LANES], own[:, LANES:] + extra], axis=1)
    out_ref[...] = jnp.broadcast_to(parcel[None], out_ref.shape)


def layer_sums(partners_ref, table_ref, in_ref, g_ref, out_ref, *gfar_refs):
    for gfar_ref in gfar_refs:
        gfar_ref[...] = arrived(in_ref, partners_ref)
    place = lax.broadcasted_iota(jnp.int32, (8, LANES), 1) // JR
    nothing = jnp.zeros((8, LANES), F32)
    products, sums = [nothing, nothing], nothing
    for p in range(in_ref.shape[0]):
        near = [in_ref[p, :, :LANES], in_ref[p, :, LANES:]]
        sums = sums + near[1]
        for group in range(2):
            far = nothing
            for r in range(4 * group, min(4 * group + 4, ROUNDS)):
                block = in_ref[table_ref[p, r], :, group * LANES : (group + 1) * LANES]
                far = jnp.where(place == r - 4 * group, block, far)
            products[group] = products[group] + near[group] * far
    cross = jnp.sum(products[0] + products[1], axis=1, keepdims=True)
    lane = lax.broadcasted_iota(jnp.int32, (8, LANES), 1)
    sums = sums - jnp.where(lane == CURVATURE, cross, 0.0)
    parcel = jnp.concatenate([g_ref[:, :FACE], sums], axis=1)
    out_ref[...] = jnp.broadcast_to(parcel[None], out_ref.shape)


def step_of(in_ref):
    total = in_ref[0, :, LANES:]
    for layer in range(1, in_ref.shape[0]):
        total = total + in_ref[layer, :, LANES:]
    square = total[:, SQUARE : SQUARE + 1]
    curvature = total[:, CURVATURE : CURVATURE + 1]
    return (square + 1e-6) / (curvature + 1e-6)


def moved(x, g, step, contact):
    out = x - step * g
    return jnp.where(contact == 1, jnp.maximum(out, 0.0), out)


def first_step(in_ref):
    line = jnp.sum(in_ref[...], axis=0, keepdims=True)
    line = jnp.broadcast_to(line, (8, LANES))
    lane = lax.broadcasted_iota(jnp.int32, (8, LANES), 1)
    row = lax.broadcasted_iota(jnp.int32, (8, LANES), 0)
    square = lane_sum(jnp.where(lane == row, line, 0.0))
    curvature = lane_sum(jnp.where(lane == row + 8, line, 0.0))
    return (square + 1e-6) / (curvature + 1e-6)


def first_advance(in_ref, *refs):
    *refs, table_ref = refs
    plans = table_ref.shape[0]
    lines = in_ref[pl.ds(0, plans, stride=in_ref.shape[0] // plans), :]
    table_ref[...] = pltpu.roll(lines, LANES - NAMES, 1)[:, :8].astype(jnp.int32)
    gabove_ref, *refs = refs
    advance_by(first_step(in_ref), gabove_ref[...], *refs)


def advance(layer_ref, in_ref, *refs):
    layers = in_ref.shape[0]
    layer = layer_ref[0, 0]
    gabove = in_ref[jnp.minimum(layer + 1, layers - 1), :, :FACE]
    gabove = jnp.where(layer < layers - 1, gabove, 0.0)
    advance_by(step_of(in_ref), gabove, *refs)


def advance_by(step, gabove, x_ref, g_ref, contact_ref, load_ref,
               own_ref, gown_ref, far_ref, gfar_ref, below_ref, gbelow_ref, above_ref,
               valid_ref, onehot_ref, halves_ref,
               g_out, gown_out, last_out, x_out, *halo_outs):
    x = moved(x_ref[...], g_ref[...], step, contact_ref[...])
    x_out[...] = x
    halo = []
    for held_ref, slope in (
        (own_ref, gown_ref[...]), (far_ref, gfar_ref[...]), (below_ref, gbelow_ref[...]), (above_ref, gabove),
    ):
        halo.append(moved(held_ref[:8], slope, step, held_ref[8:]))
    for held_ref, value, held_out in zip((own_ref, far_ref, below_ref, above_ref), halo, halo_outs):
        held_out[...] = jnp.concatenate([value, held_ref[8:]], axis=0)
    onehot = onehot_ref[...]
    image = dense(x, halves_ref[0], halves_ref[1])
    gradient = with_coupling(image, x, load_ref[...], *halo, valid_ref[...], onehot)
    give_gradient(gradient, onehot, g_out, gown_out, last_out)


def finish(in_ref, x_ref, g_ref, contact_ref, x_out, g_out):
    g = g_ref[...]
    g_out[...] = g
    x_out[...] = moved(x_ref[...], g, step_of(in_ref), contact_ref[...])


def swap(outgoing, axis):
    return lax.all_to_all(outgoing, axis, split_axis=0, concat_axis=0, tiled=True)


def lift(face, step):
    layers = lax.axis_size("layer")
    return lax.ppermute(
        face, "layer", [(i, i + step) for i in range(layers) if 0 <= i + step < layers]
    )


def shards(dual_block, start, load, partners, jump_rows, counts, contact):
    block, x, target = dual_block[0, 0], start[0, 0], load[0, 0]
    rows, amounts, flags = jump_rows.reshape(ROUNDS, 1, JR), counts[0], contact[0]
    loads, width = x.shape
    plans, layers = lax.axis_size("plan"), lax.axis_size("layer")
    field, jump, face = shape(loads, width), shape(loads, JW), shape(loads, FACE)
    jump2, face2, face3 = shape(2 * loads, JW), shape(2 * loads, FACE), shape(3 * loads, FACE)
    flops = 4 * 16 * width * width
    layer = jnp.stack([lax.axis_index("layer"), layers]).astype(jnp.int32).reshape(1, 2)
    amounts, layer = lax.optimization_barrier((amounts, layer))
    held = pltpu.VMEM((width, width), F32)
    chunk_sems = pltpu.SemaphoreType.DMA((CHUNKS,))

    onehot, valid, own, hown, h, out, first, last, halves = call(
        prepare, "prepare",
        (shape(width, JW, dtype=BF16), jump, jump2, jump, field, shape(plans, loads, LANES), face3, face3,
         shape(2, width, width, dtype=BF16)),
        [HBM] * 7, 16, flops, 4 * width * width,
        [
            held, pltpu.VMEM(x.shape, F32), pltpu.VMEM(target.shape, F32),
            pltpu.VMEM(flags.shape, jnp.int32), pltpu.VMEM(rows.shape, jnp.int32),
            pltpu.SMEM(partners.shape, jnp.int32), pltpu.SMEM(amounts.shape, jnp.int32),
            chunk_sems, pltpu.SemaphoreType.DMA((6,)),
        ],
    )(*(pltpu.with_memory_space_constraint(a, pltpu.HBM) for a in (block, x, target, flags, rows, partners, amounts)))
    below, above, out = lax.optimization_barrier((lift(last, 1), lift(first, -1), out))
    incoming = swap(out, "plan")
    g, gown, far, gfar, below, gbelow, above, gabove, out = call(
        first_gradient, "first_gradient",
        (field, jump, jump2, jump, face2, face, face2, face,
         shape(plans * layers, LANES)),
        [SMEM] * 2 + [VMEM] * 10, 12, flops, 4 * width * width,
    )(partners, layer, halves, x, h, own, hown, incoming, below, above, valid, onehot)
    incoming = swap(out, ("plan", "layer"))

    after = (field, jump, face, field, jump2, jump2, face2, face2)
    g, gown, last, x, own, far, below, above, table = call(
        first_advance, "first_advance", after + (shape(plans, 8, dtype=jnp.int32),),
        [VMEM] * 16, 12, flops, 4 * width * width,
    )(incoming, gabove, x, g, flags, target, own, gown, far, gfar, below, gbelow, above,
      valid, onehot, halves)

    for iteration in range(1, ITERS):
        gbelow = lift(last, 1)
        sums = call(
            local_sums, "local_sums", face, [VMEM] * 2, 12, flops, 4 * width * width,
        )(g, halves)
        out = call(announce, "announce", shape(plans, loads, JW), [VMEM] * 5, 8)(
            sums, g, gown, valid, gbelow
        )
        ending = iteration == ITERS - 1
        out, *gfar = call(
            layer_sums, "layer_sums", (shape(layers, loads, FACE + LANES),) + (() if ending else (jump,)),
            [SMEM] * 2 + [VMEM] * 2, 8,
        )(partners, table, swap(out, "plan"), g)
        incoming = swap(out, "layer")
        if ending:
            x, g = call(finish, "finish", (field, field), [VMEM] * 4, 8)(incoming, x, g, flags)
            break
        g, gown, last, x, *halo = call(
            advance, "advance", after[:4] if iteration == ITERS - 2 else after,
            [SMEM] + [VMEM] * 15, 12, flops, 4 * width * width,
        )(layer, incoming, x, g, flags, target, own, gown, far, *gfar, below, gbelow, above,
          valid, onehot, halves)
        own, far, below, above = halo or (None,) * 4
    return x[None, None], g[None, None]


def solution(mesh):
    in_specs = (
        P("layer", "plan", None, None),
        P("layer", "plan", None, None),
        P("layer", "plan", None, None),
        P("plan", None),
        P("layer", "plan", None, None),
        P("layer", "plan", None),
        P("layer", "plan", None),
    )
    out_specs = (P("layer", "plan", None, None), P("layer", "plan", None, None))
    return jax.shard_map(shards, mesh=mesh, in_specs=in_specs, out_specs=out_specs, check_vma=False)
```

```python
import jax
import jax.numpy as jnp
from jax import lax
from jax.experimental import pallas as pl
from jax.experimental.pallas import tpu as pltpu
from jax.sharding import PartitionSpec as P

FACE = 128
JR = 32
ROUNDS = 6
ITERS = 4
LANES = 128
HALF = 3
JW = 2 * LANES
CHUNKS = 4
NAMES = 16
SQUARE, CURVATURE = HALF * JR, HALF * JR + 1
F32 = jnp.float32
BF16 = jnp.bfloat16

VMEM = pl.BlockSpec(memory_space=pltpu.VMEM)
SMEM = pl.BlockSpec(memory_space=pltpu.SMEM)
HBM = pl.BlockSpec(memory_space=pltpu.HBM)


def shape(*dims, dtype=F32):
    return jax.ShapeDtypeStruct(dims, dtype)


def call(body, name, outs, specs, limit, flops=0, traffic=0, scratch=()):
    return pl.pallas_call(
        body,
        name=name,
        out_shape=outs,
        in_specs=specs,
        scratch_shapes=scratch,
        out_specs=jax.tree.map(lambda _: VMEM, outs),
        compiler_params=pltpu.CompilerParams(vmem_limit_bytes=limit * 2**20),
        cost_estimate=pl.CostEstimate(flops=flops, bytes_accessed=traffic, transcendentals=0),
    )


def pieces(value, count):
    parts = []
    for _ in range(count):
        part = value.astype(BF16).astype(F32)
        parts.append(part)
        value = value - part
    return parts


def lane_sum(value):
    return jnp.sum(value, axis=1, keepdims=True)


def dense(field, high, low):
    lhs = jnp.concatenate(pieces(field, 2), axis=0).astype(BF16)
    total = jnp.dot(lhs, high, preferred_element_type=F32)
    total = total + jnp.dot(lhs, low, preferred_element_type=F32)
    return total[:8] + total[8:]


def pick(field, onehot, *extra):
    lhs = jnp.concatenate(pieces(field, 3) + list(extra), axis=0).astype(BF16)
    out = jnp.dot(lhs, onehot, preferred_element_type=F32)
    return [out[:8] + out[8:16] + out[16:24]] + [
        out[24 + 8 * i : 32 + 8 * i] for i in range(len(extra))
    ]


def spread(jumps, onehot):
    lhs = jnp.concatenate(pieces(jumps, 3), axis=0).astype(BF16)
    out = lax.dot_general(lhs, onehot, (((1,), (1,)), ((), ())), preferred_element_type=F32)
    return out[:8] + out[8:16] + out[16:24]


def half_of(in_ref, table_ref, plan):
    place = lax.broadcasted_iota(jnp.int32, (8, LANES), 1) // JR
    total = jnp.zeros((8, LANES), F32)
    for r in range(HALF):
        total = jnp.where(place == r, in_ref[table_ref[plan, r]], total)
    return total


def stream_dense(field, block_ref, rows_ref, sems, keep):
    lhs = jnp.concatenate(pieces(field, 2), axis=0).astype(BF16)
    depth = rows_ref.shape[0] // CHUNKS
    total = jnp.zeros((lhs.shape[0], rows_ref.shape[1]), F32)
    for chunk in range(CHUNKS):
        at = slice(chunk * depth, (chunk + 1) * depth)
        chunk_copy(block_ref, rows_ref, sems, chunk).wait()
        rows = rows_ref[at, :]
        high = rows.astype(BF16)
        low = (rows - high.astype(F32)).astype(BF16)
        keep[0, at, :] = high
        keep[1, at, :] = low
        total = total + jnp.dot(lhs[:, at], high, preferred_element_type=F32)
        total = total + jnp.dot(lhs[:, at], low, preferred_element_type=F32)
    return total[:8] + total[8:]


def chunk_copy(block_ref, rows_ref, sems, chunk):
    depth = rows_ref.shape[0] // CHUNKS
    at = pl.ds(chunk * depth, depth)
    return pltpu.make_async_copy(block_ref.at[at, :], rows_ref.at[at, :], sems.at[chunk])


def prepare(block_ref, x_hbm, load_hbm, contact_hbm, rows_hbm, partners_hbm, counts_hbm,
            onehot_ref, valid_ref, own_ref, hown_ref, h_ref, out_ref, first_ref, last_ref, halves_ref,
            held_ref, x_ref, load_ref, contact_ref, rows_ref, partners_ref, counts_ref, sems, more_sems):
    small = [
        pltpu.make_async_copy(source, target, more_sems.at[i])
        for i, (source, target) in enumerate((
            (rows_hbm, rows_ref), (counts_hbm, counts_ref), (x_hbm, x_ref),
            (contact_hbm, contact_ref), (partners_hbm, partners_ref), (load_hbm, load_ref),
        ))
    ]
    for copy in small:
        copy.start()
    for chunk in range(CHUNKS):
        chunk_copy(block_ref, held_ref, sems, chunk).start()
    for copy in small:
        copy.wait()
    x = x_ref[...]
    width = x.shape[1]
    spare = [jnp.full((1, LANES - HALF * JR), -1, jnp.int32)]
    rows = [rows_ref[r] for r in range(ROUNDS)]
    rows = jnp.concatenate(rows[:HALF] + spare + rows[HALF:] + spare, axis=1)
    hit = lax.broadcasted_iota(jnp.int32, (width, JW), 0) == rows
    onehot = jnp.where(hit, 1.0, 0.0).astype(BF16)
    onehot_ref[...] = onehot
    lane = lax.broadcasted_iota(jnp.int32, (8, JW), 1)
    valid = jnp.zeros((8, JW), F32)
    for r in range(ROUNDS):
        start = r // HALF * LANES + r % HALF * JR
        inside = (lane >= start) & (lane < start + counts_ref[0, r])
        valid = jnp.where(inside, 1.0, valid)
    valid_ref[...] = valid
    contact = jnp.broadcast_to(jnp.where(contact_ref[...] == 1, 1.0, 0.0), x.shape)
    own, own_contact = pick(x, onehot, contact)
    own_ref[...] = jnp.concatenate([own, own_contact], axis=0)
    position = lax.broadcasted_iota(jnp.int32, x.shape, 1)
    edge = (position < FACE) | (position >= width - FACE)
    h = spread(valid * own, onehot) + jnp.where(edge, x, 0.0) - load_ref[...]
    h = h + stream_dense(x, block_ref, held_ref, sems, halves_ref)
    h_ref[...] = h
    (hown,) = pick(h, onehot)
    hown_ref[...] = hown
    out_ref[...] = jnp.zeros_like(out_ref)
    place = lax.broadcasted_iota(jnp.int32, (8, LANES), 1) // JR
    for r in range(ROUNDS):
        group, slot = divmod(r, HALF)
        at = slice(group * LANES, (group + 1) * LANES)
        parcel = jnp.zeros((8, LANES), F32)
        for i, jump in enumerate((own, hown, own_contact)):
            block = pltpu.roll(jump[:, at], (i * JR) % LANES, 1) if i else jump[:, at]
            parcel = jnp.where(place == (slot + i) % (LANES // JR), block, parcel)
        out_ref[partners_ref[0, r]] = parcel
    both = jnp.concatenate([x, h, contact], axis=0)
    first_ref[...] = both[:, :FACE]
    last_ref[...] = both[:, width - FACE :]


def with_coupling(image, x, load, own, far, below, above, valid, onehot):
    width = x.shape[1]
    total = image + spread(valid * (own - far), onehot) - load
    head = total[:, :FACE] + (x[:, :FACE] - below)
    tail = total[:, width - FACE :] + (x[:, width - FACE :] - above)
    return jnp.concatenate([head, total[:, FACE : width - FACE], tail], axis=1)


def first_gradient(partners_ref, where_ref, halves_ref, x_ref, h_ref, own_ref, hown_ref, in_ref,
                   below_in, above_in, valid_ref, onehot_ref,
                   g_ref, gown_ref, far_ref, gfar_ref, below_ref, gbelow_ref, above_ref, gabove_ref,
                   all_ref, masks_ref):
    width = x_ref.shape[1]
    place = lax.broadcasted_iota(jnp.int32, (8, LANES), 1) // JR
    parts = [[jnp.zeros((8, LANES), F32)] * 2 for _ in range(3)]
    for r in range(ROUNDS):
        group, slot = divmod(r, HALF)
        parcel = in_ref[partners_ref[0, r]]
        for i in range(3):
            block = pltpu.roll(parcel, LANES - i * JR, 1) if i else parcel
            parts[i][group] = jnp.where(place == slot, block, parts[i][group])
    far, hfar, far_contact = (jnp.concatenate(part, axis=1) for part in parts)
    valid = valid_ref[...]
    own = own_ref[:8]
    far_ref[...] = jnp.concatenate([far, far_contact], axis=0)
    gown = hown_ref[...] - valid * far
    gfar = hfar - valid * own
    gown_ref[...] = gown
    gfar_ref[...] = gfar
    below, above = below_in[...], above_in[...]
    below_ref[...] = jnp.concatenate([below[:8], below[16:]], axis=0)
    above_ref[...] = jnp.concatenate([above[:8], above[16:]], axis=0)
    layer, layers, core = where_ref[0, 0], where_ref[0, 1], lax.rem(where_ref[0, 2], 2)
    member = lax.broadcasted_iota(jnp.int32, (masks_ref.shape[1], LANES), 0)
    masks_ref[0] = jnp.where(member == 2 * (layer + 1) + core, 1.0, 0.0)
    masks_ref[1] = jnp.where(member == 2 * layer + 1 - core, 1.0, 0.0)
    masks_ref[2] = jnp.where(member >= 0, core, 0).astype(F32)
    gbelow = jnp.where(layer > 0, below[8:16] - x_ref[:, :FACE], 0.0)
    gabove = jnp.where(layer < layers - 1, above[8:16] - x_ref[:, width - FACE :], 0.0)
    gbelow_ref[...] = gbelow
    gabove_ref[...] = gabove
    h = h_ref[...] - spread(valid * far, onehot_ref[...])
    first = h[:, :FACE] - below[:8]
    last = h[:, width - FACE :] - above[:8]
    g = jnp.concatenate([first, h[:, FACE : width - FACE], last], axis=1)
    g_ref[...] = g
    jumps = valid * gown * (gown - gfar)
    terms = first * (first - gbelow) + last * (last - gabove) + jumps[:, :LANES] + jumps[:, LANES:]
    square = lane_sum(g * g)
    curvature = lane_sum(terms) + lane_sum(g * dense(g, halves_ref[0], halves_ref[1]))
    lane = lax.broadcasted_iota(jnp.int32, (8, LANES), 1)
    row = lax.broadcasted_iota(jnp.int32, (8, LANES), 0)
    line = jnp.where(lane == row, square, 0.0) + jnp.where(lane == row + 8, curvature, 0.0)
    line = jnp.sum(line, axis=0, keepdims=True)
    short = lax.broadcasted_iota(jnp.int32, (1, LANES), 1)
    for r in range(ROUNDS):
        name = jnp.full((1, LANES), partners_ref[0, r], jnp.int32).astype(F32)
        line = jnp.where(short == NAMES + r, name, line)
    all_ref[...] = jnp.broadcast_to(line, all_ref.shape)


def give_gradient(gradient, onehot, g_ref, gown_ref, last_ref):
    g_ref[...] = gradient
    last_ref[...] = gradient[:, gradient.shape[1] - FACE :]
    gown_ref[...] = pick(gradient, onehot)[0]


def local_sums(g_ref, halves_ref, sums_ref):
    g = g_ref[...]
    image = dense(g, halves_ref[0], halves_ref[1])
    width = g.shape[1]
    terms = g * image
    edges = g[:, :FACE] * g[:, :FACE] + g[:, width - FACE :] * g[:, width - FACE :]
    square = jnp.sum(g * g, axis=1, keepdims=True)
    curvature = jnp.sum(terms, axis=1, keepdims=True) + jnp.sum(edges, axis=1, keepdims=True)
    lane = lax.broadcasted_iota(jnp.int32, (8, LANES), 1)
    sums_ref[...] = jnp.where(lane == SQUARE, square, jnp.where(lane == CURVATURE, curvature, 0.0))


def announce(sums_ref, g_ref, gown_ref, valid_ref, below_ref, out_ref):
    own = valid_ref[...] * gown_ref[...]
    squares = own * own
    pairs = g_ref[:, :FACE] * below_ref[...]
    terms = squares[:, :LANES] + squares[:, LANES:] - 2.0 * pairs
    more = jnp.sum(terms, axis=1, keepdims=True)
    lane = lax.broadcasted_iota(jnp.int32, (8, LANES), 1)
    extra = sums_ref[...] + jnp.where(lane == CURVATURE, more, 0.0)
    halves = own[:, :LANES] + extra, own[:, LANES:] + extra
    for plan in range(out_ref.shape[0]):
        out_ref[plan] = halves[plan % 2]


def layer_sums(where_ref, table_ref, in_ref, g_ref, out_ref, *gfar_refs):
    plan = where_ref[0, 2]
    for gfar_ref in gfar_refs:
        gfar_ref[...] = half_of(in_ref, table_ref, plan)
    products = sums = jnp.zeros((8, LANES), F32)
    for p in range(in_ref.shape[0]):
        near = in_ref[p]
        sums = sums + near
        products = products + near * half_of(in_ref, table_ref, p)
    cross = lane_sum(products)
    lane = lax.broadcasted_iota(jnp.int32, (8, LANES), 1)
    sums = 0.5 * sums - jnp.where(lane == CURVATURE, cross, 0.0)
    sibling = half_of(in_ref, table_ref, plan + 1 - 2 * lax.rem(plan, 2))
    parcel = jnp.concatenate([g_ref[:, :FACE], jnp.where(lane < SQUARE, sibling, sums)], axis=1)
    out_ref[...] = jnp.broadcast_to(parcel[None], out_ref.shape)


def step_of(in_ref):
    total = in_ref[0, :, LANES:]
    for member in range(1, in_ref.shape[0]):
        total = total + in_ref[member, :, LANES:]
    square = total[:, SQUARE : SQUARE + 1]
    curvature = total[:, CURVATURE : CURVATURE + 1]
    return (square + 1e-6) / (curvature + 1e-6)


def moved(x, g, step, contact):
    out = x - step * g
    return jnp.where(contact == 1, jnp.maximum(out, 0.0), out)


def first_step(in_ref):
    line = jnp.sum(in_ref[...], axis=0, keepdims=True)
    line = jnp.broadcast_to(line, (8, LANES))
    lane = lax.broadcasted_iota(jnp.int32, (8, LANES), 1)
    row = lax.broadcasted_iota(jnp.int32, (8, LANES), 0)
    square = lane_sum(jnp.where(lane == row, line, 0.0))
    curvature = lane_sum(jnp.where(lane == row + 8, line, 0.0))
    return (square + 1e-6) / (curvature + 1e-6)


def first_advance(in_ref, masks_ref, *refs):
    *refs, table_ref = refs
    plans = table_ref.shape[0]
    lines = in_ref[pl.ds(0, plans, stride=in_ref.shape[0] // plans), :]
    names = jnp.where(
        masks_ref[2, :1] == 0.0,
        pltpu.roll(lines, LANES - NAMES, 1),
        pltpu.roll(lines, LANES - NAMES - HALF, 1),
    )
    table_ref[...] = names[:, :8].astype(jnp.int32)
    gabove_ref, gfar_ref, *refs = refs
    advance_by(first_step(in_ref), gabove_ref[...], gfar_ref[...], *refs)


def advance(in_ref, masks_ref, half_ref, *refs):
    gabove = other = jnp.zeros((8, LANES), F32)
    for member in range(in_ref.shape[0]):
        at = slice(member, member + 1)
        gabove = jnp.where(masks_ref[0, at] == 1.0, in_ref[member, :, :FACE], gabove)
        other = jnp.where(masks_ref[1, at] == 1.0, in_ref[member, :, LANES:], other)
    lane = lax.broadcasted_iota(jnp.int32, (8, LANES), 1)
    half, other = half_ref[...], jnp.where(lane < SQUARE, other, 0.0)
    even = masks_ref[2, :1] == 0.0
    gfar = jnp.concatenate([jnp.where(even, half, other), jnp.where(even, other, half)], axis=1)
    advance_by(step_of(in_ref), gabove, gfar, *refs)


def advance_by(step, gabove, gfar, x_ref, g_ref, contact_ref, load_ref,
               own_ref, gown_ref, far_ref, below_ref, gbelow_ref, above_ref,
               valid_ref, onehot_ref, halves_ref,
               g_out, gown_out, last_out, x_out, *halo_outs):
    x = moved(x_ref[...], g_ref[...], step, contact_ref[...])
    x_out[...] = x
    halo = []
    for held_ref, slope in (
        (own_ref, gown_ref[...]), (far_ref, gfar), (below_ref, gbelow_ref[...]), (above_ref, gabove),
    ):
        halo.append(moved(held_ref[:8], slope, step, held_ref[8:]))
    for held_ref, value, held_out in zip((own_ref, far_ref, below_ref, above_ref), halo, halo_outs):
        held_out[...] = jnp.concatenate([value, held_ref[8:]], axis=0)
    onehot = onehot_ref[...]
    image = dense(x, halves_ref[0], halves_ref[1])
    gradient = with_coupling(image, x, load_ref[...], *halo, valid_ref[...], onehot)
    give_gradient(gradient, onehot, g_out, gown_out, last_out)


def finish(in_ref, x_ref, g_ref, contact_ref, x_out, g_out):
    g = g_ref[...]
    g_out[...] = g
    x_out[...] = moved(x_ref[...], g, step_of(in_ref), contact_ref[...])


def swap(outgoing, axis, groups=None):
    return lax.all_to_all(
        outgoing, axis, split_axis=0, concat_axis=0, tiled=True, axis_index_groups=groups
    )


def lift(face, step):
    layers = lax.axis_size("layer")
    return lax.ppermute(
        face, "layer", [(i, i + step) for i in range(layers) if 0 <= i + step < layers]
    )


def shards(dual_block, start, load, partners, jump_rows, counts, contact):
    block, x, target = dual_block[0, 0], start[0, 0], load[0, 0]
    rows, amounts, flags = jump_rows.reshape(ROUNDS, 1, JR), counts[0], contact[0]
    loads, width = x.shape
    plans, layers = lax.axis_size("plan"), lax.axis_size("layer")
    field, jump, face = shape(loads, width), shape(loads, JW), shape(loads, FACE)
    jump2, face2, face3 = shape(2 * loads, JW), shape(2 * loads, FACE), shape(3 * loads, FACE)
    flops = 4 * 16 * width * width
    position = jnp.stack([lax.axis_index("layer"), layers, lax.axis_index("plan")])
    position = position.astype(jnp.int32).reshape(1, 3)
    amounts, position = lax.optimization_barrier((amounts, position))
    columns = [
        [(chip + core) * layers + layer for layer in range(layers) for core in range(2)]
        for chip in range(0, plans, 2)
    ]
    held = pltpu.VMEM((width, width), F32)
    chunk_sems = pltpu.SemaphoreType.DMA((CHUNKS,))

    onehot, valid, own, hown, h, out, first, last, halves = call(
        prepare, "prepare",
        (shape(width, JW, dtype=BF16), jump, jump2, jump, field, shape(plans, loads, LANES), face3, face3,
         shape(2, width, width, dtype=BF16)),
        [HBM] * 7, 16, flops, 4 * width * width,
        [
            held, pltpu.VMEM(x.shape, F32), pltpu.VMEM(target.shape, F32),
            pltpu.VMEM(flags.shape, jnp.int32), pltpu.VMEM(rows.shape, jnp.int32),
            pltpu.SMEM(partners.shape, jnp.int32), pltpu.SMEM(amounts.shape, jnp.int32),
            chunk_sems, pltpu.SemaphoreType.DMA((6,)),
        ],
    )(*(pltpu.with_memory_space_constraint(a, pltpu.HBM) for a in (block, x, target, flags, rows, partners, amounts)))
    below, above, out = lax.optimization_barrier((lift(last, 1), lift(first, -1), out))
    incoming = swap(out, "plan")
    g, gown, far, gfar, below, gbelow, above, gabove, out, masks = call(
        first_gradient, "first_gradient",
        (field, jump, jump2, jump, face2, face, face2, face,
         shape(plans * layers, LANES), shape(3, 2 * layers, LANES)),
        [SMEM] * 2 + [VMEM] * 10, 12, flops, 4 * width * width,
    )(partners, position, halves, x, h, own, hown, incoming, below, above, valid, onehot)
    incoming = swap(out, ("plan", "layer"))

    after = (field, jump, face, field, jump2, jump2, face2, face2)
    g, gown, last, x, own, far, below, above, table = call(
        first_advance, "first_advance", after + (shape(plans, 8, dtype=jnp.int32),),
        [VMEM] * 17, 12, flops, 4 * width * width,
    )(incoming, masks, gabove, gfar, x, g, flags, target, own, gown, far, below, gbelow, above,
      valid, onehot, halves)

    for iteration in range(1, ITERS):
        gbelow = lift(last, 1)
        sums = call(
            local_sums, "local_sums", face, [VMEM] * 2, 12, flops, 4 * width * width,
        )(g, halves)
        out = call(announce, "announce", shape(plans, loads, LANES), [VMEM] * 5, 8)(
            sums, g, gown, valid, gbelow
        )
        ending = iteration == ITERS - 1
        out, *half = call(
            layer_sums, "layer_sums",
            (shape(2 * layers, loads, FACE + LANES),) + (() if ending else (shape(loads, LANES),)),
            [SMEM] * 2 + [VMEM] * 2, 8,
        )(position, table, swap(out, "plan"), g)
        incoming = swap(out, ("plan", "layer"), columns)
        if ending:
            x, g = call(finish, "finish", (field, field), [VMEM] * 4, 8)(incoming, x, g, flags)
            break
        g, gown, last, x, *halo = call(
            advance, "advance", after[:4] if iteration == ITERS - 2 else after,
            [VMEM] * 16, 12, flops, 4 * width * width,
        )(incoming, masks, *half, x, g, flags, target, own, gown, far, below, gbelow, above,
          valid, onehot, halves)
        own, far, below, above = halo or (None,) * 4
    return x[None, None], g[None, None]


def solution(mesh):
    in_specs = (
        P("layer", "plan", None, None),
        P("layer", "plan", None, None),
        P("layer", "plan", None, None),
        P("plan", None),
        P("layer", "plan", None, None),
        P("layer", "plan", None),
        P("layer", "plan", None),
    )
    out_specs = (P("layer", "plan", None, None), P("layer", "plan", None, None))
    return jax.shard_map(shards, mesh=mesh, in_specs=in_specs, out_specs=out_specs, check_vma=False)
```

```python
import jax
import jax.numpy as jnp
from jax import lax
from jax.experimental import pallas as pl
from jax.experimental.pallas import tpu as pltpu
from jax.sharding import PartitionSpec as P

FACE = 128
JR = 32
ROUNDS = 6
ITERS = 4
LANES = 128
HALF = 3
JW = 2 * LANES
CHUNKS = 4
NAMES = 16
SQUARE, CURVATURE = HALF * JR, HALF * JR + 1
F32 = jnp.float32
BF16 = jnp.bfloat16

VMEM = pl.BlockSpec(memory_space=pltpu.VMEM)
SMEM = pl.BlockSpec(memory_space=pltpu.SMEM)
HBM = pl.BlockSpec(memory_space=pltpu.HBM)


def shape(*dims, dtype=F32):
    return jax.ShapeDtypeStruct(dims, dtype)


def call(body, name, outs, specs, limit, flops=0, traffic=0, scratch=()):
    return pl.pallas_call(
        body,
        name=name,
        out_shape=outs,
        in_specs=specs,
        scratch_shapes=scratch,
        out_specs=jax.tree.map(lambda _: VMEM, outs),
        compiler_params=pltpu.CompilerParams(vmem_limit_bytes=limit * 2**20),
        cost_estimate=pl.CostEstimate(flops=flops, bytes_accessed=traffic, transcendentals=0),
    )


def pieces(value, count):
    parts = []
    for _ in range(count):
        part = value.astype(BF16).astype(F32)
        parts.append(part)
        value = value - part
    return parts


def lane_sum(value):
    return jnp.sum(value, axis=1, keepdims=True)


def dense(field, halves_ref, columns=slice(None)):
    lhs = jnp.concatenate(pieces(field, 2), axis=0).astype(BF16)
    total = jnp.dot(lhs, halves_ref[0, :, columns], preferred_element_type=F32)
    total = total + jnp.dot(lhs, halves_ref[1, :, columns], preferred_element_type=F32)
    return total[:8] + total[8:]


def pick(field, onehot, *extra):
    lhs = jnp.concatenate(pieces(field, 3) + list(extra), axis=0).astype(BF16)
    out = jnp.dot(lhs, onehot, preferred_element_type=F32)
    return [out[:8] + out[8:16] + out[16:24]] + [
        out[24 + 8 * i : 32 + 8 * i] for i in range(len(extra))
    ]


def spread(jumps, onehot):
    lhs = jnp.concatenate(pieces(jumps, 3), axis=0).astype(BF16)
    out = lax.dot_general(lhs, onehot, (((1,), (1,)), ((), ())), preferred_element_type=F32)
    return out[:8] + out[8:16] + out[16:24]


def half_of(in_ref, table_ref, plan):
    place = lax.broadcasted_iota(jnp.int32, (8, LANES), 1) // JR
    total = jnp.zeros((8, LANES), F32)
    for r in range(HALF):
        total = jnp.where(place == r, in_ref[table_ref[plan, r]], total)
    return total


def stream_dense(field, block_ref, rows_ref, sems, keep):
    lhs = jnp.concatenate(pieces(field, 2), axis=0).astype(BF16)
    depth = rows_ref.shape[0] // CHUNKS
    total = jnp.zeros((lhs.shape[0], rows_ref.shape[1]), F32)
    for chunk in range(CHUNKS):
        at = slice(chunk * depth, (chunk + 1) * depth)
        chunk_copy(block_ref, rows_ref, sems, chunk).wait()
        rows = rows_ref[at, :]
        high = rows.astype(BF16)
        low = (rows - high.astype(F32)).astype(BF16)
        keep[0, at, :] = high
        keep[1, at, :] = low
        total = total + jnp.dot(lhs[:, at], high, preferred_element_type=F32)
        total = total + jnp.dot(lhs[:, at], low, preferred_element_type=F32)
    return total[:8] + total[8:]


def chunk_copy(block_ref, rows_ref, sems, chunk):
    depth = rows_ref.shape[0] // CHUNKS
    at = pl.ds(chunk * depth, depth)
    return pltpu.make_async_copy(block_ref.at[at, :], rows_ref.at[at, :], sems.at[chunk])


def prepare(block_ref, x_hbm, load_hbm, contact_hbm, rows_hbm, partners_hbm, counts_hbm,
            onehot_ref, valid_ref, own_ref, hown_ref, h_ref, out_ref, first_ref, last_ref, halves_ref,
            held_ref, x_ref, load_ref, contact_ref, rows_ref, partners_ref, counts_ref, sems, more_sems):
    small = [
        pltpu.make_async_copy(source, target, more_sems.at[i])
        for i, (source, target) in enumerate((
            (rows_hbm, rows_ref), (counts_hbm, counts_ref), (x_hbm, x_ref),
            (contact_hbm, contact_ref), (partners_hbm, partners_ref), (load_hbm, load_ref),
        ))
    ]
    for copy in small:
        copy.start()
    for chunk in range(CHUNKS):
        chunk_copy(block_ref, held_ref, sems, chunk).start()
    for copy in small:
        copy.wait()
    x = x_ref[...]
    width = x.shape[1]
    spare = [jnp.full((1, LANES - HALF * JR), -1, jnp.int32)]
    rows = [rows_ref[r] for r in range(ROUNDS)]
    rows = jnp.concatenate(rows[:HALF] + spare + rows[HALF:] + spare, axis=1)
    hit = lax.broadcasted_iota(jnp.int32, (width, JW), 0) == rows
    onehot = jnp.where(hit, 1.0, 0.0).astype(BF16)
    onehot_ref[...] = onehot
    lane = lax.broadcasted_iota(jnp.int32, (8, JW), 1)
    valid = jnp.zeros((8, JW), F32)
    for r in range(ROUNDS):
        start = r // HALF * LANES + r % HALF * JR
        inside = (lane >= start) & (lane < start + counts_ref[0, r])
        valid = jnp.where(inside, 1.0, valid)
    valid_ref[...] = valid
    contact = jnp.broadcast_to(jnp.where(contact_ref[...] == 1, 1.0, 0.0), x.shape)
    own, own_contact = pick(x, onehot, contact)
    own_ref[...] = jnp.concatenate([own, own_contact], axis=0)
    position = lax.broadcasted_iota(jnp.int32, x.shape, 1)
    edge = (position < FACE) | (position >= width - FACE)
    h = spread(valid * own, onehot) + jnp.where(edge, x, 0.0) - load_ref[...]
    h = h + stream_dense(x, block_ref, held_ref, sems, halves_ref)
    h_ref[...] = h
    (hown,) = pick(h, onehot)
    hown_ref[...] = hown
    out_ref[...] = jnp.zeros_like(out_ref)
    place = lax.broadcasted_iota(jnp.int32, (8, LANES), 1) // JR
    for r in range(ROUNDS):
        group, slot = divmod(r, HALF)
        at = slice(group * LANES, (group + 1) * LANES)
        parcel = jnp.zeros((8, LANES), F32)
        for i, jump in enumerate((own, hown, own_contact)):
            block = pltpu.roll(jump[:, at], (i * JR) % LANES, 1) if i else jump[:, at]
            parcel = jnp.where(place == (slot + i) % (LANES // JR), block, parcel)
        out_ref[partners_ref[0, r]] = parcel
    both = jnp.concatenate([x, h, contact], axis=0)
    first_ref[...] = both[:, :FACE]
    last_ref[...] = both[:, width - FACE :]


def first_gradient(partners_ref, where_ref, halves_ref, x_ref, h_ref, own_ref, hown_ref, in_ref,
                   below_in, above_in, valid_ref, onehot_ref,
                   g_ref, gown_ref, far_ref, gfar_ref, below_ref, gbelow_ref, above_ref, gabove_ref,
                   all_ref, masks_ref):
    width = x_ref.shape[1]
    place = lax.broadcasted_iota(jnp.int32, (8, LANES), 1) // JR
    parts = [[jnp.zeros((8, LANES), F32)] * 2 for _ in range(3)]
    for r in range(ROUNDS):
        group, slot = divmod(r, HALF)
        parcel = in_ref[partners_ref[0, r]]
        for i in range(3):
            block = pltpu.roll(parcel, LANES - i * JR, 1) if i else parcel
            parts[i][group] = jnp.where(place == slot, block, parts[i][group])
    far, hfar, far_contact = (jnp.concatenate(part, axis=1) for part in parts)
    valid = valid_ref[...]
    own = own_ref[:8]
    far_ref[...] = jnp.concatenate([far, far_contact], axis=0)
    gown = hown_ref[...] - valid * far
    gfar = hfar - valid * own
    gown_ref[...] = gown
    gfar_ref[...] = gfar
    below, above = below_in[...], above_in[...]
    below_ref[...] = jnp.concatenate([below[:8], below[16:]], axis=0)
    above_ref[...] = jnp.concatenate([above[:8], above[16:]], axis=0)
    layer, layers, core = where_ref[0, 0], where_ref[0, 1], lax.rem(where_ref[0, 2], 2)
    member = lax.broadcasted_iota(jnp.int32, (masks_ref.shape[1], LANES), 0)
    masks_ref[0] = jnp.where(member == 2 * (layer + 1) + core, 1.0, 0.0)
    masks_ref[1] = jnp.where(member == 2 * layer + 1 - core, 1.0, 0.0)
    masks_ref[2] = jnp.where(member >= 0, core, 0).astype(F32)
    gbelow = jnp.where(layer > 0, below[8:16] - x_ref[:, :FACE], 0.0)
    gabove = jnp.where(layer < layers - 1, above[8:16] - x_ref[:, width - FACE :], 0.0)
    gbelow_ref[...] = gbelow
    gabove_ref[...] = gabove
    h = h_ref[...] - spread(valid * far, onehot_ref[...])
    first = h[:, :FACE] - below[:8]
    last = h[:, width - FACE :] - above[:8]
    g = jnp.concatenate([first, h[:, FACE : width - FACE], last], axis=1)
    g_ref[...] = g
    jumps = valid * gown * (gown - gfar)
    terms = first * (first - gbelow) + last * (last - gabove) + jumps[:, :LANES] + jumps[:, LANES:]
    square = lane_sum(g * g)
    curvature = lane_sum(terms) + lane_sum(g * dense(g, halves_ref))
    lane = lax.broadcasted_iota(jnp.int32, (8, LANES), 1)
    row = lax.broadcasted_iota(jnp.int32, (8, LANES), 0)
    line = jnp.where(lane == row, square, 0.0) + jnp.where(lane == row + 8, curvature, 0.0)
    line = jnp.sum(line, axis=0, keepdims=True)
    short = lax.broadcasted_iota(jnp.int32, (1, LANES), 1)
    for r in range(ROUNDS):
        name = jnp.full((1, LANES), partners_ref[0, r], jnp.int32).astype(F32)
        line = jnp.where(short == NAMES + r, name, line)
    all_ref[...] = jnp.broadcast_to(line, all_ref.shape)


def local_sums(g, halves_ref):
    width = g.shape[1]
    first, last = g[:, :FACE], g[:, width - FACE :]
    square = lane_sum(g * g)
    curvature = lane_sum(g * dense(g, halves_ref)) + lane_sum(first * first + last * last)
    lane = lax.broadcasted_iota(jnp.int32, (8, LANES), 1)
    return jnp.where(lane == SQUARE, square, jnp.where(lane == CURVATURE, curvature, 0.0))


def announce(sums_ref, g_ref, gown_ref, valid_ref, below_ref, out_ref):
    own = valid_ref[...] * gown_ref[...]
    squares = own * own
    pairs = g_ref[:, :FACE] * below_ref[...]
    terms = squares[:, :LANES] + squares[:, LANES:] - 2.0 * pairs
    more = jnp.sum(terms, axis=1, keepdims=True)
    lane = lax.broadcasted_iota(jnp.int32, (8, LANES), 1)
    extra = sums_ref[...] + jnp.where(lane == CURVATURE, more, 0.0)
    halves = own[:, :LANES] + extra, own[:, LANES:] + extra
    for plan in range(out_ref.shape[0]):
        out_ref[plan] = halves[plan % 2]


def layer_sums(where_ref, table_ref, in_ref, g_ref, out_ref, *gfar_refs):
    plan = where_ref[0, 2]
    for gfar_ref in gfar_refs:
        gfar_ref[...] = half_of(in_ref, table_ref, plan)
    products = sums = jnp.zeros((8, LANES), F32)
    for p in range(in_ref.shape[0]):
        near = in_ref[p]
        sums = sums + near
        products = products + near * half_of(in_ref, table_ref, p)
    cross = lane_sum(products)
    lane = lax.broadcasted_iota(jnp.int32, (8, LANES), 1)
    sums = 0.5 * sums - jnp.where(lane == CURVATURE, cross, 0.0)
    if gfar_refs:
        sibling = half_of(in_ref, table_ref, plan + 1 - 2 * lax.rem(plan, 2))
        sums = jnp.concatenate([jnp.where(lane < SQUARE, sibling, sums), g_ref[:, :FACE]], axis=1)
    out_ref[...] = jnp.broadcast_to(sums[None], out_ref.shape)


def step_of(in_ref):
    total = in_ref[0, :, :LANES]
    for member in range(1, in_ref.shape[0]):
        total = total + in_ref[member, :, :LANES]
    square = total[:, SQUARE : SQUARE + 1]
    curvature = total[:, CURVATURE : CURVATURE + 1]
    return (square + 1e-6) / (curvature + 1e-6)


def moved(x, g, step, contact):
    out = x - step * g
    return jnp.where(contact == 1, jnp.maximum(out, 0.0), out)


def first_step(in_ref):
    line = jnp.sum(in_ref[...], axis=0, keepdims=True)
    line = jnp.broadcast_to(line, (8, LANES))
    lane = lax.broadcasted_iota(jnp.int32, (8, LANES), 1)
    row = lax.broadcasted_iota(jnp.int32, (8, LANES), 0)
    square = lane_sum(jnp.where(lane == row, line, 0.0))
    curvature = lane_sum(jnp.where(lane == row + 8, line, 0.0))
    return (square + 1e-6) / (curvature + 1e-6)


def chosen(in_ref, mask, columns):
    total = jnp.zeros((8, LANES), F32)
    for member in range(in_ref.shape[0]):
        total = jnp.where(mask[member : member + 1] == 1.0, in_ref[member, :, columns], total)
    return total


def first_face(in_ref, gabove_ref, *refs):
    face_by(first_step(in_ref), gabove_ref[...], *refs)


def next_face(in_ref, masks_ref, *refs):
    face_by(step_of(in_ref), chosen(in_ref, masks_ref[0], slice(LANES, None)), *refs)


def face_by(step, gabove, x_ref, g_ref, contact_ref, load_ref, above_ref, halves_ref,
            x_out, last_out, step_out, above_out):
    x = moved(x_ref[...], g_ref[...], step, contact_ref[...])
    x_out[...] = x
    step_out[...] = jnp.broadcast_to(step, step_out.shape)
    above = moved(above_ref[:8], gabove, step, above_ref[8:])
    above_out[...] = jnp.concatenate([above, above_ref[8:]], axis=0)
    at = slice(x.shape[1] - FACE, x.shape[1])
    last_out[...] = dense(x, halves_ref, at) - load_ref[:, at] + (x[:, at] - above)


def first_rest(in_ref, masks_ref, gfar_ref, *refs):
    *refs, table_ref = refs
    plans = table_ref.shape[0]
    lines = in_ref[pl.ds(0, plans, stride=in_ref.shape[0] // plans), :]
    names = jnp.where(
        masks_ref[2, :1] == 0.0,
        pltpu.roll(lines, LANES - NAMES, 1),
        pltpu.roll(lines, LANES - NAMES - HALF, 1),
    )
    table_ref[...] = names[:, :8].astype(jnp.int32)
    rest_by(gfar_ref[...], *refs)


def next_rest(in_ref, masks_ref, half_ref, *refs):
    lane = lax.broadcasted_iota(jnp.int32, (8, LANES), 1)
    other = chosen(in_ref, masks_ref[1], slice(LANES))
    half, other = half_ref[...], jnp.where(lane < SQUARE, other, 0.0)
    even = masks_ref[2, :1] == 0.0
    rest_by(
        jnp.concatenate([jnp.where(even, half, other), jnp.where(even, other, half)], axis=1), *refs
    )


def rest_by(gfar, step_ref, x_ref, last_ref, load_ref, own_ref, gown_ref, far_ref,
            below_ref, gbelow_ref, valid_ref, onehot_ref, halves_ref,
            g_out, gown_out, sums_out, *halo_outs):
    step, x = step_ref[:, :1], x_ref[...]
    inner = x.shape[1] - FACE
    halo = []
    for held_ref, slope in ((own_ref, gown_ref[...]), (far_ref, gfar), (below_ref, gbelow_ref[...])):
        halo.append(moved(held_ref[:8], slope, step, held_ref[8:]))
    for held_ref, value, held_out in zip((own_ref, far_ref, below_ref), halo, halo_outs):
        held_out[...] = jnp.concatenate([value, held_ref[8:]], axis=0)
    own, far, below = halo
    onehot = onehot_ref[...]
    jumps = spread(valid_ref[...] * (own - far), onehot)
    total = dense(x, halves_ref, slice(inner)) + jumps[:, :inner] - load_ref[:, :inner]
    head = total[:, :FACE] + (x[:, :FACE] - below)
    g = jnp.concatenate([head, total[:, FACE:], last_ref[...]], axis=1)
    g_out[...] = g
    gown_out[...] = pick(g, onehot)[0]
    sums_out[...] = local_sums(g, halves_ref)


def finish(in_ref, x_ref, g_ref, contact_ref, x_out, g_out):
    g = g_ref[...]
    g_out[...] = g
    x_out[...] = moved(x_ref[...], g, step_of(in_ref), contact_ref[...])


def swap(outgoing, axis, groups=None):
    return lax.all_to_all(
        outgoing, axis, split_axis=0, concat_axis=0, tiled=True, axis_index_groups=groups
    )


def lift(face, step):
    layers = lax.axis_size("layer")
    return lax.ppermute(
        face, "layer", [(i, i + step) for i in range(layers) if 0 <= i + step < layers]
    )


def shards(dual_block, start, load, partners, jump_rows, counts, contact):
    block, x, target = dual_block[0, 0], start[0, 0], load[0, 0]
    rows, amounts, flags = jump_rows.reshape(ROUNDS, 1, JR), counts[0], contact[0]
    loads, width = x.shape
    plans, layers = lax.axis_size("plan"), lax.axis_size("layer")
    field, jump, face = shape(loads, width), shape(loads, JW), shape(loads, FACE)
    jump2, face2, face3 = shape(2 * loads, JW), shape(2 * loads, FACE), shape(3 * loads, FACE)
    flops = 4 * 16 * width * width
    position = jnp.stack([lax.axis_index("layer"), layers, lax.axis_index("plan")])
    position = position.astype(jnp.int32).reshape(1, 3)
    amounts, position = lax.optimization_barrier((amounts, position))
    columns = [
        [(chip + core) * layers + layer for layer in range(layers) for core in range(2)]
        for chip in range(0, plans, 2)
    ]
    held = pltpu.VMEM((width, width), F32)
    chunk_sems = pltpu.SemaphoreType.DMA((CHUNKS,))

    onehot, valid, own, hown, h, out, first, last, halves = call(
        prepare, "prepare",
        (shape(width, JW, dtype=BF16), jump, jump2, jump, field, shape(plans, loads, LANES), face3, face3,
         shape(2, width, width, dtype=BF16)),
        [HBM] * 7, 16, flops, 4 * width * width,
        [
            held, pltpu.VMEM(x.shape, F32), pltpu.VMEM(target.shape, F32),
            pltpu.VMEM(flags.shape, jnp.int32), pltpu.VMEM(rows.shape, jnp.int32),
            pltpu.SMEM(partners.shape, jnp.int32), pltpu.SMEM(amounts.shape, jnp.int32),
            chunk_sems, pltpu.SemaphoreType.DMA((6,)),
        ],
    )(*(pltpu.with_memory_space_constraint(a, pltpu.HBM) for a in (block, x, target, flags, rows, partners, amounts)))
    below, above, out = lax.optimization_barrier((lift(last, 1), lift(first, -1), out))
    incoming = swap(out, "plan")
    g, gown, far, gfar, below, gbelow, above, gabove, out, masks = call(
        first_gradient, "first_gradient",
        (field, jump, jump2, jump, face2, face, face2, face,
         shape(plans * layers, LANES), shape(3, 2 * layers, LANES)),
        [SMEM] * 2 + [VMEM] * 10, 12, flops, 4 * width * width,
    )(partners, position, halves, x, h, own, hown, incoming, below, above, valid, onehot)
    incoming = swap(out, ("plan", "layer"))

    early = (field, face, face, face2)
    x, last, step, above = call(
        first_face, "first_face", early, [VMEM] * 8, 12, flops // 8, width * width // 2,
    )(incoming, gabove, x, g, flags, target, above, halves)
    late = (field, jump, face, jump2, jump2, face2)
    below_next = lift(last, 1)
    g, gown, sums, own, far, below, table = call(
        first_rest, "first_rest", late + (shape(plans, 8, dtype=jnp.int32),),
        [VMEM] * 15, 12, 2 * flops, 8 * width * width,
    )(incoming, masks, gfar, step, x, last, target, own, gown, far, below, gbelow, valid, onehot, halves)

    for iteration in range(1, ITERS):
        gbelow = below_next
        out = call(announce, "announce", shape(plans, loads, LANES), [VMEM] * 5, 8)(
            sums, g, gown, valid, gbelow
        )
        ending = iteration == ITERS - 1
        parcel = shape(2 * layers, loads, LANES if ending else LANES + FACE)
        out, *half = call(
            layer_sums, "layer_sums", (parcel,) + (() if ending else (shape(loads, LANES),)),
            [SMEM] * 2 + [VMEM] * 2, 8,
        )(position, table, swap(out, "plan"), g)
        incoming = swap(out, ("plan", "layer"), columns)
        if ending:
            x, g = call(finish, "finish", (field, field), [VMEM] * 4, 8)(incoming, x, g, flags)
            break
        x, last, step, above = call(
            next_face, "next_face", early, [VMEM] * 8, 12, flops // 8, width * width // 2,
        )(incoming, masks, x, g, flags, target, above, halves)
        below_next = lift(last, 1)
        g, gown, sums, *halo = call(
            next_rest, "next_rest", late[:3] if iteration == ITERS - 2 else late,
            [VMEM] * 15, 12, 2 * flops, 8 * width * width,
        )(incoming, masks, *half, step, x, last, target, own, gown, far, below, gbelow,
          valid, onehot, halves)
        own, far, below = halo or (None,) * 3
    return x[None, None], g[None, None]


def solution(mesh):
    in_specs = (
        P("layer", "plan", None, None),
        P("layer", "plan", None, None),
        P("layer", "plan", None, None),
        P("plan", None),
        P("layer", "plan", None, None),
        P("layer", "plan", None),
        P("layer", "plan", None),
    )
    out_specs = (P("layer", "plan", None, None), P("layer", "plan", None, None))
    return jax.shard_map(shards, mesh=mesh, in_specs=in_specs, out_specs=out_specs, check_vma=False)
```

```python
import functools

import jax
import jax.numpy as jnp
from jax import lax
from jax.experimental import pallas as pl
from jax.experimental.pallas import tpu as pltpu
from jax.sharding import PartitionSpec as P

FACE = 128
JR = 32
ROUNDS = 6
ITERS = 4
LANES = 128
HALF = 3
JW = 2 * LANES
CHUNKS = 4
NAMES = 16
SQUARE, CURVATURE = HALF * JR, HALF * JR + 1
F32 = jnp.float32
BF16 = jnp.bfloat16

VMEM = pl.BlockSpec(memory_space=pltpu.VMEM)
SMEM = pl.BlockSpec(memory_space=pltpu.SMEM)
HBM = pl.BlockSpec(memory_space=pltpu.HBM)


def shape(*dims, dtype=F32):
    return jax.ShapeDtypeStruct(dims, dtype)


def call(body, name, outs, specs, limit, flops=0, traffic=0, scratch=()):
    return pl.pallas_call(
        body,
        name=name,
        out_shape=outs,
        in_specs=specs,
        scratch_shapes=scratch,
        out_specs=jax.tree.map(lambda out: VMEM if isinstance(out, jax.ShapeDtypeStruct) else HBM, outs),
        compiler_params=pltpu.CompilerParams(vmem_limit_bytes=limit * 2**20),
        cost_estimate=pl.CostEstimate(flops=flops, bytes_accessed=traffic, transcendentals=0),
    )


def pieces(value, count):
    parts = []
    for _ in range(count):
        part = value.astype(BF16).astype(F32)
        parts.append(part)
        value = value - part
    return parts


def lane_sum(value):
    return jnp.sum(value, axis=1, keepdims=True)


def dense(field, high_ref, low_ref, columns=slice(None), before_low=None):
    lhs = jnp.concatenate(pieces(field, 2), axis=0).astype(BF16)
    total = jnp.dot(lhs, high_ref[:, columns], preferred_element_type=F32)
    if before_low is not None:
        before_low()
    total = total + jnp.dot(lhs, low_ref[:, columns], preferred_element_type=F32)
    return total[:8] + total[8:]


def pick(field, onehot, *extra):
    lhs = jnp.concatenate(pieces(field, 3) + list(extra), axis=0).astype(BF16)
    out = jnp.dot(lhs, onehot, preferred_element_type=F32)
    return [out[:8] + out[8:16] + out[16:24]] + [
        out[24 + 8 * i : 32 + 8 * i] for i in range(len(extra))
    ]


def spread(jumps, onehot):
    lhs = jnp.concatenate(pieces(jumps, 3), axis=0).astype(BF16)
    out = lax.dot_general(lhs, onehot, (((1,), (1,)), ((), ())), preferred_element_type=F32)
    return out[:8] + out[8:16] + out[16:24]


def half_of(in_ref, table_ref, plan):
    place = lax.broadcasted_iota(jnp.int32, (8, LANES), 1) // JR
    total = jnp.zeros((8, LANES), F32)
    for r in range(HALF):
        total = jnp.where(place == r, in_ref[table_ref[plan, r]], total)
    return total


def stream_dense(field, block_ref, rows_ref, sems, high_ref, low_ref, give):
    lhs = jnp.concatenate(pieces(field, 2), axis=0).astype(BF16)
    depth = rows_ref.shape[0] // CHUNKS
    total = jnp.zeros((lhs.shape[0], rows_ref.shape[1]), F32)
    for chunk in range(CHUNKS):
        at = slice(chunk * depth, (chunk + 1) * depth)
        chunk_copy(block_ref, rows_ref, sems, chunk).wait()
        rows = rows_ref[at, :]
        high = rows.astype(BF16)
        low = (rows - high.astype(F32)).astype(BF16)
        high_ref[at, :] = high
        low_ref[at, :] = low
        give(chunk).start()
        total = total + jnp.dot(lhs[:, at], high, preferred_element_type=F32)
        total = total + jnp.dot(lhs[:, at], low, preferred_element_type=F32)
    return total[:8] + total[8:]


def chunk_copy(source_ref, target_ref, sems, chunk):
    depth = source_ref.shape[0] // CHUNKS
    at = pl.ds(chunk * depth, depth)
    return pltpu.make_async_copy(source_ref.at[at, :], target_ref.at[at, :], sems.at[chunk])


def prepare(block_ref, x_hbm, load_hbm, contact_hbm, rows_hbm, partners_hbm, counts_hbm,
            onehot_ref, valid_ref, own_ref, hown_ref, h_ref, out_ref, first_ref, last_ref, high_ref,
            low_hbm, held_ref, low_ref, x_ref, load_ref, contact_ref, rows_ref, partners_ref, counts_ref,
            sems, low_sems, more_sems):
    small = [
        pltpu.make_async_copy(source, target, more_sems.at[i])
        for i, (source, target) in enumerate((
            (rows_hbm, rows_ref), (counts_hbm, counts_ref), (x_hbm, x_ref),
            (contact_hbm, contact_ref), (partners_hbm, partners_ref), (load_hbm, load_ref),
        ))
    ]
    for copy in small:
        copy.start()
    for chunk in range(CHUNKS):
        chunk_copy(block_ref, held_ref, sems, chunk).start()
    for copy in small:
        copy.wait()
    x = x_ref[...]
    width = x.shape[1]
    spare = [jnp.full((1, LANES - HALF * JR), -1, jnp.int32)]
    rows = [rows_ref[r] for r in range(ROUNDS)]
    rows = jnp.concatenate(rows[:HALF] + spare + rows[HALF:] + spare, axis=1)
    hit = lax.broadcasted_iota(jnp.int32, (width, JW), 0) == rows
    onehot = jnp.where(hit, 1.0, 0.0).astype(BF16)
    onehot_ref[...] = onehot
    lane = lax.broadcasted_iota(jnp.int32, (8, JW), 1)
    valid = jnp.zeros((8, JW), F32)
    for r in range(ROUNDS):
        start = r // HALF * LANES + r % HALF * JR
        inside = (lane >= start) & (lane < start + counts_ref[0, r])
        valid = jnp.where(inside, 1.0, valid)
    valid_ref[...] = valid
    contact = jnp.broadcast_to(jnp.where(contact_ref[...] == 1, 1.0, 0.0), x.shape)
    own, own_contact = pick(x, onehot, contact)
    own_ref[...] = jnp.concatenate([own, own_contact], axis=0)
    position = lax.broadcasted_iota(jnp.int32, x.shape, 1)
    edge = (position < FACE) | (position >= width - FACE)
    h = spread(valid * own, onehot) + jnp.where(edge, x, 0.0) - load_ref[...]
    low_copy = functools.partial(chunk_copy, low_ref, low_hbm, low_sems)
    h = h + stream_dense(x, block_ref, held_ref, sems, high_ref, low_ref, low_copy)
    h_ref[...] = h
    (hown,) = pick(h, onehot)
    hown_ref[...] = hown
    out_ref[...] = jnp.zeros_like(out_ref)
    place = lax.broadcasted_iota(jnp.int32, (8, LANES), 1) // JR
    for r in range(ROUNDS):
        group, slot = divmod(r, HALF)
        at = slice(group * LANES, (group + 1) * LANES)
        parcel = jnp.zeros((8, LANES), F32)
        for i, jump in enumerate((own, hown, own_contact)):
            block = pltpu.roll(jump[:, at], (i * JR) % LANES, 1) if i else jump[:, at]
            parcel = jnp.where(place == (slot + i) % (LANES // JR), block, parcel)
        out_ref[partners_ref[0, r]] = parcel
    both = jnp.concatenate([x, h, contact], axis=0)
    first_ref[...] = both[:, :FACE]
    last_ref[...] = both[:, width - FACE :]
    for chunk in range(CHUNKS):
        low_copy(chunk).wait()


def first_gradient(partners_ref, where_ref, low_hbm, high_ref, x_ref, h_ref, own_ref, hown_ref, in_ref,
                   below_in, above_in, valid_ref, onehot_ref,
                   g_ref, gown_ref, far_ref, gfar_ref, below_ref, gbelow_ref, above_ref, gabove_ref,
                   all_ref, masks_ref, low_ref, sem):
    low_copy = pltpu.make_async_copy(low_hbm, low_ref, sem)
    low_copy.start()
    width = x_ref.shape[1]
    place = lax.broadcasted_iota(jnp.int32, (8, LANES), 1) // JR
    parts = [[jnp.zeros((8, LANES), F32)] * 2 for _ in range(3)]
    for r in range(ROUNDS):
        group, slot = divmod(r, HALF)
        parcel = in_ref[partners_ref[0, r]]
        for i in range(3):
            block = pltpu.roll(parcel, LANES - i * JR, 1) if i else parcel
            parts[i][group] = jnp.where(place == slot, block, parts[i][group])
    far, hfar, far_contact = (jnp.concatenate(part, axis=1) for part in parts)
    valid = valid_ref[...]
    own = own_ref[:8]
    far_ref[...] = jnp.concatenate([far, far_contact], axis=0)
    gown = hown_ref[...] - valid * far
    gfar = hfar - valid * own
    gown_ref[...] = gown
    gfar_ref[...] = gfar
    below, above = below_in[...], above_in[...]
    below_ref[...] = jnp.concatenate([below[:8], below[16:]], axis=0)
    above_ref[...] = jnp.concatenate([above[:8], above[16:]], axis=0)
    layer, layers, core = where_ref[0, 0], where_ref[0, 1], lax.rem(where_ref[0, 2], 2)
    member = lax.broadcasted_iota(jnp.int32, (masks_ref.shape[1], LANES), 0)
    masks_ref[0] = jnp.where(member == 2 * (layer + 1) + core, 1.0, 0.0)
    masks_ref[1] = jnp.where(member == 2 * layer + 1 - core, 1.0, 0.0)
    masks_ref[2] = jnp.where(member >= 0, core, 0).astype(F32)
    gbelow = jnp.where(layer > 0, below[8:16] - x_ref[:, :FACE], 0.0)
    gabove = jnp.where(layer < layers - 1, above[8:16] - x_ref[:, width - FACE :], 0.0)
    gbelow_ref[...] = gbelow
    gabove_ref[...] = gabove
    h = h_ref[...] - spread(valid * far, onehot_ref[...])
    first = h[:, :FACE] - below[:8]
    last = h[:, width - FACE :] - above[:8]
    g = jnp.concatenate([first, h[:, FACE : width - FACE], last], axis=1)
    g_ref[...] = g
    jumps = valid * gown * (gown - gfar)
    terms = first * (first - gbelow) + last * (last - gabove) + jumps[:, :LANES] + jumps[:, LANES:]
    square = lane_sum(g * g)
    image = dense(g, high_ref, low_ref, before_low=low_copy.wait)
    curvature = lane_sum(terms) + lane_sum(g * image)
    lane = lax.broadcasted_iota(jnp.int32, (8, LANES), 1)
    row = lax.broadcasted_iota(jnp.int32, (8, LANES), 0)
    line = jnp.where(lane == row, square, 0.0) + jnp.where(lane == row + 8, curvature, 0.0)
    line = jnp.sum(line, axis=0, keepdims=True)
    short = lax.broadcasted_iota(jnp.int32, (1, LANES), 1)
    for r in range(ROUNDS):
        name = jnp.full((1, LANES), partners_ref[0, r], jnp.int32).astype(F32)
        line = jnp.where(short == NAMES + r, name, line)
    all_ref[...] = jnp.broadcast_to(line, all_ref.shape)


def local_sums(g, high_ref, low_ref):
    width = g.shape[1]
    first, last = g[:, :FACE], g[:, width - FACE :]
    square = lane_sum(g * g)
    curvature = lane_sum(g * dense(g, high_ref, low_ref)) + lane_sum(first * first + last * last)
    lane = lax.broadcasted_iota(jnp.int32, (8, LANES), 1)
    return jnp.where(lane == SQUARE, square, jnp.where(lane == CURVATURE, curvature, 0.0))


def announce(sums_ref, g_ref, gown_ref, valid_ref, below_ref, out_ref):
    own = valid_ref[...] * gown_ref[...]
    squares = own * own
    pairs = g_ref[:, :FACE] * below_ref[...]
    terms = squares[:, :LANES] + squares[:, LANES:] - 2.0 * pairs
    more = jnp.sum(terms, axis=1, keepdims=True)
    lane = lax.broadcasted_iota(jnp.int32, (8, LANES), 1)
    extra = sums_ref[...] + jnp.where(lane == CURVATURE, more, 0.0)
    halves = own[:, :LANES] + extra, own[:, LANES:] + extra
    for plan in range(out_ref.shape[0]):
        out_ref[plan] = halves[plan % 2]


def layer_sums(where_ref, table_ref, in_ref, g_ref, out_ref, *gfar_refs):
    plan = where_ref[0, 2]
    for gfar_ref in gfar_refs:
        gfar_ref[...] = half_of(in_ref, table_ref, plan)
    products = sums = jnp.zeros((8, LANES), F32)
    for p in range(in_ref.shape[0]):
        near = in_ref[p]
        sums = sums + near
        products = products + near * half_of(in_ref, table_ref, p)
    cross = lane_sum(products)
    lane = lax.broadcasted_iota(jnp.int32, (8, LANES), 1)
    sums = 0.5 * sums - jnp.where(lane == CURVATURE, cross, 0.0)
    if gfar_refs:
        sibling = half_of(in_ref, table_ref, plan + 1 - 2 * lax.rem(plan, 2))
        sums = jnp.concatenate([jnp.where(lane < SQUARE, sibling, sums), g_ref[:, :FACE]], axis=1)
    out_ref[...] = jnp.broadcast_to(sums[None], out_ref.shape)


def step_of(in_ref):
    total = in_ref[0, :, :LANES]
    for member in range(1, in_ref.shape[0]):
        total = total + in_ref[member, :, :LANES]
    square = total[:, SQUARE : SQUARE + 1]
    curvature = total[:, CURVATURE : CURVATURE + 1]
    return (square + 1e-6) / (curvature + 1e-6)


def moved(x, g, step, contact):
    out = x - step * g
    return jnp.where(contact == 1, jnp.maximum(out, 0.0), out)


def first_step(in_ref):
    line = jnp.sum(in_ref[...], axis=0, keepdims=True)
    line = jnp.broadcast_to(line, (8, LANES))
    lane = lax.broadcasted_iota(jnp.int32, (8, LANES), 1)
    row = lax.broadcasted_iota(jnp.int32, (8, LANES), 0)
    square = lane_sum(jnp.where(lane == row, line, 0.0))
    curvature = lane_sum(jnp.where(lane == row + 8, line, 0.0))
    return (square + 1e-6) / (curvature + 1e-6)


def chosen(in_ref, mask, columns):
    total = jnp.zeros((8, LANES), F32)
    for member in range(in_ref.shape[0]):
        total = jnp.where(mask[member : member + 1] == 1.0, in_ref[member, :, columns], total)
    return total


def first_face(in_ref, gabove_ref, *refs):
    face_by(first_step(in_ref), gabove_ref[...], *refs)


def next_face(in_ref, masks_ref, *refs):
    face_by(step_of(in_ref), chosen(in_ref, masks_ref[0], slice(LANES, None)), *refs)


def face_by(step, gabove, x_ref, g_ref, contact_ref, load_ref, above_ref, high_ref, low_ref,
            x_out, last_out, step_out, *above_outs):
    x = moved(x_ref[...], g_ref[...], step, contact_ref[...])
    x_out[...] = x
    step_out[...] = jnp.broadcast_to(step, step_out.shape)
    above = moved(above_ref[:8], gabove, step, above_ref[8:])
    for above_out in above_outs:
        above_out[...] = jnp.concatenate([above, above_ref[8:]], axis=0)
    at = slice(x.shape[1] - FACE, x.shape[1])
    last_out[...] = dense(x, high_ref, low_ref, at) - load_ref[:, at] + (x[:, at] - above)


def first_rest(in_ref, masks_ref, gfar_ref, *refs):
    *refs, table_ref = refs
    plans = table_ref.shape[0]
    lines = in_ref[pl.ds(0, plans, stride=in_ref.shape[0] // plans), :]
    names = jnp.where(
        masks_ref[2, :1] == 0.0,
        pltpu.roll(lines, LANES - NAMES, 1),
        pltpu.roll(lines, LANES - NAMES - HALF, 1),
    )
    table_ref[...] = names[:, :8].astype(jnp.int32)
    rest_by(gfar_ref[...], *refs)


def next_rest(in_ref, masks_ref, half_ref, *refs):
    lane = lax.broadcasted_iota(jnp.int32, (8, LANES), 1)
    other = chosen(in_ref, masks_ref[1], slice(LANES))
    half, other = half_ref[...], jnp.where(lane < SQUARE, other, 0.0)
    even = masks_ref[2, :1] == 0.0
    rest_by(
        jnp.concatenate([jnp.where(even, half, other), jnp.where(even, other, half)], axis=1), *refs
    )


def rest_by(gfar, step_ref, x_ref, last_ref, load_ref, own_ref, gown_ref, far_ref,
            below_ref, gbelow_ref, valid_ref, onehot_ref, high_ref, low_ref,
            g_out, gown_out, sums_out, *halo_outs):
    step, x = step_ref[:, :1], x_ref[...]
    inner = x.shape[1] - FACE
    halo = []
    for held_ref, slope in ((own_ref, gown_ref[...]), (far_ref, gfar), (below_ref, gbelow_ref[...])):
        halo.append(moved(held_ref[:8], slope, step, held_ref[8:]))
    for held_ref, value, held_out in zip((own_ref, far_ref, below_ref), halo, halo_outs):
        held_out[...] = jnp.concatenate([value, held_ref[8:]], axis=0)
    own, far, below = halo
    onehot = onehot_ref[...]
    jumps = spread(valid_ref[...] * (own - far), onehot)
    total = dense(x, high_ref, low_ref, slice(inner)) + jumps[:, :inner] - load_ref[:, :inner]
    head = total[:, :FACE] + (x[:, :FACE] - below)
    g = jnp.concatenate([head, total[:, FACE:], last_ref[...]], axis=1)
    g_out[...] = g
    gown_out[...] = pick(g, onehot)[0]
    sums_out[...] = local_sums(g, high_ref, low_ref)


def finish(in_ref, x_ref, g_ref, contact_ref, x_out, g_out):
    g = g_ref[...]
    g_out[...] = g
    x_out[...] = moved(x_ref[...], g, step_of(in_ref), contact_ref[...])


def swap(outgoing, axis, groups=None):
    return lax.all_to_all(
        outgoing, axis, split_axis=0, concat_axis=0, tiled=True, axis_index_groups=groups
    )


def lift(face, step):
    layers = lax.axis_size("layer")
    return lax.ppermute(
        face, "layer", [(i, i + step) for i in range(layers) if 0 <= i + step < layers]
    )


def shards(dual_block, start, load, partners, jump_rows, counts, contact):
    block, x, target = dual_block[0, 0], start[0, 0], load[0, 0]
    rows, amounts, flags = jump_rows.reshape(ROUNDS, 1, JR), counts[0], contact[0]
    loads, width = x.shape
    plans, layers = lax.axis_size("plan"), lax.axis_size("layer")
    field, jump, face = shape(loads, width), shape(loads, JW), shape(loads, FACE)
    jump2, face2, face3 = shape(2 * loads, JW), shape(2 * loads, FACE), shape(3 * loads, FACE)
    flops = 4 * 16 * width * width
    position = jnp.stack([lax.axis_index("layer"), layers, lax.axis_index("plan")])
    position = position.astype(jnp.int32).reshape(1, 3)
    amounts, position = lax.optimization_barrier((amounts, position))
    columns = [
        [(chip + core) * layers + layer for layer in range(layers) for core in range(2)]
        for chip in range(0, plans, 2)
    ]
    half_shape = shape(width, width, dtype=BF16)
    held = pltpu.VMEM((width, width), F32)
    chunk_sems = pltpu.SemaphoreType.DMA((CHUNKS,))

    onehot, valid, own, hown, h, out, first, last, high, low = call(
        prepare, "prepare",
        (shape(width, JW, dtype=BF16), jump, jump2, jump, field, shape(plans, loads, LANES), face3, face3,
         half_shape, pltpu.HBM(half_shape.shape, BF16)),
        [HBM] * 7, 16, flops, 4 * width * width,
        [
            held, pltpu.VMEM((width, width), BF16), pltpu.VMEM(x.shape, F32), pltpu.VMEM(target.shape, F32),
            pltpu.VMEM(flags.shape, jnp.int32), pltpu.VMEM(rows.shape, jnp.int32),
            pltpu.SMEM(partners.shape, jnp.int32), pltpu.SMEM(amounts.shape, jnp.int32),
            chunk_sems, chunk_sems, pltpu.SemaphoreType.DMA((6,)),
        ],
    )(*(pltpu.with_memory_space_constraint(a, pltpu.HBM) for a in (block, x, target, flags, rows, partners, amounts)))
    incoming = swap(out, "plan")
    below, above = lift(last, 1), lift(first, -1)
    g, gown, far, gfar, below, gbelow, above, gabove, out, masks, low = call(
        first_gradient, "first_gradient",
        (field, jump, jump2, jump, face2, face, face2, face,
         shape(plans * layers, LANES), shape(3, 2 * layers, LANES), half_shape),
        [SMEM] * 2 + [HBM] + [VMEM] * 10, 12, flops, 4 * width * width, [pltpu.SemaphoreType.DMA],
    )(partners, position, pltpu.with_memory_space_constraint(low, pltpu.HBM), high, x, h, own, hown, incoming, below, above, valid, onehot)
    incoming = swap(out, ("plan", "layer"))

    early = (field, face, face, face2)
    x, last, step, above = call(
        first_face, "first_face", early, [VMEM] * 9, 12, flops // 8, width * width // 2,
    )(incoming, gabove, x, g, flags, target, above, high, low)
    late = (field, jump, face, jump2, jump2, face2)
    below_next = lift(last, 1)
    g, gown, sums, own, far, below, table = call(
        first_rest, "first_rest", late + (shape(plans, 8, dtype=jnp.int32),),
        [VMEM] * 16, 12, 2 * flops, 8 * width * width,
    )(incoming, masks, gfar, step, x, last, target, own, gown, far, below, gbelow, valid, onehot, high, low)

    for iteration in range(1, ITERS):
        gbelow = below_next
        out = call(announce, "announce", shape(plans, loads, LANES), [VMEM] * 5, 8)(
            sums, g, gown, valid, gbelow
        )
        ending = iteration == ITERS - 1
        parcel = shape(2 * layers, loads, LANES if ending else LANES + FACE)
        out, *half = call(
            layer_sums, "layer_sums", (parcel,) + (() if ending else (shape(loads, LANES),)),
            [SMEM] * 2 + [VMEM] * 2, 8,
        )(position, table, swap(out, "plan"), g)
        incoming = swap(out, ("plan", "layer"), columns)
        if ending:
            x, g = call(finish, "finish", (field, field), [VMEM] * 4, 8)(incoming, x, g, flags)
            break
        x, last, step, *above = call(
            next_face, "next_face", early[:3] if iteration == ITERS - 2 else early, [VMEM] * 9, 12, flops // 8, width * width // 2,
        )(incoming, masks, x, g, flags, target, above, high, low)
        below_next = lift(last, 1)
        g, gown, sums, *halo = call(
            next_rest, "next_rest", late[:3] if iteration == ITERS - 2 else late,
            [VMEM] * 16, 12, 2 * flops, 8 * width * width,
        )(incoming, masks, *half, step, x, last, target, own, gown, far, below, gbelow,
          valid, onehot, high, low)
        (above,), (own, far, below) = above or (None,), halo or (None,) * 3
    return x[None, None], g[None, None]


def solution(mesh):
    in_specs = (
        P("layer", "plan", None, None),
        P("layer", "plan", None, None),
        P("layer", "plan", None, None),
        P("plan", None),
        P("layer", "plan", None, None),
        P("layer", "plan", None),
        P("layer", "plan", None),
    )
    out_specs = (P("layer", "plan", None, None), P("layer", "plan", None, None))
    return jax.shard_map(shards, mesh=mesh, in_specs=in_specs, out_specs=out_specs, check_vma=False)
```

```python
import jax
import jax.numpy as jnp
from jax import lax
from jax.experimental import pallas as pl
from jax.experimental.pallas import tpu as pltpu
from jax.sharding import PartitionSpec as P

FACE = 128
JR = 32
ROUNDS = 6
ITERS = 4
LANES = 128
HALF = 3
JW = 2 * LANES
CHUNKS = 4
LOW_CHUNKS = 8
NAMES = 16
SQUARE, CURVATURE = HALF * JR, HALF * JR + 1
F32 = jnp.float32
BF16 = jnp.bfloat16

VMEM = pl.BlockSpec(memory_space=pltpu.VMEM)
SMEM = pl.BlockSpec(memory_space=pltpu.SMEM)
HBM = pl.BlockSpec(memory_space=pltpu.HBM)


def shape(*dims, dtype=F32):
    return jax.ShapeDtypeStruct(dims, dtype)


def call(body, name, outs, specs, limit, flops=0, traffic=0, scratch=()):
    return pl.pallas_call(
        body,
        name=name,
        out_shape=outs,
        in_specs=specs,
        scratch_shapes=scratch,
        out_specs=jax.tree.map(lambda out: VMEM if isinstance(out, jax.ShapeDtypeStruct) else HBM, outs),
        compiler_params=pltpu.CompilerParams(vmem_limit_bytes=limit * 2**20),
        cost_estimate=pl.CostEstimate(flops=flops, bytes_accessed=traffic, transcendentals=0),
    )


def pieces(value, count):
    parts = []
    for _ in range(count):
        part = value.astype(BF16).astype(F32)
        parts.append(part)
        value = value - part
    return parts


def lane_sum(value):
    return jnp.sum(value, axis=1, keepdims=True)


def dense(field, high_ref, low_ref, columns=slice(None), copies=()):
    lhs = jnp.concatenate(pieces(field, 2), axis=0).astype(BF16)
    total = jnp.dot(lhs, high_ref[:, columns], preferred_element_type=F32)
    for copy in copies:
        copy.wait()
    total = total + jnp.dot(lhs, low_ref[:, columns], preferred_element_type=F32)
    return total[:8] + total[8:]


def pick(field, onehot, *extra):
    lhs = jnp.concatenate(pieces(field, 3) + list(extra), axis=0).astype(BF16)
    out = jnp.dot(lhs, onehot, preferred_element_type=F32)
    return [out[:8] + out[8:16] + out[16:24]] + [
        out[24 + 8 * i : 32 + 8 * i] for i in range(len(extra))
    ]


def spread(jumps, onehot):
    lhs = jnp.concatenate(pieces(jumps, 3), axis=0).astype(BF16)
    out = lax.dot_general(lhs, onehot, (((1,), (1,)), ((), ())), preferred_element_type=F32)
    return out[:8] + out[8:16] + out[16:24]


def half_of(in_ref, table_ref, plan):
    place = lax.broadcasted_iota(jnp.int32, (8, LANES), 1) // JR
    total = jnp.zeros((8, LANES), F32)
    for r in range(HALF):
        total = jnp.where(place == r, in_ref[table_ref[plan, r]], total)
    return total


def stream_dense(field, block_ref, rows_ref, sems, high_ref, low_ref):
    lhs = jnp.concatenate(pieces(field, 2), axis=0).astype(BF16)
    depth = rows_ref.shape[0] // CHUNKS
    total = jnp.zeros((lhs.shape[0], rows_ref.shape[1]), F32)
    for chunk in range(CHUNKS):
        at = slice(chunk * depth, (chunk + 1) * depth)
        chunk_copy(block_ref, rows_ref, sems, chunk, CHUNKS).wait()
        rows = rows_ref[at, :]
        high = rows.astype(BF16)
        low = (rows - high.astype(F32)).astype(BF16)
        high_ref[at, :] = high
        low_ref[at, :] = low
        total = total + jnp.dot(lhs[:, at], high, preferred_element_type=F32)
        total = total + jnp.dot(lhs[:, at], low, preferred_element_type=F32)
    return total[:8] + total[8:]


def chunk_copy(source_ref, target_ref, sems, chunk, chunks):
    depth = source_ref.shape[0] // chunks
    at = pl.ds(chunk * depth, depth)
    return pltpu.make_async_copy(source_ref.at[at, :], target_ref.at[at, :], sems.at[chunk])


def low_copies(source_ref, target_ref, sems):
    return [chunk_copy(source_ref, target_ref, sems, chunk, LOW_CHUNKS) for chunk in range(LOW_CHUNKS)]


def prepare(block_ref, x_hbm, load_hbm, contact_hbm, rows_hbm, counts_hbm,
            onehot_ref, valid_ref, own_ref, h_ref, first_ref, last_ref, high_ref, low_ref,
            held_ref, x_ref, load_ref, contact_ref, rows_ref, counts_ref, sems, more_sems):
    small = [
        pltpu.make_async_copy(source, target, more_sems.at[i])
        for i, (source, target) in enumerate((
            (rows_hbm, rows_ref), (counts_hbm, counts_ref), (x_hbm, x_ref),
            (contact_hbm, contact_ref), (load_hbm, load_ref),
        ))
    ]
    for copy in small:
        copy.start()
    for chunk in range(CHUNKS):
        chunk_copy(block_ref, held_ref, sems, chunk, CHUNKS).start()
    for copy in small:
        copy.wait()
    x = x_ref[...]
    width = x.shape[1]
    spare = [jnp.full((1, LANES - HALF * JR), -1, jnp.int32)]
    rows = [rows_ref[r] for r in range(ROUNDS)]
    rows = jnp.concatenate(rows[:HALF] + spare + rows[HALF:] + spare, axis=1)
    hit = lax.broadcasted_iota(jnp.int32, (width, JW), 0) == rows
    onehot = jnp.where(hit, 1.0, 0.0).astype(BF16)
    onehot_ref[...] = onehot
    lane = lax.broadcasted_iota(jnp.int32, (8, JW), 1)
    valid = jnp.zeros((8, JW), F32)
    for r in range(ROUNDS):
        start = r // HALF * LANES + r % HALF * JR
        inside = (lane >= start) & (lane < start + counts_ref[0, r])
        valid = jnp.where(inside, 1.0, valid)
    valid_ref[...] = valid
    contact = jnp.broadcast_to(jnp.where(contact_ref[...] == 1, 1.0, 0.0), x.shape)
    own, own_contact = pick(x, onehot, contact)
    own_ref[...] = jnp.concatenate([own, own_contact], axis=0)
    position = lax.broadcasted_iota(jnp.int32, x.shape, 1)
    edge = (position < FACE) | (position >= width - FACE)
    h = spread(valid * own, onehot) + jnp.where(edge, x, 0.0) - load_ref[...]
    h = h + stream_dense(x, block_ref, held_ref, sems, high_ref, low_ref)
    h_ref[...] = h
    both = jnp.concatenate([x, h, contact], axis=0)
    first_ref[...] = both[:, :FACE]
    last_ref[...] = both[:, width - FACE :]


def address(partners_hbm, own_ref, h_ref, onehot_ref, low_ref,
            hown_ref, out_ref, low_hbm, partners_ref, sem, low_sems):
    names = pltpu.make_async_copy(partners_hbm, partners_ref, sem)
    names.start()
    copies = low_copies(low_ref, low_hbm, low_sems)
    for copy in copies:
        copy.start()
    own, own_contact = own_ref[:8], own_ref[8:]
    (hown,) = pick(h_ref[...], onehot_ref[...])
    hown_ref[...] = hown
    names.wait()
    out_ref[...] = jnp.zeros_like(out_ref)
    place = lax.broadcasted_iota(jnp.int32, (8, LANES), 1) // JR
    for r in range(ROUNDS):
        group, slot = divmod(r, HALF)
        at = slice(group * LANES, (group + 1) * LANES)
        parcel = jnp.zeros((8, LANES), F32)
        for i, jump in enumerate((own, hown, own_contact)):
            block = pltpu.roll(jump[:, at], (i * JR) % LANES, 1) if i else jump[:, at]
            parcel = jnp.where(place == (slot + i) % (LANES // JR), block, parcel)
        out_ref[partners_ref[0, r]] = parcel
    for copy in copies:
        copy.wait()


def first_gradient(partners_ref, where_ref, low_hbm, high_ref, x_ref, h_ref, own_ref, hown_ref, in_ref,
                   below_in, above_in, valid_ref, onehot_ref,
                   g_ref, gown_ref, far_ref, gfar_ref, below_ref, gbelow_ref, above_ref, gabove_ref,
                   all_ref, masks_ref, low_ref, sems):
    copies = low_copies(low_hbm, low_ref, sems)
    for copy in copies:
        copy.start()
    width = x_ref.shape[1]
    place = lax.broadcasted_iota(jnp.int32, (8, LANES), 1) // JR
    parts = [[jnp.zeros((8, LANES), F32)] * 2 for _ in range(3)]
    for r in range(ROUNDS):
        group, slot = divmod(r, HALF)
        parcel = in_ref[partners_ref[0, r]]
        for i in range(3):
            block = pltpu.roll(parcel, LANES - i * JR, 1) if i else parcel
            parts[i][group] = jnp.where(place == slot, block, parts[i][group])
    far, hfar, far_contact = (jnp.concatenate(part, axis=1) for part in parts)
    valid = valid_ref[...]
    own = own_ref[:8]
    far_ref[...] = jnp.concatenate([far, far_contact], axis=0)
    gown = hown_ref[...] - valid * far
    gfar = hfar - valid * own
    gown_ref[...] = gown
    gfar_ref[...] = gfar
    below, above = below_in[...], above_in[...]
    below_ref[...] = jnp.concatenate([below[:8], below[16:]], axis=0)
    above_ref[...] = jnp.concatenate([above[:8], above[16:]], axis=0)
    layer, layers, core = where_ref[0, 0], where_ref[0, 1], lax.rem(where_ref[0, 2], 2)
    member = lax.broadcasted_iota(jnp.int32, (masks_ref.shape[1], LANES), 0)
    masks_ref[0] = jnp.where(member == 2 * (layer + 1) + core, 1.0, 0.0)
    masks_ref[1] = jnp.where(member == 2 * layer + 1 - core, 1.0, 0.0)
    masks_ref[2] = jnp.where(member >= 0, core, 0).astype(F32)
    gbelow = jnp.where(layer > 0, below[8:16] - x_ref[:, :FACE], 0.0)
    gabove = jnp.where(layer < layers - 1, above[8:16] - x_ref[:, width - FACE :], 0.0)
    gbelow_ref[...] = gbelow
    gabove_ref[...] = gabove
    h = h_ref[...] - spread(valid * far, onehot_ref[...])
    first = h[:, :FACE] - below[:8]
    last = h[:, width - FACE :] - above[:8]
    g = jnp.concatenate([first, h[:, FACE : width - FACE], last], axis=1)
    g_ref[...] = g
    jumps = valid * gown * (gown - gfar)
    terms = first * (first - gbelow) + last * (last - gabove) + jumps[:, :LANES] + jumps[:, LANES:]
    square = lane_sum(g * g)
    image = dense(g, high_ref, low_ref, copies=copies)
    curvature = lane_sum(terms) + lane_sum(g * image)
    lane = lax.broadcasted_iota(jnp.int32, (8, LANES), 1)
    row = lax.broadcasted_iota(jnp.int32, (8, LANES), 0)
    line = jnp.where(lane == row, square, 0.0) + jnp.where(lane == row + 8, curvature, 0.0)
    line = jnp.sum(line, axis=0, keepdims=True)
    short = lax.broadcasted_iota(jnp.int32, (1, LANES), 1)
    for r in range(ROUNDS):
        name = jnp.full((1, LANES), partners_ref[0, r], jnp.int32).astype(F32)
        line = jnp.where(short == NAMES + r, name, line)
    all_ref[...] = jnp.broadcast_to(line, all_ref.shape)


def local_sums(g, high_ref, low_ref):
    width = g.shape[1]
    first, last = g[:, :FACE], g[:, width - FACE :]
    square = lane_sum(g * g)
    curvature = lane_sum(g * dense(g, high_ref, low_ref)) + lane_sum(first * first + last * last)
    lane = lax.broadcasted_iota(jnp.int32, (8, LANES), 1)
    return jnp.where(lane == SQUARE, square, jnp.where(lane == CURVATURE, curvature, 0.0))


def announce(sums_ref, g_ref, gown_ref, valid_ref, below_ref, out_ref):
    own = valid_ref[...] * gown_ref[...]
    squares = own * own
    pairs = g_ref[:, :FACE] * below_ref[...]
    terms = squares[:, :LANES] + squares[:, LANES:] - 2.0 * pairs
    more = jnp.sum(terms, axis=1, keepdims=True)
    lane = lax.broadcasted_iota(jnp.int32, (8, LANES), 1)
    extra = sums_ref[...] + jnp.where(lane == CURVATURE, more, 0.0)
    halves = own[:, :LANES] + extra, own[:, LANES:] + extra
    for plan in range(out_ref.shape[0]):
        out_ref[plan] = halves[plan % 2]


def layer_sums(where_ref, table_ref, in_ref, g_ref, out_ref, *gfar_refs):
    plan = where_ref[0, 2]
    for gfar_ref in gfar_refs:
        gfar_ref[...] = half_of(in_ref, table_ref, plan)
    products = sums = jnp.zeros((8, LANES), F32)
    for p in range(in_ref.shape[0]):
        near = in_ref[p]
        sums = sums + near
        products = products + near * half_of(in_ref, table_ref, p)
    cross = lane_sum(products)
    lane = lax.broadcasted_iota(jnp.int32, (8, LANES), 1)
    sums = 0.5 * sums - jnp.where(lane == CURVATURE, cross, 0.0)
    if gfar_refs:
        sibling = half_of(in_ref, table_ref, plan + 1 - 2 * lax.rem(plan, 2))
        sums = jnp.concatenate([jnp.where(lane < SQUARE, sibling, sums), g_ref[:, :FACE]], axis=1)
    out_ref[...] = jnp.broadcast_to(sums[None], out_ref.shape)


def step_of(in_ref):
    total = in_ref[0, :, :LANES]
    for member in range(1, in_ref.shape[0]):
        total = total + in_ref[member, :, :LANES]
    square = total[:, SQUARE : SQUARE + 1]
    curvature = total[:, CURVATURE : CURVATURE + 1]
    return (square + 1e-6) / (curvature + 1e-6)


def moved(x, g, step, contact):
    out = x - step * g
    return jnp.where(contact == 1, jnp.maximum(out, 0.0), out)


def first_step(in_ref):
    line = jnp.sum(in_ref[...], axis=0, keepdims=True)
    line = jnp.broadcast_to(line, (8, LANES))
    lane = lax.broadcasted_iota(jnp.int32, (8, LANES), 1)
    row = lax.broadcasted_iota(jnp.int32, (8, LANES), 0)
    square = lane_sum(jnp.where(lane == row, line, 0.0))
    curvature = lane_sum(jnp.where(lane == row + 8, line, 0.0))
    return (square + 1e-6) / (curvature + 1e-6)


def chosen(in_ref, mask, columns):
    total = jnp.zeros((8, LANES), F32)
    for member in range(in_ref.shape[0]):
        total = jnp.where(mask[member : member + 1] == 1.0, in_ref[member, :, columns], total)
    return total


def first_face(in_ref, gabove_ref, *refs):
    face_by(first_step(in_ref), gabove_ref[...], *refs)


def next_face(in_ref, masks_ref, *refs):
    face_by(step_of(in_ref), chosen(in_ref, masks_ref[0], slice(LANES, None)), *refs)


def face_by(step, gabove, x_ref, g_ref, contact_ref, load_ref, above_ref, high_ref, low_ref,
            x_out, last_out, step_out, *above_outs):
    x = moved(x_ref[...], g_ref[...], step, contact_ref[...])
    x_out[...] = x
    step_out[...] = jnp.broadcast_to(step, step_out.shape)
    above = moved(above_ref[:8], gabove, step, above_ref[8:])
    for above_out in above_outs:
        above_out[...] = jnp.concatenate([above, above_ref[8:]], axis=0)
    at = slice(x.shape[1] - FACE, x.shape[1])
    last_out[...] = dense(x, high_ref, low_ref, at) - load_ref[:, at] + (x[:, at] - above)


def first_rest(in_ref, masks_ref, gfar_ref, *refs):
    *refs, table_ref = refs
    plans = table_ref.shape[0]
    lines = in_ref[pl.ds(0, plans, stride=in_ref.shape[0] // plans), :]
    names = jnp.where(
        masks_ref[2, :1] == 0.0,
        pltpu.roll(lines, LANES - NAMES, 1),
        pltpu.roll(lines, LANES - NAMES - HALF, 1),
    )
    table_ref[...] = names[:, :8].astype(jnp.int32)
    rest_by(gfar_ref[...], *refs)


def next_rest(in_ref, masks_ref, half_ref, *refs):
    lane = lax.broadcasted_iota(jnp.int32, (8, LANES), 1)
    other = chosen(in_ref, masks_ref[1], slice(LANES))
    half, other = half_ref[...], jnp.where(lane < SQUARE, other, 0.0)
    even = masks_ref[2, :1] == 0.0
    rest_by(
        jnp.concatenate([jnp.where(even, half, other), jnp.where(even, other, half)], axis=1), *refs
    )


def rest_by(gfar, step_ref, x_ref, last_ref, load_ref, own_ref, gown_ref, far_ref,
            below_ref, gbelow_ref, valid_ref, onehot_ref, high_ref, low_ref,
            g_out, gown_out, sums_out, *halo_outs):
    step, x = step_ref[:, :1], x_ref[...]
    inner = x.shape[1] - FACE
    halo = []
    for held_ref, slope in ((own_ref, gown_ref[...]), (far_ref, gfar), (below_ref, gbelow_ref[...])):
        halo.append(moved(held_ref[:8], slope, step, held_ref[8:]))
    for held_ref, value, held_out in zip((own_ref, far_ref, below_ref), halo, halo_outs):
        held_out[...] = jnp.concatenate([value, held_ref[8:]], axis=0)
    own, far, below = halo
    onehot = onehot_ref[...]
    jumps = spread(valid_ref[...] * (own - far), onehot)
    total = dense(x, high_ref, low_ref, slice(inner)) + jumps[:, :inner] - load_ref[:, :inner]
    head = total[:, :FACE] + (x[:, :FACE] - below)
    g = jnp.concatenate([head, total[:, FACE:], last_ref[...]], axis=1)
    g_out[...] = g
    gown_out[...] = pick(g, onehot)[0]
    sums_out[...] = local_sums(g, high_ref, low_ref)


def finish(in_ref, x_ref, g_ref, contact_ref, x_out, g_out):
    g = g_ref[...]
    g_out[...] = g
    x_out[...] = moved(x_ref[...], g, step_of(in_ref), contact_ref[...])


def swap(outgoing, axis, groups=None):
    return lax.all_to_all(
        outgoing, axis, split_axis=0, concat_axis=0, tiled=True, axis_index_groups=groups
    )


def lift(face, step):
    layers = lax.axis_size("layer")
    return lax.ppermute(
        face, "layer", [(i, i + step) for i in range(layers) if 0 <= i + step < layers]
    )


def shards(dual_block, start, load, partners, jump_rows, counts, contact):
    block, x, target = dual_block[0, 0], start[0, 0], load[0, 0]
    rows, amounts, flags = jump_rows.reshape(ROUNDS, 1, JR), counts[0], contact[0]
    loads, width = x.shape
    plans, layers = lax.axis_size("plan"), lax.axis_size("layer")
    field, jump, face = shape(loads, width), shape(loads, JW), shape(loads, FACE)
    jump2, face2, face3 = shape(2 * loads, JW), shape(2 * loads, FACE), shape(3 * loads, FACE)
    flops = 4 * 16 * width * width
    position = jnp.stack([lax.axis_index("layer"), layers, lax.axis_index("plan")])
    position = position.astype(jnp.int32).reshape(1, 3)
    amounts, position = lax.optimization_barrier((amounts, position))
    columns = [
        [(chip + core) * layers + layer for layer in range(layers) for core in range(2)]
        for chip in range(0, plans, 2)
    ]
    half_shape = shape(width, width, dtype=BF16)
    held = pltpu.VMEM((width, width), F32)

    low_sems = pltpu.SemaphoreType.DMA((LOW_CHUNKS,))
    hbm = lambda *arrays: tuple(pltpu.with_memory_space_constraint(a, pltpu.HBM) for a in arrays)

    onehot, valid, own, h, first, last, high, low = call(
        prepare, "prepare",
        (shape(width, JW, dtype=BF16), jump, jump2, field, face3, face3, half_shape, half_shape),
        [HBM] * 6, 16, flops, 4 * width * width,
        [
            held, pltpu.VMEM(x.shape, F32), pltpu.VMEM(target.shape, F32),
            pltpu.VMEM(flags.shape, jnp.int32), pltpu.VMEM(rows.shape, jnp.int32),
            pltpu.SMEM(amounts.shape, jnp.int32), pltpu.SemaphoreType.DMA((CHUNKS,)),
            pltpu.SemaphoreType.DMA((5,)),
        ],
    )(*hbm(block, x, target, flags, rows, amounts))
    below, above = lift(last, 1), lift(first, -1)
    below, h_then = lax.optimization_barrier((below, h))
    hown, out, low = call(
        address, "address",
        (jump, shape(plans, loads, LANES), pltpu.HBM(half_shape.shape, BF16)),
        [HBM] + [VMEM] * 4, 8, 2**28, 4 * width * width,
        [pltpu.SMEM(partners.shape, jnp.int32), pltpu.SemaphoreType.DMA, low_sems],
    )(*hbm(partners), own, h_then, onehot, low)
    incoming = swap(out, "plan")
    g, gown, far, gfar, below, gbelow, above, gabove, out, masks, low = call(
        first_gradient, "first_gradient",
        (field, jump, jump2, jump, face2, face, face2, face,
         shape(plans * layers, LANES), shape(3, 2 * layers, LANES), half_shape),
        [SMEM] * 2 + [HBM] + [VMEM] * 10, 12, flops, 4 * width * width, [low_sems],
    )(partners, position, *hbm(low), high, x, h, own, hown, incoming, below, above, valid, onehot)
    incoming = swap(out, ("plan", "layer"))

    early = (field, face, face, face2)
    x, last, step, above = call(
        first_face, "first_face", early, [VMEM] * 9, 12, flops // 8, width * width // 2,
    )(incoming, gabove, x, g, flags, target, above, high, low)
    late = (field, jump, face, jump2, jump2, face2)
    below_next = lift(last, 1)
    g, gown, sums, own, far, below, table = call(
        first_rest, "first_rest", late + (shape(plans, 8, dtype=jnp.int32),),
        [VMEM] * 16, 12, 2 * flops, 8 * width * width,
    )(incoming, masks, gfar, step, x, last, target, own, gown, far, below, gbelow, valid, onehot, high, low)

    for iteration in range(1, ITERS):
        gbelow = below_next
        out = call(announce, "announce", shape(plans, loads, LANES), [VMEM] * 5, 8)(
            sums, g, gown, valid, gbelow
        )
        ending = iteration == ITERS - 1
        parcel = shape(2 * layers, loads, LANES if ending else LANES + FACE)
        out, *half = call(
            layer_sums, "layer_sums", (parcel,) + (() if ending else (shape(loads, LANES),)),
            [SMEM] * 2 + [VMEM] * 2, 8,
        )(position, table, swap(out, "plan"), g)
        incoming = swap(out, ("plan", "layer"), columns)
        if ending:
            x, g = call(finish, "finish", (field, field), [VMEM] * 4, 8)(incoming, x, g, flags)
            break
        x, last, step, *above = call(
            next_face, "next_face", early[:3] if iteration == ITERS - 2 else early, [VMEM] * 9, 12, flops // 8, width * width // 2,
        )(incoming, masks, x, g, flags, target, above, high, low)
        below_next = lift(last, 1)
        g, gown, sums, *halo = call(
            next_rest, "next_rest", late[:3] if iteration == ITERS - 2 else late,
            [VMEM] * 16, 12, 2 * flops, 8 * width * width,
        )(incoming, masks, *half, step, x, last, target, own, gown, far, below, gbelow,
          valid, onehot, high, low)
        (above,), (own, far, below) = above or (None,), halo or (None,) * 3
    return x[None, None], g[None, None]


def solution(mesh):
    in_specs = (
        P("layer", "plan", None, None),
        P("layer", "plan", None, None),
        P("layer", "plan", None, None),
        P("plan", None),
        P("layer", "plan", None, None),
        P("layer", "plan", None),
        P("layer", "plan", None),
    )
    out_specs = (P("layer", "plan", None, None), P("layer", "plan", None, None))
    return jax.shard_map(shards, mesh=mesh, in_specs=in_specs, out_specs=out_specs, check_vma=False)
```

```python
import functools

import jax
import jax.numpy as jnp
from jax import lax
from jax.experimental import pallas as pl
from jax.experimental.pallas import tpu as pltpu
from jax.sharding import PartitionSpec as P

FACE = 128
JR = 32
ROUNDS = 6
ITERS = 4
LANES = 128
HALF = 3
JW = 2 * LANES
STRIP = 32
CHUNKS = 4
NAMES = 16
SQUARE, CURVATURE = HALF * JR, HALF * JR + 1
F32 = jnp.float32
BF16 = jnp.bfloat16

VMEM = pl.BlockSpec(memory_space=pltpu.VMEM)
SMEM = pl.BlockSpec(memory_space=pltpu.SMEM)
HBM = pl.BlockSpec(memory_space=pltpu.HBM)


def shape(*dims, dtype=F32):
    return jax.ShapeDtypeStruct(dims, dtype)


def call(body, name, outs, specs, limit, flops=0, traffic=0, scratch=()):
    return pl.pallas_call(
        body,
        name=name,
        out_shape=outs,
        in_specs=specs,
        scratch_shapes=scratch,
        out_specs=jax.tree.map(lambda out: VMEM if isinstance(out, jax.ShapeDtypeStruct) else HBM, outs),
        compiler_params=pltpu.CompilerParams(vmem_limit_bytes=limit * 2**20),
        cost_estimate=pl.CostEstimate(flops=flops, bytes_accessed=traffic, transcendentals=0),
    )


def pieces(value, count):
    parts = []
    for _ in range(count):
        part = value.astype(BF16).astype(F32)
        parts.append(part)
        value = value - part
    return parts


def lane_sum(value):
    return jnp.sum(value, axis=1, keepdims=True)


def dense(field, high_ref, low_ref, columns=slice(None), copies=()):
    lhs = jnp.concatenate(pieces(field, 2), axis=0).astype(BF16)
    depth = field.shape[1] // CHUNKS
    total = 0.0
    for half_ref, arrivals in ((high_ref, ()), (low_ref, copies)):
        for chunk in range(CHUNKS):
            for copy in arrivals[chunk : chunk + 1]:
                copy.wait()
            at = slice(chunk * depth, (chunk + 1) * depth)
            total = total + jnp.dot(lhs[:, at], half_ref[at, columns], preferred_element_type=F32)
    return total[:8] + total[8:]


def pick(field, onehot, *extra):
    lhs = jnp.concatenate(pieces(field, 3) + list(extra), axis=0).astype(BF16)
    out = jnp.dot(lhs, onehot, preferred_element_type=F32)
    return [out[:8] + out[8:16] + out[16:24]] + [
        out[24 + 8 * i : 32 + 8 * i] for i in range(len(extra))
    ]


def spread(jumps, onehot):
    lhs = jnp.concatenate(pieces(jumps, 3), axis=0).astype(BF16)
    out = lax.dot_general(lhs, onehot, (((1,), (1,)), ((), ())), preferred_element_type=F32)
    return out[:8] + out[8:16] + out[16:24]


def half_of(in_ref, table_ref, plan):
    place = lax.broadcasted_iota(jnp.int32, (8, LANES), 1) // JR
    total = jnp.zeros((8, LANES), F32)
    for r in range(HALF):
        total = jnp.where(place == r, in_ref[table_ref[plan, r]], total)
    return total


def stream_dense(field, block_ref, rows_ref, sems, high_ref, low_ref, give):
    lhs = jnp.concatenate(pieces(field, 2), axis=0).astype(BF16)
    depth = rows_ref.shape[0] // CHUNKS
    total = jnp.zeros((lhs.shape[0], rows_ref.shape[1]), F32)
    for chunk in range(CHUNKS):
        at = slice(chunk * depth, (chunk + 1) * depth)
        chunk_copy(block_ref, rows_ref, sems, chunk).wait()
        for first in range(at.start, at.stop, STRIP):
            strip = slice(first, first + STRIP)
            rows = rows_ref[strip, :]
            high = rows.astype(BF16)
            high_ref[strip, :] = high
            low_ref[strip, :] = (rows - high.astype(F32)).astype(BF16)
        give(chunk).start()
        total = total + jnp.dot(lhs[:, at], high_ref[at, :], preferred_element_type=F32)
        total = total + jnp.dot(lhs[:, at], low_ref[at, :], preferred_element_type=F32)
    return total[:8] + total[8:]


def chunk_copy(source_ref, target_ref, sems, chunk):
    depth = source_ref.shape[0] // CHUNKS
    at = pl.ds(chunk * depth, depth)
    return pltpu.make_async_copy(source_ref.at[at, :], target_ref.at[at, :], sems.at[chunk])


def prepare(block_ref, x_hbm, load_hbm, contact_hbm, rows_hbm, partners_hbm, counts_hbm,
            onehot_ref, valid_ref, own_ref, hown_ref, h_ref, out_ref, first_ref, last_ref, high_ref,
            low_hbm, held_ref, low_ref, x_ref, load_ref, contact_ref, rows_ref, partners_ref, counts_ref,
            sems, low_sems, more_sems):
    small = [
        pltpu.make_async_copy(source, target, more_sems.at[i])
        for i, (source, target) in enumerate((
            (rows_hbm, rows_ref), (counts_hbm, counts_ref), (x_hbm, x_ref),
            (contact_hbm, contact_ref), (partners_hbm, partners_ref), (load_hbm, load_ref),
        ))
    ]
    for copy in small:
        copy.start()
    for chunk in range(CHUNKS):
        chunk_copy(block_ref, held_ref, sems, chunk).start()
    for copy in small:
        copy.wait()
    x = x_ref[...]
    width = x.shape[1]
    spare = [jnp.full((1, LANES - HALF * JR), -1, jnp.int32)]
    rows = [rows_ref[r] for r in range(ROUNDS)]
    rows = jnp.concatenate(rows[:HALF] + spare + rows[HALF:] + spare, axis=1)
    hit = lax.broadcasted_iota(jnp.int32, (width, JW), 0) == rows
    onehot_ref[...] = jnp.where(hit, 1.0, 0.0).astype(BF16)
    lane = lax.broadcasted_iota(jnp.int32, (8, JW), 1)
    valid = jnp.zeros((8, JW), F32)
    for r in range(ROUNDS):
        start = r // HALF * LANES + r % HALF * JR
        inside = (lane >= start) & (lane < start + counts_ref[0, r])
        valid = jnp.where(inside, 1.0, valid)
    valid_ref[...] = valid
    contact = jnp.broadcast_to(jnp.where(contact_ref[...] == 1, 1.0, 0.0), x.shape)
    own, own_contact = pick(x, onehot_ref[...], contact)
    own_ref[...] = jnp.concatenate([own, own_contact], axis=0)
    position = lax.broadcasted_iota(jnp.int32, x.shape, 1)
    edge = (position < FACE) | (position >= width - FACE)
    h = spread(valid * own, onehot_ref[...]) + jnp.where(edge, x, 0.0) - load_ref[...]
    low_copy = functools.partial(chunk_copy, low_ref, low_hbm, low_sems)
    h = h + stream_dense(x, block_ref, held_ref, sems, high_ref, low_ref, low_copy)
    h_ref[...] = h
    (hown,) = pick(h, onehot_ref[...])
    hown_ref[...] = hown
    out_ref[...] = jnp.zeros_like(out_ref)
    place = lax.broadcasted_iota(jnp.int32, (8, LANES), 1) // JR
    for r in range(ROUNDS):
        group, slot = divmod(r, HALF)
        at = slice(group * LANES, (group + 1) * LANES)
        parcel = jnp.zeros((8, LANES), F32)
        for i, jump in enumerate((own, hown, own_contact)):
            block = pltpu.roll(jump[:, at], (i * JR) % LANES, 1) if i else jump[:, at]
            parcel = jnp.where(place == (slot + i) % (LANES // JR), block, parcel)
        out_ref[partners_ref[0, r]] = parcel
    both = jnp.concatenate([x, h, contact], axis=0)
    first_ref[...] = both[:, :FACE]
    last_ref[...] = both[:, width - FACE :]
    for chunk in range(CHUNKS):
        low_copy(chunk).wait()


def first_gradient(partners_ref, where_ref, low_hbm, high_ref, x_ref, h_ref, own_ref, hown_ref, in_ref,
                   below_in, above_in, valid_ref, onehot_ref,
                   g_ref, gown_ref, far_ref, gfar_ref, below_ref, gbelow_ref, above_ref, gabove_ref,
                   all_ref, masks_ref, low_ref, sems):
    copies = [chunk_copy(low_hbm, low_ref, sems, chunk) for chunk in range(CHUNKS)]
    for copy in copies:
        copy.start()
    width = x_ref.shape[1]
    place = lax.broadcasted_iota(jnp.int32, (8, LANES), 1) // JR
    parts = [[jnp.zeros((8, LANES), F32)] * 2 for _ in range(3)]
    for r in range(ROUNDS):
        group, slot = divmod(r, HALF)
        parcel = in_ref[partners_ref[0, r]]
        for i in range(3):
            block = pltpu.roll(parcel, LANES - i * JR, 1) if i else parcel
            parts[i][group] = jnp.where(place == slot, block, parts[i][group])
    far, hfar, far_contact = (jnp.concatenate(part, axis=1) for part in parts)
    valid = valid_ref[...]
    own = own_ref[:8]
    far_ref[...] = jnp.concatenate([far, far_contact], axis=0)
    gown = hown_ref[...] - valid * far
    gfar = hfar - valid * own
    gown_ref[...] = gown
    gfar_ref[...] = gfar
    below, above = below_in[...], above_in[...]
    below_ref[...] = jnp.concatenate([below[:8], below[16:]], axis=0)
    above_ref[...] = jnp.concatenate([above[:8], above[16:]], axis=0)
    layer, layers, core = where_ref[0, 0], where_ref[0, 1], lax.rem(where_ref[0, 2], 2)
    member = lax.broadcasted_iota(jnp.int32, (masks_ref.shape[1], LANES), 0)
    masks_ref[0] = jnp.where(member == 2 * (layer + 1) + core, 1.0, 0.0)
    masks_ref[1] = jnp.where(member == 2 * layer + 1 - core, 1.0, 0.0)
    masks_ref[2] = jnp.where(member >= 0, core, 0).astype(F32)
    gbelow = jnp.where(layer > 0, below[8:16] - x_ref[:, :FACE], 0.0)
    gabove = jnp.where(layer < layers - 1, above[8:16] - x_ref[:, width - FACE :], 0.0)
    gbelow_ref[...] = gbelow
    gabove_ref[...] = gabove
    h = h_ref[...] - spread(valid * far, onehot_ref[...])
    first = h[:, :FACE] - below[:8]
    last = h[:, width - FACE :] - above[:8]
    g = jnp.concatenate([first, h[:, FACE : width - FACE], last], axis=1)
    g_ref[...] = g
    jumps = valid * gown * (gown - gfar)
    terms = first * (first - gbelow) + last * (last - gabove) + jumps[:, :LANES] + jumps[:, LANES:]
    square = lane_sum(g * g)
    image = dense(g, high_ref, low_ref, copies=copies)
    curvature = lane_sum(terms) + lane_sum(g * image)
    lane = lax.broadcasted_iota(jnp.int32, (8, LANES), 1)
    row = lax.broadcasted_iota(jnp.int32, (8, LANES), 0)
    line = jnp.where(lane == row, square, 0.0) + jnp.where(lane == row + 8, curvature, 0.0)
    line = jnp.sum(line, axis=0, keepdims=True)
    short = lax.broadcasted_iota(jnp.int32, (1, LANES), 1)
    for r in range(ROUNDS):
        name = jnp.full((1, LANES), partners_ref[0, r], jnp.int32).astype(F32)
        line = jnp.where(short == NAMES + r, name, line)
    all_ref[...] = jnp.broadcast_to(line, all_ref.shape)


def local_sums(g, high_ref, low_ref):
    width = g.shape[1]
    first, last = g[:, :FACE], g[:, width - FACE :]
    square = lane_sum(g * g)
    curvature = lane_sum(g * dense(g, high_ref, low_ref)) + lane_sum(first * first + last * last)
    lane = lax.broadcasted_iota(jnp.int32, (8, LANES), 1)
    return jnp.where(lane == SQUARE, square, jnp.where(lane == CURVATURE, curvature, 0.0))


def announce(sums_ref, g_ref, gown_ref, valid_ref, below_ref, out_ref):
    own = valid_ref[...] * gown_ref[...]
    squares = own * own
    pairs = g_ref[:, :FACE] * below_ref[...]
    terms = squares[:, :LANES] + squares[:, LANES:] - 2.0 * pairs
    more = jnp.sum(terms, axis=1, keepdims=True)
    lane = lax.broadcasted_iota(jnp.int32, (8, LANES), 1)
    extra = sums_ref[...] + jnp.where(lane == CURVATURE, more, 0.0)
    halves = own[:, :LANES] + extra, own[:, LANES:] + extra
    for plan in range(out_ref.shape[0]):
        out_ref[plan] = halves[plan % 2]


def layer_sums(where_ref, table_ref, in_ref, g_ref, out_ref, *gfar_refs):
    plan = where_ref[0, 2]
    for gfar_ref in gfar_refs:
        gfar_ref[...] = half_of(in_ref, table_ref, plan)
    products = sums = jnp.zeros((8, LANES), F32)
    for p in range(in_ref.shape[0]):
        near = in_ref[p]
        sums = sums + near
        products = products + near * half_of(in_ref, table_ref, p)
    cross = lane_sum(products)
    lane = lax.broadcasted_iota(jnp.int32, (8, LANES), 1)
    sums = 0.5 * sums - jnp.where(lane == CURVATURE, cross, 0.0)
    if gfar_refs:
        sibling = half_of(in_ref, table_ref, plan + 1 - 2 * lax.rem(plan, 2))
        sums = jnp.concatenate([jnp.where(lane < SQUARE, sibling, sums), g_ref[:, :FACE]], axis=1)
    out_ref[...] = jnp.broadcast_to(sums[None], out_ref.shape)


def step_of(in_ref):
    total = in_ref[0, :, :LANES]
    for member in range(1, in_ref.shape[0]):
        total = total + in_ref[member, :, :LANES]
    square = total[:, SQUARE : SQUARE + 1]
    curvature = total[:, CURVATURE : CURVATURE + 1]
    return (square + 1e-6) / (curvature + 1e-6)


def moved(x, g, step, contact):
    out = x - step * g
    return jnp.where(contact == 1, jnp.maximum(out, 0.0), out)


def first_step(in_ref):
    line = jnp.sum(in_ref[...], axis=0, keepdims=True)
    line = jnp.broadcast_to(line, (8, LANES))
    lane = lax.broadcasted_iota(jnp.int32, (8, LANES), 1)
    row = lax.broadcasted_iota(jnp.int32, (8, LANES), 0)
    square = lane_sum(jnp.where(lane == row, line, 0.0))
    curvature = lane_sum(jnp.where(lane == row + 8, line, 0.0))
    return (square + 1e-6) / (curvature + 1e-6)


def chosen(in_ref, mask, columns):
    total = jnp.zeros((8, LANES), F32)
    for member in range(in_ref.shape[0]):
        total = jnp.where(mask[member : member + 1] == 1.0, in_ref[member, :, columns], total)
    return total


def first_face(in_ref, gabove_ref, *refs):
    face_by(first_step(in_ref), gabove_ref[...], *refs)


def next_face(in_ref, masks_ref, *refs):
    face_by(step_of(in_ref), chosen(in_ref, masks_ref[0], slice(LANES, None)), *refs)


def face_by(step, gabove, x_ref, g_ref, contact_ref, load_ref, above_ref, high_ref, low_ref,
            x_out, last_out, step_out, *above_outs):
    x = moved(x_ref[...], g_ref[...], step, contact_ref[...])
    x_out[...] = x
    step_out[...] = jnp.broadcast_to(step, step_out.shape)
    above = moved(above_ref[:8], gabove, step, above_ref[8:])
    for above_out in above_outs:
        above_out[...] = jnp.concatenate([above, above_ref[8:]], axis=0)
    at = slice(x.shape[1] - FACE, x.shape[1])
    last_out[...] = dense(x, high_ref, low_ref, at) - load_ref[:, at] + (x[:, at] - above)


def first_rest(in_ref, masks_ref, gfar_ref, *refs):
    *refs, table_ref = refs
    plans = table_ref.shape[0]
    lines = in_ref[pl.ds(0, plans, stride=in_ref.shape[0] // plans), :]
    names = jnp.where(
        masks_ref[2, :1] == 0.0,
        pltpu.roll(lines, LANES - NAMES, 1),
        pltpu.roll(lines, LANES - NAMES - HALF, 1),
    )
    table_ref[...] = names[:, :8].astype(jnp.int32)
    rest_by(gfar_ref[...], *refs)


def next_rest(in_ref, masks_ref, half_ref, *refs):
    lane = lax.broadcasted_iota(jnp.int32, (8, LANES), 1)
    other = chosen(in_ref, masks_ref[1], slice(LANES))
    half, other = half_ref[...], jnp.where(lane < SQUARE, other, 0.0)
    even = masks_ref[2, :1] == 0.0
    rest_by(
        jnp.concatenate([jnp.where(even, half, other), jnp.where(even, other, half)], axis=1), *refs
    )


def rest_by(gfar, step_ref, x_ref, last_ref, load_ref, own_ref, gown_ref, far_ref,
            below_ref, gbelow_ref, valid_ref, onehot_ref, high_ref, low_ref,
            g_out, gown_out, sums_out, *halo_outs):
    step, x = step_ref[:, :1], x_ref[...]
    inner = x.shape[1] - FACE
    halo = []
    for held_ref, slope in ((own_ref, gown_ref[...]), (far_ref, gfar), (below_ref, gbelow_ref[...])):
        halo.append(moved(held_ref[:8], slope, step, held_ref[8:]))
    for held_ref, value, held_out in zip((own_ref, far_ref, below_ref), halo, halo_outs):
        held_out[...] = jnp.concatenate([value, held_ref[8:]], axis=0)
    own, far, below = halo
    onehot = onehot_ref[...]
    jumps = spread(valid_ref[...] * (own - far), onehot)
    total = dense(x, high_ref, low_ref, slice(inner)) + jumps[:, :inner] - load_ref[:, :inner]
    head = total[:, :FACE] + (x[:, :FACE] - below)
    g = jnp.concatenate([head, total[:, FACE:], last_ref[...]], axis=1)
    g_out[...] = g
    gown_out[...] = pick(g, onehot)[0]
    sums_out[...] = local_sums(g, high_ref, low_ref)


def finish(in_ref, x_ref, g_ref, contact_ref, x_out, g_out):
    g = g_ref[...]
    g_out[...] = g
    x_out[...] = moved(x_ref[...], g, step_of(in_ref), contact_ref[...])


def swap(outgoing, axis, groups=None):
    return lax.all_to_all(
        outgoing, axis, split_axis=0, concat_axis=0, tiled=True, axis_index_groups=groups
    )


def lift(face, step):
    layers = lax.axis_size("layer")
    return lax.ppermute(
        face, "layer", [(i, i + step) for i in range(layers) if 0 <= i + step < layers]
    )


def shards(dual_block, start, load, partners, jump_rows, counts, contact):
    block, x, target = dual_block[0, 0], start[0, 0], load[0, 0]
    rows, amounts, flags = jump_rows.reshape(ROUNDS, 1, JR), counts[0], contact[0]
    loads, width = x.shape
    plans, layers = lax.axis_size("plan"), lax.axis_size("layer")
    field, jump, face = shape(loads, width), shape(loads, JW), shape(loads, FACE)
    jump2, face2, face3 = shape(2 * loads, JW), shape(2 * loads, FACE), shape(3 * loads, FACE)
    flops = 4 * 16 * width * width
    position = jnp.stack([lax.axis_index("layer"), layers, lax.axis_index("plan")])
    position = position.astype(jnp.int32).reshape(1, 3)
    amounts, position = lax.optimization_barrier((amounts, position))
    columns = [
        [(chip + core) * layers + layer for layer in range(layers) for core in range(2)]
        for chip in range(0, plans, 2)
    ]
    half_shape = shape(width, width, dtype=BF16)
    held = pltpu.VMEM((width, width), F32)
    chunk_sems = pltpu.SemaphoreType.DMA((CHUNKS,))

    onehot, valid, own, hown, h, out, first, last, high, low = call(
        prepare, "prepare",
        (shape(width, JW, dtype=BF16), jump, jump2, jump, field, shape(plans, loads, LANES), face3, face3,
         half_shape, pltpu.HBM(half_shape.shape, BF16)),
        [HBM] * 7, 16, flops, 4 * width * width,
        [
            held, pltpu.VMEM((width, width), BF16), pltpu.VMEM(x.shape, F32), pltpu.VMEM(target.shape, F32),
            pltpu.VMEM(flags.shape, jnp.int32), pltpu.VMEM(rows.shape, jnp.int32),
            pltpu.SMEM(partners.shape, jnp.int32), pltpu.SMEM(amounts.shape, jnp.int32),
            chunk_sems, chunk_sems, pltpu.SemaphoreType.DMA((6,)),
        ],
    )(*(pltpu.with_memory_space_constraint(a, pltpu.HBM) for a in (block, x, target, flags, rows, partners, amounts)))
    incoming = swap(out, "plan")
    below, above = lift(last, 1), lift(first, -1)
    g, gown, far, gfar, below, gbelow, above, gabove, out, masks, low = call(
        first_gradient, "first_gradient",
        (field, jump, jump2, jump, face2, face, face2, face,
         shape(plans * layers, LANES), shape(3, 2 * layers, LANES), half_shape),
        [SMEM] * 2 + [HBM] + [VMEM] * 10, 12, flops, 4 * width * width, [chunk_sems],
    )(partners, position, pltpu.with_memory_space_constraint(low, pltpu.HBM), high, x, h, own, hown, incoming, below, above, valid, onehot)
    incoming = swap(out, ("plan", "layer"))

    early = (field, face, face, face2)
    x, last, step, above = call(
        first_face, "first_face", early, [VMEM] * 9, 12, flops // 8, width * width // 2,
    )(incoming, gabove, x, g, flags, target, above, high, low)
    late = (field, jump, face, jump2, jump2, face2)
    below_next = lift(last, 1)
    g, gown, sums, own, far, below, table = call(
        first_rest, "first_rest", late + (shape(plans, 8, dtype=jnp.int32),),
        [VMEM] * 16, 12, 2 * flops, 8 * width * width,
    )(incoming, masks, gfar, step, x, last, target, own, gown, far, below, gbelow, valid, onehot, high, low)

    for iteration in range(1, ITERS):
        gbelow = below_next
        out = call(announce, "announce", shape(plans, loads, LANES), [VMEM] * 5, 8)(
            sums, g, gown, valid, gbelow
        )
        ending = iteration == ITERS - 1
        parcel = shape(2 * layers, loads, LANES if ending else LANES + FACE)
        out, *half = call(
            layer_sums, "layer_sums", (parcel,) + (() if ending else (shape(loads, LANES),)),
            [SMEM] * 2 + [VMEM] * 2, 8,
        )(position, table, swap(out, "plan"), g)
        incoming = swap(out, ("plan", "layer"), columns)
        if ending:
            x, g = call(finish, "finish", (field, field), [VMEM] * 4, 8)(incoming, x, g, flags)
            break
        x, last, step, *above = call(
            next_face, "next_face", early[:3] if iteration == ITERS - 2 else early, [VMEM] * 9, 12, flops // 8, width * width // 2,
        )(incoming, masks, x, g, flags, target, above, high, low)
        below_next = lift(last, 1)
        g, gown, sums, *halo = call(
            next_rest, "next_rest", late[:3] if iteration == ITERS - 2 else late,
            [VMEM] * 16, 12, 2 * flops, 8 * width * width,
        )(incoming, masks, *half, step, x, last, target, own, gown, far, below, gbelow,
          valid, onehot, high, low)
        (above,), (own, far, below) = above or (None,), halo or (None,) * 3
    return x[None, None], g[None, None]


def solution(mesh):
    in_specs = (
        P("layer", "plan", None, None),
        P("layer", "plan", None, None),
        P("layer", "plan", None, None),
        P("plan", None),
        P("layer", "plan", None, None),
        P("layer", "plan", None),
        P("layer", "plan", None),
    )
    out_specs = (P("layer", "plan", None, None), P("layer", "plan", None, None))
    return jax.shard_map(shards, mesh=mesh, in_specs=in_specs, out_specs=out_specs, check_vma=False)
```

```python
import functools

import jax
import jax.numpy as jnp
from jax import lax
from jax.experimental import pallas as pl
from jax.experimental.pallas import tpu as pltpu
from jax.sharding import PartitionSpec as P

FACE = 128
JR = 32
ROUNDS = 6
ITERS = 4
LANES = 128
HALF = 3
JW = 2 * LANES
STRIP = 32
CHUNKS = 4
NAMES = 16
SQUARE, CURVATURE = HALF * JR, HALF * JR + 1
F32 = jnp.float32
BF16 = jnp.bfloat16

VMEM = pl.BlockSpec(memory_space=pltpu.VMEM)
SMEM = pl.BlockSpec(memory_space=pltpu.SMEM)
HBM = pl.BlockSpec(memory_space=pltpu.HBM)


def shape(*dims, dtype=F32):
    return jax.ShapeDtypeStruct(dims, dtype)


def call(body, name, outs, specs, limit, flops=0, traffic=0, scratch=()):
    return pl.pallas_call(
        body,
        name=name,
        out_shape=outs,
        in_specs=specs,
        scratch_shapes=scratch,
        out_specs=jax.tree.map(lambda out: VMEM if isinstance(out, jax.ShapeDtypeStruct) else HBM, outs),
        compiler_params=pltpu.CompilerParams(vmem_limit_bytes=limit * 2**20),
        cost_estimate=pl.CostEstimate(flops=flops, bytes_accessed=traffic, transcendentals=0),
    )


def pieces(value, count):
    parts = []
    for _ in range(count):
        part = value.astype(BF16).astype(F32)
        parts.append(part)
        value = value - part
    return parts


def lane_sum(value):
    return jnp.sum(value, axis=1, keepdims=True)


def dense(field, high_ref, low_ref, columns=slice(None), copies=()):
    lhs = jnp.concatenate(pieces(field, 2), axis=0).astype(BF16)
    depth = field.shape[1] // CHUNKS
    total = 0.0
    for half_ref, arrivals in ((high_ref, ()), (low_ref, copies)):
        for chunk in range(CHUNKS):
            for copy in arrivals[chunk : chunk + 1]:
                copy.wait()
            at = slice(chunk * depth, (chunk + 1) * depth)
            total = total + jnp.dot(lhs[:, at], half_ref[at, columns], preferred_element_type=F32)
    return total[:8] + total[8:]


def pick(field, onehot, *extra):
    lhs = jnp.concatenate(pieces(field, 3) + list(extra), axis=0).astype(BF16)
    out = jnp.dot(lhs, onehot, preferred_element_type=F32)
    return [out[:8] + out[8:16] + out[16:24]] + [
        out[24 + 8 * i : 32 + 8 * i] for i in range(len(extra))
    ]


def spread(jumps, onehot):
    lhs = jnp.concatenate(pieces(jumps, 3), axis=0).astype(BF16)
    out = lax.dot_general(lhs, onehot, (((1,), (1,)), ((), ())), preferred_element_type=F32)
    return out[:8] + out[8:16] + out[16:24]


def half_of(in_ref, table_ref, plan):
    place = lax.broadcasted_iota(jnp.int32, (8, LANES), 1) // JR
    total = jnp.zeros((8, LANES), F32)
    for r in range(HALF):
        total = jnp.where(place == r, in_ref[table_ref[plan, r]], total)
    return total


def stream_dense(field, block_ref, rows_ref, sems, high_ref, low_ref, give):
    lhs = jnp.concatenate(pieces(field, 2), axis=0).astype(BF16)
    depth = rows_ref.shape[0] // CHUNKS
    total = jnp.zeros((lhs.shape[0], rows_ref.shape[1]), F32)
    for chunk in range(CHUNKS):
        at = slice(chunk * depth, (chunk + 1) * depth)
        chunk_copy(block_ref, rows_ref, sems, chunk).wait()
        for first in range(at.start, at.stop, STRIP):
            strip = slice(first, first + STRIP)
            rows = rows_ref[strip, :]
            high = rows.astype(BF16)
            high_ref[strip, :] = high
            low_ref[strip, :] = (rows - high.astype(F32)).astype(BF16)
        give(chunk).start()
        total = total + jnp.dot(lhs[:, at], high_ref[at, :], preferred_element_type=F32)
        total = total + jnp.dot(lhs[:, at], low_ref[at, :], preferred_element_type=F32)
    return total[:8] + total[8:]


def chunk_copy(source_ref, target_ref, sems, chunk):
    depth = source_ref.shape[0] // CHUNKS
    at = pl.ds(chunk * depth, depth)
    return pltpu.make_async_copy(source_ref.at[at, :], target_ref.at[at, :], sems.at[chunk])


def prepare(block_ref, x_hbm, load_hbm, contact_hbm, rows_hbm, partners_hbm, counts_hbm,
            onehot_ref, valid_ref, own_ref, hown_ref, h_ref, out_ref, first_ref, last_ref, high_ref,
            low_hbm, held_ref, low_ref, x_ref, load_ref, contact_ref, rows_ref, partners_ref, counts_ref,
            sems, low_sems, more_sems):
    small = [
        pltpu.make_async_copy(source, target, more_sems.at[i])
        for i, (source, target) in enumerate((
            (rows_hbm, rows_ref), (counts_hbm, counts_ref), (x_hbm, x_ref),
            (contact_hbm, contact_ref), (partners_hbm, partners_ref), (load_hbm, load_ref),
        ))
    ]
    for copy in small:
        copy.start()
    for chunk in range(CHUNKS):
        chunk_copy(block_ref, held_ref, sems, chunk).start()
    for copy in small:
        copy.wait()
    x = x_ref[...]
    width = x.shape[1]
    spare = [jnp.full((1, LANES - HALF * JR), -1, jnp.int32)]
    rows = [rows_ref[r] for r in range(ROUNDS)]
    rows = jnp.concatenate(rows[:HALF] + spare + rows[HALF:] + spare, axis=1)
    hit = lax.broadcasted_iota(jnp.int32, (width, JW), 0) == rows
    onehot_ref[...] = jnp.where(hit, 1.0, 0.0).astype(BF16)
    lane = lax.broadcasted_iota(jnp.int32, (8, JW), 1)
    valid = jnp.zeros((8, JW), F32)
    for r in range(ROUNDS):
        start = r // HALF * LANES + r % HALF * JR
        inside = (lane >= start) & (lane < start + counts_ref[0, r])
        valid = jnp.where(inside, 1.0, valid)
    valid_ref[...] = valid
    contact = jnp.broadcast_to(jnp.where(contact_ref[...] == 1, 1.0, 0.0), x.shape)
    own, own_contact = pick(x, onehot_ref[...], contact)
    own_ref[...] = jnp.concatenate([own, own_contact], axis=0)
    position = lax.broadcasted_iota(jnp.int32, x.shape, 1)
    edge = (position < FACE) | (position >= width - FACE)
    h = spread(valid * own, onehot_ref[...]) + jnp.where(edge, x, 0.0) - load_ref[...]
    low_copy = functools.partial(chunk_copy, low_ref, low_hbm, low_sems)
    h = h + stream_dense(x, block_ref, held_ref, sems, high_ref, low_ref, low_copy)
    h_ref[...] = h
    (hown,) = pick(h, onehot_ref[...])
    hown_ref[...] = hown
    out_ref[...] = jnp.zeros_like(out_ref)
    place = lax.broadcasted_iota(jnp.int32, (8, LANES), 1) // JR
    for r in range(ROUNDS):
        group, slot = divmod(r, HALF)
        at = slice(group * LANES, (group + 1) * LANES)
        parcel = jnp.zeros((8, LANES), F32)
        for i, jump in enumerate((own, hown, own_contact)):
            block = pltpu.roll(jump[:, at], (i * JR) % LANES, 1) if i else jump[:, at]
            parcel = jnp.where(place == (slot + i) % (LANES // JR), block, parcel)
        out_ref[partners_ref[0, r]] = parcel
    both = jnp.concatenate([x, h, contact], axis=0)
    first_ref[...] = both[:, :FACE]
    last_ref[...] = both[:, width - FACE :]
    for chunk in range(CHUNKS):
        low_copy(chunk).wait()


def first_gradient(partners_ref, where_ref, low_hbm, high_ref, x_ref, h_ref, own_ref, hown_ref, in_ref,
                   below_in, above_in, valid_ref, onehot_ref,
                   g_ref, gown_ref, far_ref, gfar_ref, below_ref, gbelow_ref, above_ref, gabove_ref,
                   all_ref, masks_ref, low_ref, sems):
    copies = [chunk_copy(low_hbm, low_ref, sems, chunk) for chunk in range(CHUNKS)]
    for copy in copies:
        copy.start()
    width = x_ref.shape[1]
    place = lax.broadcasted_iota(jnp.int32, (8, LANES), 1) // JR
    parts = [[jnp.zeros((8, LANES), F32)] * 2 for _ in range(3)]
    for r in range(ROUNDS):
        group, slot = divmod(r, HALF)
        parcel = in_ref[partners_ref[0, r]]
        for i in range(3):
            block = pltpu.roll(parcel, LANES - i * JR, 1) if i else parcel
            parts[i][group] = jnp.where(place == slot, block, parts[i][group])
    far, hfar, far_contact = (jnp.concatenate(part, axis=1) for part in parts)
    valid = valid_ref[...]
    own = own_ref[:8]
    far_ref[...] = jnp.concatenate([far, far_contact], axis=0)
    gown = hown_ref[...] - valid * far
    gfar = hfar - valid * own
    gown_ref[...] = gown
    gfar_ref[...] = gfar
    below, above = below_in[...], above_in[...]
    below_ref[...] = jnp.concatenate([below[:8], below[16:]], axis=0)
    above_ref[...] = jnp.concatenate([above[:8], above[16:]], axis=0)
    layer, layers, core = where_ref[0, 0], where_ref[0, 1], lax.rem(where_ref[0, 2], 2)
    member = lax.broadcasted_iota(jnp.int32, (masks_ref.shape[1], LANES), 0)
    masks_ref[0] = jnp.where(member == 2 * (layer + 1) + core, 1.0, 0.0)
    masks_ref[1] = jnp.where(member == 2 * layer + 1 - core, 1.0, 0.0)
    masks_ref[2] = jnp.where(member >= 0, core, 0).astype(F32)
    gbelow = jnp.where(layer > 0, below[8:16] - x_ref[:, :FACE], 0.0)
    gabove = jnp.where(layer < layers - 1, above[8:16] - x_ref[:, width - FACE :], 0.0)
    gbelow_ref[...] = gbelow
    gabove_ref[...] = gabove
    h = h_ref[...] - spread(valid * far, onehot_ref[...])
    first = h[:, :FACE] - below[:8]
    last = h[:, width - FACE :] - above[:8]
    g = jnp.concatenate([first, h[:, FACE : width - FACE], last], axis=1)
    g_ref[...] = g
    jumps = valid * gown * (gown - gfar)
    terms = first * (first - gbelow) + last * (last - gabove) + jumps[:, :LANES] + jumps[:, LANES:]
    square = lane_sum(g * g)
    image = dense(g, high_ref, low_ref, copies=copies)
    curvature = lane_sum(terms) + lane_sum(g * image)
    lane = lax.broadcasted_iota(jnp.int32, (8, LANES), 1)
    row = lax.broadcasted_iota(jnp.int32, (8, LANES), 0)
    line = jnp.where(lane == row, square, 0.0) + jnp.where(lane == row + 8, curvature, 0.0)
    line = jnp.sum(line, axis=0, keepdims=True)
    short = lax.broadcasted_iota(jnp.int32, (1, LANES), 1)
    for r in range(ROUNDS):
        name = jnp.full((1, LANES), partners_ref[0, r], jnp.int32).astype(F32)
        line = jnp.where(short == NAMES + r, name, line)
    all_ref[...] = jnp.broadcast_to(line, all_ref.shape)


def local_sums(g, high_ref, low_ref):
    width = g.shape[1]
    first, last = g[:, :FACE], g[:, width - FACE :]
    square = lane_sum(g * g)
    curvature = lane_sum(g * dense(g, high_ref, low_ref)) + lane_sum(first * first + last * last)
    lane = lax.broadcasted_iota(jnp.int32, (8, LANES), 1)
    return jnp.where(lane == SQUARE, square, jnp.where(lane == CURVATURE, curvature, 0.0))


def add_pairs(sums_ref, g_ref, gown_ref, valid_ref, below_ref, out_ref):
    own = valid_ref[...] * gown_ref[...]
    squares = own * own
    pairs = g_ref[:, :FACE] * below_ref[...]
    terms = squares[:, :LANES] + squares[:, LANES:] - 2.0 * pairs
    lane = lax.broadcasted_iota(jnp.int32, (8, LANES), 1)
    out_ref[...] = sums_ref[...] + jnp.where(lane == CURVATURE, lane_sum(terms), 0.0)


def announce(sums_ref, keep_ref, swapped_ref, out_ref):
    parcel = jnp.concatenate([keep_ref[...] + sums_ref[...], swapped_ref[...]], axis=0)
    out_ref[...] = jnp.broadcast_to(parcel[None], out_ref.shape)


def layer_sums(where_ref, table_ref, in_ref, g_ref, out_ref, *gfar_refs):
    plan = where_ref[0, 2]
    core = lax.rem(plan, 2)
    for gfar_ref in gfar_refs:
        gfar_ref[...] = half_of(in_ref, table_ref, plan)
    products = sums = jnp.zeros((8, LANES), F32)
    for p in range(in_ref.shape[0]):
        near = in_ref[p + core if p % 2 == 0 else p - core]
        sums = sums + near
        products = products + near * half_of(in_ref, table_ref, p)
    lane = lax.broadcasted_iota(jnp.int32, (8, LANES), 1)
    sums = sums - jnp.where(lane == CURVATURE, lane_sum(products), 0.0)
    if gfar_refs:
        sibling = half_of(in_ref, table_ref, plan + 1 - 2 * core)
        sums = jnp.concatenate([jnp.where(lane < SQUARE, sibling, sums), g_ref[:, :FACE]], axis=1)
    out_ref[...] = jnp.broadcast_to(sums[None], out_ref.shape)


def step_of(in_ref):
    total = in_ref[0, :, :LANES]
    for member in range(1, in_ref.shape[0]):
        total = total + in_ref[member, :, :LANES]
    square = total[:, SQUARE : SQUARE + 1]
    curvature = total[:, CURVATURE : CURVATURE + 1]
    return (square + 1e-6) / (curvature + 1e-6)


def moved(x, g, step, contact):
    out = x - step * g
    return jnp.where(contact == 1, jnp.maximum(out, 0.0), out)


def first_step(in_ref):
    line = jnp.sum(in_ref[...], axis=0, keepdims=True)
    line = jnp.broadcast_to(line, (8, LANES))
    lane = lax.broadcasted_iota(jnp.int32, (8, LANES), 1)
    row = lax.broadcasted_iota(jnp.int32, (8, LANES), 0)
    square = lane_sum(jnp.where(lane == row, line, 0.0))
    curvature = lane_sum(jnp.where(lane == row + 8, line, 0.0))
    return (square + 1e-6) / (curvature + 1e-6)


def chosen(in_ref, mask, columns):
    total = jnp.zeros((8, LANES), F32)
    for member in range(in_ref.shape[0]):
        total = jnp.where(mask[member : member + 1] == 1.0, in_ref[member, :, columns], total)
    return total


def first_face(in_ref, gabove_ref, *refs):
    face_by(first_step(in_ref), gabove_ref[...], *refs)


def next_face(in_ref, masks_ref, *refs):
    face_by(step_of(in_ref), chosen(in_ref, masks_ref[0], slice(LANES, None)), *refs)


def face_by(step, gabove, x_ref, g_ref, contact_ref, load_ref, above_ref, high_ref, low_ref,
            x_out, last_out, step_out, *above_outs):
    x = moved(x_ref[...], g_ref[...], step, contact_ref[...])
    x_out[...] = x
    step_out[...] = jnp.broadcast_to(step, step_out.shape)
    above = moved(above_ref[:8], gabove, step, above_ref[8:])
    for above_out in above_outs:
        above_out[...] = jnp.concatenate([above, above_ref[8:]], axis=0)
    at = slice(x.shape[1] - FACE, x.shape[1])
    last_out[...] = dense(x, high_ref, low_ref, at) - load_ref[:, at] + (x[:, at] - above)


def first_rest(in_ref, masks_ref, gfar_ref, *refs):
    *refs, table_ref = refs
    plans = table_ref.shape[0]
    lines = in_ref[pl.ds(0, plans, stride=in_ref.shape[0] // plans), :]
    names = jnp.where(
        masks_ref[2, :1] == 0.0,
        pltpu.roll(lines, LANES - NAMES, 1),
        pltpu.roll(lines, LANES - NAMES - HALF, 1),
    )
    names = names[:, :8].astype(jnp.int32)
    other = names + 1 - 2 * (names & 1)
    table_ref[...] = jnp.where(masks_ref[2, :1, :8] == 0.0, names, other)
    rest_by(gfar_ref[...], masks_ref, *refs)


def next_rest(in_ref, masks_ref, half_ref, *refs):
    lane = lax.broadcasted_iota(jnp.int32, (8, LANES), 1)
    other = chosen(in_ref, masks_ref[1], slice(LANES))
    half, other = half_ref[...], jnp.where(lane < SQUARE, other, 0.0)
    even = masks_ref[2, :1] == 0.0
    rest_by(
        jnp.concatenate([jnp.where(even, half, other), jnp.where(even, other, half)], axis=1),
        masks_ref, *refs,
    )


def rest_by(gfar, masks_ref, step_ref, x_ref, last_ref, load_ref, own_ref, gown_ref, far_ref,
            below_ref, gbelow_ref, valid_ref, onehot_ref, high_ref, low_ref,
            g_out, gown_out, sums_out, keep_out, give_out, *halo_outs):
    step, x = step_ref[:, :1], x_ref[...]
    inner = x.shape[1] - FACE
    halo = []
    for held_ref, slope in ((own_ref, gown_ref[...]), (far_ref, gfar), (below_ref, gbelow_ref[...])):
        halo.append(moved(held_ref[:8], slope, step, held_ref[8:]))
    for held_ref, value, held_out in zip((own_ref, far_ref, below_ref), halo, halo_outs):
        held_out[...] = jnp.concatenate([value, held_ref[8:]], axis=0)
    own, far, below = halo
    onehot = onehot_ref[...]
    jumps = spread(valid_ref[...] * (own - far), onehot)
    total = dense(x, high_ref, low_ref, slice(inner)) + jumps[:, :inner] - load_ref[:, :inner]
    head = total[:, :FACE] + (x[:, :FACE] - below)
    g = jnp.concatenate([head, total[:, FACE:], last_ref[...]], axis=1)
    g_out[...] = g
    gown = pick(g, onehot)[0]
    gown_out[...] = gown
    jumps = valid_ref[...] * gown
    even = masks_ref[2, :1] == 0.0
    keep_out[...] = jnp.where(even, jumps[:, :LANES], jumps[:, LANES:])
    give_out[...] = jnp.where(even, jumps[:, LANES:], jumps[:, :LANES])
    sums_out[...] = local_sums(g, high_ref, low_ref)


def finish(in_ref, x_ref, g_ref, contact_ref, x_out, g_out):
    g = g_ref[...]
    g_out[...] = g
    x_out[...] = moved(x_ref[...], g, step_of(in_ref), contact_ref[...])


def swap(outgoing, axis, groups=None):
    return lax.all_to_all(
        outgoing, axis, split_axis=0, concat_axis=0, tiled=True, axis_index_groups=groups
    )


def lift(face, step):
    layers = lax.axis_size("layer")
    return lax.ppermute(
        face, "layer", [(i, i + step) for i in range(layers) if 0 <= i + step < layers]
    )


def shards(dual_block, start, load, partners, jump_rows, counts, contact):
    block, x, target = dual_block[0, 0], start[0, 0], load[0, 0]
    rows, amounts, flags = jump_rows.reshape(ROUNDS, 1, JR), counts[0], contact[0]
    loads, width = x.shape
    plans, layers = lax.axis_size("plan"), lax.axis_size("layer")
    field, jump, face = shape(loads, width), shape(loads, JW), shape(loads, FACE)
    jump2, face2, face3 = shape(2 * loads, JW), shape(2 * loads, FACE), shape(3 * loads, FACE)
    flops = 4 * 16 * width * width
    position = jnp.stack([lax.axis_index("layer"), layers, lax.axis_index("plan")])
    position = position.astype(jnp.int32).reshape(1, 3)
    amounts, position = lax.optimization_barrier((amounts, position))
    cores = [list(range(core, plans, 2)) for core in range(2)]
    columns = [
        [(chip + core) * layers + layer for layer in range(layers) for core in range(2)]
        for chip in range(0, plans, 2)
    ]
    half_shape = shape(width, width, dtype=BF16)
    held = pltpu.VMEM((width, width), F32)
    chunk_sems = pltpu.SemaphoreType.DMA((CHUNKS,))

    onehot, valid, own, hown, h, out, first, last, high, low = call(
        prepare, "prepare",
        (shape(width, JW, dtype=BF16), jump, jump2, jump, field, shape(plans, loads, LANES), face3, face3,
         half_shape, pltpu.HBM(half_shape.shape, BF16)),
        [HBM] * 7, 16, flops, 4 * width * width,
        [
            held, pltpu.VMEM((width, width), BF16), pltpu.VMEM(x.shape, F32), pltpu.VMEM(target.shape, F32),
            pltpu.VMEM(flags.shape, jnp.int32), pltpu.VMEM(rows.shape, jnp.int32),
            pltpu.SMEM(partners.shape, jnp.int32), pltpu.SMEM(amounts.shape, jnp.int32),
            chunk_sems, chunk_sems, pltpu.SemaphoreType.DMA((6,)),
        ],
    )(*(pltpu.with_memory_space_constraint(a, pltpu.HBM) for a in (block, x, target, flags, rows, partners, amounts)))
    incoming = swap(out, "plan")
    below, above = lift(last, 1), lift(first, -1)
    g, gown, far, gfar, below, gbelow, above, gabove, out, masks, low = call(
        first_gradient, "first_gradient",
        (field, jump, jump2, jump, face2, face, face2, face,
         shape(plans * layers, LANES), shape(3, 2 * layers, LANES), half_shape),
        [SMEM] * 2 + [HBM] + [VMEM] * 10, 12, flops, 4 * width * width, [chunk_sems],
    )(partners, position, pltpu.with_memory_space_constraint(low, pltpu.HBM), high, x, h, own, hown, incoming, below, above, valid, onehot)
    incoming = swap(out, ("plan", "layer"))

    early = (field, face, face, face2)
    x, last, step, above = call(
        first_face, "first_face", early, [VMEM] * 9, 12, flops // 8, width * width // 2,
    )(incoming, gabove, x, g, flags, target, above, high, low)
    late = (field, jump, face, face, face, jump2, jump2, face2)
    below_next = lift(last, 1)
    g, gown, sums, keep, give, own, far, below, table = call(
        first_rest, "first_rest", late + (shape(plans, 8, dtype=jnp.int32),),
        [VMEM] * 16, 12, 2 * flops, 8 * width * width,
    )(incoming, masks, gfar, step, x, last, target, own, gown, far, below, gbelow, valid, onehot, high, low)

    for iteration in range(1, ITERS):
        gbelow = below_next
        sums = call(add_pairs, "add_pairs", face, [VMEM] * 5, 8)(sums, g, gown, valid, gbelow)
        swapped = lax.ppermute(give, "plan", [(p, p ^ 1) for p in range(plans)])
        out = call(announce, "announce", shape(plans // 2, 2 * loads, LANES), [VMEM] * 3, 8)(
            sums, keep, swapped
        )
        everyone = swap(out, "plan", cores).reshape(plans, loads, LANES)
        ending = iteration == ITERS - 1
        parcel = shape(2 * layers, loads, LANES if ending else LANES + FACE)
        out, *half = call(
            layer_sums, "layer_sums", (parcel,) + (() if ending else (shape(loads, LANES),)),
            [SMEM] * 2 + [VMEM] * 2, 8,
        )(position, table, everyone, g)
        incoming = swap(out, ("plan", "layer"), columns)
        if ending:
            x, g = call(finish, "finish", (field, field), [VMEM] * 4, 8)(incoming, x, g, flags)
            break
        x, last, step, *above = call(
            next_face, "next_face", early[:3] if iteration == ITERS - 2 else early, [VMEM] * 9, 12, flops // 8, width * width // 2,
        )(incoming, masks, x, g, flags, target, above, high, low)
        below_next = lift(last, 1)
        g, gown, sums, keep, give, *halo = call(
            next_rest, "next_rest", late[:5] if iteration == ITERS - 2 else late,
            [VMEM] * 16, 12, 2 * flops, 8 * width * width,
        )(incoming, masks, *half, step, x, last, target, own, gown, far, below, gbelow,
          valid, onehot, high, low)
        (above,), (own, far, below) = above or (None,), halo or (None,) * 3
    return x[None, None], g[None, None]


def solution(mesh):
    in_specs = (
        P("layer", "plan", None, None),
        P("layer", "plan", None, None),
        P("layer", "plan", None, None),
        P("plan", None),
        P("layer", "plan", None, None),
        P("layer", "plan", None),
        P("layer", "plan", None),
    )
    out_specs = (P("layer", "plan", None, None), P("layer", "plan", None, None))
    return jax.shard_map(shards, mesh=mesh, in_specs=in_specs, out_specs=out_specs, check_vma=False)
```

```python
import jax
import jax.numpy as jnp
from jax import lax
from jax.experimental import pallas as pl
from jax.experimental.pallas import tpu as pltpu
from jax.sharding import PartitionSpec as P

FACE = 128
JR = 32
ROUNDS = 6
ITERS = 4
LANES = 128
HALF = 3
JW = 2 * LANES
STRIP = 32
CHUNKS = 4
NAMES = 16
SQUARE, CURVATURE = HALF * JR, HALF * JR + 1
F32 = jnp.float32
BF16 = jnp.bfloat16

VMEM = pl.BlockSpec(memory_space=pltpu.VMEM)
SMEM = pl.BlockSpec(memory_space=pltpu.SMEM)
HBM = pl.BlockSpec(memory_space=pltpu.HBM)


def shape(*dims, dtype=F32):
    return jax.ShapeDtypeStruct(dims, dtype)


def call(body, name, outs, specs, limit, flops=0, traffic=0, scratch=()):
    return pl.pallas_call(
        body,
        name=name,
        out_shape=outs,
        in_specs=specs,
        scratch_shapes=scratch,
        out_specs=jax.tree.map(lambda _: VMEM, outs),
        compiler_params=pltpu.CompilerParams(vmem_limit_bytes=limit * 2**20),
        cost_estimate=pl.CostEstimate(flops=flops, bytes_accessed=traffic, transcendentals=0),
    )


def pieces(value, count):
    parts = []
    for _ in range(count):
        part = value.astype(BF16).astype(F32)
        parts.append(part)
        value = value - part
    return parts


def lane_sum(value):
    return jnp.sum(value, axis=1, keepdims=True)


def dense(field, high_ref, low_ref, columns=slice(None), arrive=None):
    lhs = jnp.concatenate(pieces(field, 2), axis=0).astype(BF16)
    depth = field.shape[1] // CHUNKS
    total = 0.0
    for half_ref in (high_ref, low_ref):
        for chunk in range(CHUNKS):
            if half_ref is low_ref and arrive is not None:
                arrive(chunk)
            at = slice(chunk * depth, (chunk + 1) * depth)
            total = total + jnp.dot(lhs[:, at], half_ref[at, columns], preferred_element_type=F32)
    return total[:8] + total[8:]


def pick(field, onehot, *extra):
    lhs = jnp.concatenate(pieces(field, 3) + list(extra), axis=0).astype(BF16)
    out = jnp.dot(lhs, onehot, preferred_element_type=F32)
    return [out[:8] + out[8:16] + out[16:24]] + [
        out[24 + 8 * i : 32 + 8 * i] for i in range(len(extra))
    ]


def spread(jumps, onehot):
    lhs = jnp.concatenate(pieces(jumps, 3), axis=0).astype(BF16)
    out = lax.dot_general(lhs, onehot, (((1,), (1,)), ((), ())), preferred_element_type=F32)
    return out[:8] + out[8:16] + out[16:24]


def half_of(in_ref, table_ref, plan):
    place = lax.broadcasted_iota(jnp.int32, (8, LANES), 1) // JR
    total = jnp.zeros((8, LANES), F32)
    for r in range(HALF):
        total = jnp.where(place == r, in_ref[table_ref[0, HALF * plan + r]], total)
    return total


def stream_dense(field, block_ref, rows_ref, sems, high_ref, low_ref):
    lhs = jnp.concatenate(pieces(field, 2), axis=0).astype(BF16)
    depth = rows_ref.shape[0] // CHUNKS
    total = jnp.zeros((lhs.shape[0], rows_ref.shape[1]), F32)
    for chunk in range(CHUNKS):
        at = slice(chunk * depth, (chunk + 1) * depth)
        chunk_copy(block_ref, rows_ref, sems, chunk).wait()
        for first in range(at.start, at.stop, STRIP):
            strip = slice(first, first + STRIP)
            rows = rows_ref[strip, :]
            high = rows.astype(BF16)
            high_ref[strip, :] = high
            low_ref[strip, :] = (rows - high.astype(F32)).astype(BF16)
        total = total + jnp.dot(lhs[:, at], high_ref[at, :], preferred_element_type=F32)
        total = total + jnp.dot(lhs[:, at], low_ref[at, :], preferred_element_type=F32)
    return total[:8] + total[8:]


def chunk_copy(source_ref, target_ref, sems, chunk):
    depth = source_ref.shape[0] // CHUNKS
    at = pl.ds(chunk * depth, depth)
    return pltpu.make_async_copy(source_ref.at[at, :], target_ref.at[at, :], sems.at[chunk])


def prepare(block_ref, x_hbm, load_hbm, contact_hbm, rows_hbm, partners_hbm, counts_hbm,
            onehot_ref, valid_ref, own_ref, hown_ref, h_ref, out_ref, first_ref, last_ref, high_ref,
            held_ref, low_ref, x_ref, load_ref, contact_ref, rows_ref, partners_ref, counts_ref,
            sems, more_sems):
    small = [
        pltpu.make_async_copy(source, target, more_sems.at[i])
        for i, (source, target) in enumerate((
            (rows_hbm, rows_ref), (counts_hbm, counts_ref), (x_hbm, x_ref),
            (contact_hbm, contact_ref), (partners_hbm, partners_ref), (load_hbm, load_ref),
        ))
    ]
    for copy in small:
        copy.start()
    for chunk in range(CHUNKS):
        chunk_copy(block_ref, held_ref, sems, chunk).start()
    for copy in small:
        copy.wait()
    x = x_ref[...]
    width = x.shape[1]
    spare = [jnp.full((1, LANES - HALF * JR), -1, jnp.int32)]
    rows = [rows_ref[r] for r in range(ROUNDS)]
    rows = jnp.concatenate(rows[:HALF] + spare + rows[HALF:] + spare, axis=1)
    hit = lax.broadcasted_iota(jnp.int32, (width, JW), 0) == rows
    onehot_ref[...] = jnp.where(hit, 1.0, 0.0).astype(BF16)
    lane = lax.broadcasted_iota(jnp.int32, (8, JW), 1)
    valid = jnp.zeros((8, JW), F32)
    for r in range(ROUNDS):
        start = r // HALF * LANES + r % HALF * JR
        inside = (lane >= start) & (lane < start + counts_ref[0, r])
        valid = jnp.where(inside, 1.0, valid)
    valid_ref[...] = valid
    contact = jnp.broadcast_to(jnp.where(contact_ref[...] == 1, 1.0, 0.0), x.shape)
    own, own_contact = pick(x, onehot_ref[...], contact)
    own_ref[...] = jnp.concatenate([own, own_contact], axis=0)
    position = lax.broadcasted_iota(jnp.int32, x.shape, 1)
    edge = (position < FACE) | (position >= width - FACE)
    h = spread(valid * own, onehot_ref[...]) + jnp.where(edge, x, 0.0) - load_ref[...]
    h = h + stream_dense(x, block_ref, held_ref, sems, high_ref, low_ref)
    h_ref[...] = h
    (hown,) = pick(h, onehot_ref[...])
    hown_ref[...] = hown
    out_ref[...] = jnp.zeros_like(out_ref)
    place = lax.broadcasted_iota(jnp.int32, (8, LANES), 1) // JR
    for r in range(ROUNDS):
        group, slot = divmod(r, HALF)
        at = slice(group * LANES, (group + 1) * LANES)
        parcel = jnp.zeros((8, LANES), F32)
        for i, jump in enumerate((own, hown, own_contact)):
            block = pltpu.roll(jump[:, at], (i * JR) % LANES, 1) if i else jump[:, at]
            parcel = jnp.where(place == (slot + i) % (LANES // JR), block, parcel)
        out_ref[partners_ref[0, r]] = parcel
    both = jnp.concatenate([x, h, contact], axis=0)
    first_ref[...] = both[:, :FACE]
    last_ref[...] = both[:, width - FACE :]


def first_gradient(partners_ref, where_ref, block_ref, high_ref, x_ref, h_ref, own_ref, hown_ref, in_ref,
                   below_in, above_in, valid_ref, onehot_ref,
                   g_ref, gown_ref, far_ref, gfar_ref, below_ref, gbelow_ref, above_ref, gabove_ref,
                   all_ref, masks_ref, low_ref, held_ref, sems):
    for chunk in range(CHUNKS):
        chunk_copy(block_ref, held_ref, sems, chunk).start()

    def arrive(chunk):
        chunk_copy(block_ref, held_ref, sems, chunk).wait()
        depth = held_ref.shape[0] // CHUNKS
        for first in range(chunk * depth, (chunk + 1) * depth, STRIP):
            strip = slice(first, first + STRIP)
            rest = held_ref[strip, :] - high_ref[strip, :].astype(F32)
            low_ref[strip, :] = rest.astype(BF16)

    width = x_ref.shape[1]
    place = lax.broadcasted_iota(jnp.int32, (8, LANES), 1) // JR
    parts = [[jnp.zeros((8, LANES), F32)] * 2 for _ in range(3)]
    for r in range(ROUNDS):
        group, slot = divmod(r, HALF)
        parcel = in_ref[partners_ref[0, r]]
        for i in range(3):
            block = pltpu.roll(parcel, LANES - i * JR, 1) if i else parcel
            parts[i][group] = jnp.where(place == slot, block, parts[i][group])
    far, hfar, far_contact = (jnp.concatenate(part, axis=1) for part in parts)
    valid = valid_ref[...]
    own = own_ref[:8]
    far_ref[...] = jnp.concatenate([far, far_contact], axis=0)
    gown = hown_ref[...] - valid * far
    gfar = hfar - valid * own
    gown_ref[...] = gown
    gfar_ref[...] = gfar
    below, above = below_in[...], above_in[...]
    below_ref[...] = jnp.concatenate([below[:8], below[16:]], axis=0)
    above_ref[...] = jnp.concatenate([above[:8], above[16:]], axis=0)
    layer, layers, core = where_ref[0, 0], where_ref[0, 1], lax.rem(where_ref[0, 2], 2)
    member = lax.broadcasted_iota(jnp.int32, (masks_ref.shape[1], LANES), 0)
    masks_ref[0] = jnp.where(member == 2 * (layer + 1) + core, 1.0, 0.0)
    masks_ref[1] = jnp.where(member == 2 * layer + 1 - core, 1.0, 0.0)
    masks_ref[2] = jnp.where(member >= 0, core, 0).astype(F32)
    masks_ref[3] = jnp.where(member >= 0, where_ref[0, 2], 0).astype(F32)
    gbelow = jnp.where(layer > 0, below[8:16] - x_ref[:, :FACE], 0.0)
    gabove = jnp.where(layer < layers - 1, above[8:16] - x_ref[:, width - FACE :], 0.0)
    gbelow_ref[...] = gbelow
    gabove_ref[...] = gabove
    h = h_ref[...] - spread(valid * far, onehot_ref[...])
    first = h[:, :FACE] - below[:8]
    last = h[:, width - FACE :] - above[:8]
    g = jnp.concatenate([first, h[:, FACE : width - FACE], last], axis=1)
    g_ref[...] = g
    jumps = valid * gown * (gown - gfar)
    terms = first * (first - gbelow) + last * (last - gabove) + jumps[:, :LANES] + jumps[:, LANES:]
    square = lane_sum(g * g)
    image = dense(g, high_ref, low_ref, arrive=arrive)
    curvature = lane_sum(terms) + lane_sum(g * image)
    lane = lax.broadcasted_iota(jnp.int32, (8, LANES), 1)
    row = lax.broadcasted_iota(jnp.int32, (8, LANES), 0)
    line = jnp.where(lane == row, square, 0.0) + jnp.where(lane == row + 8, curvature, 0.0)
    line = jnp.sum(line, axis=0, keepdims=True)
    short = lax.broadcasted_iota(jnp.int32, (1, LANES), 1)
    for r in range(ROUNDS):
        name = jnp.full((1, LANES), partners_ref[0, r], jnp.int32).astype(F32)
        line = jnp.where(short == NAMES + r, name, line)
    all_ref[...] = jnp.broadcast_to(line, all_ref.shape)


def local_sums(g, high_ref, low_ref):
    width = g.shape[1]
    first, last = g[:, :FACE], g[:, width - FACE :]
    square = lane_sum(g * g)
    curvature = lane_sum(g * dense(g, high_ref, low_ref)) + lane_sum(first * first + last * last)
    lane = lax.broadcasted_iota(jnp.int32, (8, LANES), 1)
    return jnp.where(lane == SQUARE, square, jnp.where(lane == CURVATURE, curvature, 0.0))


def add_pairs(sums_ref, g_ref, gown_ref, valid_ref, below_ref, out_ref):
    own = valid_ref[...] * gown_ref[...]
    squares = own * own
    pairs = g_ref[:, :FACE] * below_ref[...]
    terms = squares[:, :LANES] + squares[:, LANES:] - 2.0 * pairs
    lane = lax.broadcasted_iota(jnp.int32, (8, LANES), 1)
    out_ref[...] = sums_ref[...] + jnp.where(lane == CURVATURE, lane_sum(terms), 0.0)


def announce(sums_ref, keep_ref, swapped_ref, out_ref):
    parcel = jnp.concatenate([keep_ref[...] + sums_ref[...], swapped_ref[...]], axis=0)
    out_ref[...] = jnp.broadcast_to(parcel[None], out_ref.shape)


def layer_sums(table_ref, in_ref, g_ref, out_ref, *gfar_refs):
    plan = table_ref[0, HALF * in_ref.shape[0]]
    core = lax.rem(plan, 2)
    for gfar_ref in gfar_refs:
        gfar_ref[...] = half_of(in_ref, table_ref, plan)
    products = sums = jnp.zeros((8, LANES), F32)
    for p in range(in_ref.shape[0]):
        near = in_ref[p + core if p % 2 == 0 else p - core]
        sums = sums + near
        products = products + near * half_of(in_ref, table_ref, p)
    lane = lax.broadcasted_iota(jnp.int32, (8, LANES), 1)
    sums = sums - jnp.where(lane == CURVATURE, lane_sum(products), 0.0)
    if gfar_refs:
        sibling = half_of(in_ref, table_ref, plan + 1 - 2 * core)
        sums = jnp.concatenate([jnp.where(lane < SQUARE, sibling, sums), g_ref[:, :FACE]], axis=1)
    out_ref[...] = jnp.broadcast_to(sums[None], out_ref.shape)


def step_of(in_ref):
    total = in_ref[0, :, :LANES]
    for member in range(1, in_ref.shape[0]):
        total = total + in_ref[member, :, :LANES]
    square = total[:, SQUARE : SQUARE + 1]
    curvature = total[:, CURVATURE : CURVATURE + 1]
    return (square + 1e-6) / (curvature + 1e-6)


def moved(x, g, step, contact):
    out = x - step * g
    return jnp.where(contact == 1, jnp.maximum(out, 0.0), out)


def first_step(in_ref):
    line = jnp.sum(in_ref[...], axis=0, keepdims=True)
    line = jnp.broadcast_to(line, (8, LANES))
    lane = lax.broadcasted_iota(jnp.int32, (8, LANES), 1)
    row = lax.broadcasted_iota(jnp.int32, (8, LANES), 0)
    square = lane_sum(jnp.where(lane == row, line, 0.0))
    curvature = lane_sum(jnp.where(lane == row + 8, line, 0.0))
    return (square + 1e-6) / (curvature + 1e-6)


def chosen(in_ref, mask, columns):
    total = jnp.zeros((8, LANES), F32)
    for member in range(in_ref.shape[0]):
        total = jnp.where(mask[member : member + 1] == 1.0, in_ref[member, :, columns], total)
    return total


def first_face(in_ref, gabove_ref, *refs):
    face_by(first_step(in_ref), gabove_ref[...], *refs)


def next_face(in_ref, masks_ref, *refs):
    face_by(step_of(in_ref), chosen(in_ref, masks_ref[0], slice(LANES, None)), *refs)


def face_by(step, gabove, x_ref, g_ref, contact_ref, load_ref, above_ref, high_ref, low_ref,
            x_out, last_out, step_out, *above_outs):
    x = moved(x_ref[...], g_ref[...], step, contact_ref[...])
    x_out[...] = x
    step_out[...] = jnp.broadcast_to(step, step_out.shape)
    above = moved(above_ref[:8], gabove, step, above_ref[8:])
    for above_out in above_outs:
        above_out[...] = jnp.concatenate([above, above_ref[8:]], axis=0)
    at = slice(x.shape[1] - FACE, x.shape[1])
    last_out[...] = dense(x, high_ref, low_ref, at) - load_ref[:, at] + (x[:, at] - above)


def first_rest(in_ref, masks_ref, gfar_ref, *refs):
    *refs, table_ref = refs
    plans = in_ref.shape[0] * 2 // masks_ref.shape[1]
    lines = in_ref[pl.ds(0, plans, stride=in_ref.shape[0] // plans), :]
    even = masks_ref[2, :1] == 0.0
    names = jnp.where(
        even, pltpu.roll(lines, LANES - NAMES, 1), pltpu.roll(lines, LANES - NAMES - HALF, 1)
    ).astype(jnp.int32)
    names = jnp.where(even, names, names + 1 - 2 * (names & 1)).astype(F32)
    lane = lax.broadcasted_iota(jnp.int32, (plans, LANES), 1)
    plan = lax.broadcasted_iota(jnp.int32, (plans, LANES), 0)
    table = jnp.zeros((plans, LANES), F32)
    for r in range(HALF):
        table = jnp.where(lane == HALF * plan + r, names[:, r : r + 1], table)
    table = jnp.sum(table, axis=0, keepdims=True)
    table = jnp.where(lane[:1] == HALF * plans, masks_ref[3, :1], table)
    table_ref[...] = table.astype(jnp.int32)
    rest_by(gfar_ref[...], masks_ref, *refs)


def next_rest(in_ref, masks_ref, half_ref, *refs):
    lane = lax.broadcasted_iota(jnp.int32, (8, LANES), 1)
    other = chosen(in_ref, masks_ref[1], slice(LANES))
    half, other = half_ref[...], jnp.where(lane < SQUARE, other, 0.0)
    even = masks_ref[2, :1] == 0.0
    rest_by(
        jnp.concatenate([jnp.where(even, half, other), jnp.where(even, other, half)], axis=1),
        masks_ref, *refs,
    )


def rest_by(gfar, masks_ref, step_ref, x_ref, last_ref, load_ref, own_ref, gown_ref, far_ref,
            below_ref, gbelow_ref, valid_ref, onehot_ref, high_ref, low_ref,
            g_out, gown_out, sums_out, keep_out, give_out, *halo_outs):
    step, x = step_ref[:, :1], x_ref[...]
    inner = x.shape[1] - FACE
    halo = []
    for held_ref, slope in ((own_ref, gown_ref[...]), (far_ref, gfar), (below_ref, gbelow_ref[...])):
        halo.append(moved(held_ref[:8], slope, step, held_ref[8:]))
    for held_ref, value, held_out in zip((own_ref, far_ref, below_ref), halo, halo_outs):
        held_out[...] = jnp.concatenate([value, held_ref[8:]], axis=0)
    own, far, below = halo
    onehot = onehot_ref[...]
    jumps = spread(valid_ref[...] * (own - far), onehot)
    total = dense(x, high_ref, low_ref, slice(inner)) + jumps[:, :inner] - load_ref[:, :inner]
    head = total[:, :FACE] + (x[:, :FACE] - below)
    g = jnp.concatenate([head, total[:, FACE:], last_ref[...]], axis=1)
    g_out[...] = g
    gown = pick(g, onehot)[0]
    gown_out[...] = gown
    jumps = valid_ref[...] * gown
    even = masks_ref[2, :1] == 0.0
    keep_out[...] = jnp.where(even, jumps[:, :LANES], jumps[:, LANES:])
    give_out[...] = jnp.where(even, jumps[:, LANES:], jumps[:, :LANES])
    sums_out[...] = local_sums(g, high_ref, low_ref)


def finish(in_ref, x_ref, g_ref, contact_ref, x_out, g_out):
    g = g_ref[...]
    g_out[...] = g
    x_out[...] = moved(x_ref[...], g, step_of(in_ref), contact_ref[...])


def swap(outgoing, axis, groups=None):
    return lax.all_to_all(
        outgoing, axis, split_axis=0, concat_axis=0, tiled=True, axis_index_groups=groups
    )


def lift(face, step):
    layers = lax.axis_size("layer")
    return lax.ppermute(
        face, "layer", [(i, i + step) for i in range(layers) if 0 <= i + step < layers]
    )


def shards(dual_block, start, load, partners, jump_rows, counts, contact):
    block, x, target = dual_block[0, 0], start[0, 0], load[0, 0]
    rows, amounts, flags = jump_rows.reshape(ROUNDS, 1, JR), counts[0], contact[0]
    loads, width = x.shape
    plans, layers = lax.axis_size("plan"), lax.axis_size("layer")
    field, jump, face = shape(loads, width), shape(loads, JW), shape(loads, FACE)
    jump2, face2, face3 = shape(2 * loads, JW), shape(2 * loads, FACE), shape(3 * loads, FACE)
    flops = 4 * 16 * width * width
    position = jnp.stack([lax.axis_index("layer"), layers, lax.axis_index("plan")])
    position = position.astype(jnp.int32).reshape(1, 3)
    amounts, position = lax.optimization_barrier((amounts, position))
    cores = [list(range(core, plans, 2)) for core in range(2)]
    columns = [
        [(chip + core) * layers + layer for layer in range(layers) for core in range(2)]
        for chip in range(0, plans, 2)
    ]
    half_shape = shape(width, width, dtype=BF16)
    held = pltpu.VMEM((width, width), F32)
    chunk_sems = pltpu.SemaphoreType.DMA((CHUNKS,))

    onehot, valid, own, hown, h, out, first, last, high = call(
        prepare, "prepare",
        (shape(width, JW, dtype=BF16), jump, jump2, jump, field, shape(plans, loads, LANES), face3, face3,
         half_shape),
        [HBM] * 7, 16, flops, 4 * width * width,
        [
            held, pltpu.VMEM((width, width), BF16), pltpu.VMEM(x.shape, F32), pltpu.VMEM(target.shape, F32),
            pltpu.VMEM(flags.shape, jnp.int32), pltpu.VMEM(rows.shape, jnp.int32),
            pltpu.SMEM(partners.shape, jnp.int32), pltpu.SMEM(amounts.shape, jnp.int32),
            chunk_sems, pltpu.SemaphoreType.DMA((6,)),
        ],
    )(*(pltpu.with_memory_space_constraint(a, pltpu.HBM) for a in (block, x, target, flags, rows, partners, amounts)))
    incoming = swap(out, "plan")
    below, above = lift(last, 1), lift(first, -1)
    g, gown, far, gfar, below, gbelow, above, gabove, out, masks, low = call(
        first_gradient, "first_gradient",
        (field, jump, jump2, jump, face2, face, face2, face,
         shape(plans * layers, LANES), shape(4, 2 * layers, LANES), half_shape),
        [SMEM] * 2 + [HBM] + [VMEM] * 10, 12, flops, 4 * width * width, [held, chunk_sems],
    )(partners, position, pltpu.with_memory_space_constraint(block, pltpu.HBM), high, x, h, own, hown, incoming, below, above, valid, onehot)
    incoming = swap(out, ("plan", "layer"))

    early = (field, face, face, face2)
    x, last, step, above = call(
        first_face, "first_face", early, [VMEM] * 9, 12, flops // 8, width * width // 2,
    )(incoming, gabove, x, g, flags, target, above, high, low)
    late = (field, jump, face, face, face, jump2, jump2, face2)
    below_next = lift(last, 1)
    g, gown, sums, keep, give, own, far, below, table = call(
        first_rest, "first_rest", late + (shape(1, LANES, dtype=jnp.int32),),
        [VMEM] * 16, 12, 2 * flops, 8 * width * width,
    )(incoming, masks, gfar, step, x, last, target, own, gown, far, below, gbelow, valid, onehot, high, low)

    for iteration in range(1, ITERS):
        gbelow = below_next
        sums = call(add_pairs, "add_pairs", face, [VMEM] * 5, 8)(sums, g, gown, valid, gbelow)
        swapped = lax.ppermute(give, "plan", [(p, p ^ 1) for p in range(plans)])
        out = call(announce, "announce", shape(plans // 2, 2 * loads, LANES), [VMEM] * 3, 8)(
            sums, keep, swapped
        )
        everyone = swap(out, "plan", cores).reshape(plans, loads, LANES)
        ending = iteration == ITERS - 1
        parcel = shape(2 * layers, loads, LANES if ending else LANES + FACE)
        out, *half = call(
            layer_sums, "layer_sums", (parcel,) + (() if ending else (shape(loads, LANES),)),
            [SMEM] + [VMEM] * 2, 8,
        )(table, everyone, g)
        incoming = swap(out, ("plan", "layer"), columns)
        if ending:
            x, g = call(finish, "finish", (field, field), [VMEM] * 4, 8)(incoming, x, g, flags)
            break
        x, last, step, *above = call(
            next_face, "next_face", early[:3] if iteration == ITERS - 2 else early, [VMEM] * 9, 12, flops // 8, width * width // 2,
        )(incoming, masks, x, g, flags, target, above, high, low)
        below_next = lift(last, 1)
        g, gown, sums, keep, give, *halo = call(
            next_rest, "next_rest", late[:5] if iteration == ITERS - 2 else late,
            [VMEM] * 16, 12, 2 * flops, 8 * width * width,
        )(incoming, masks, *half, step, x, last, target, own, gown, far, below, gbelow,
          valid, onehot, high, low)
        (above,), (own, far, below) = above or (None,), halo or (None,) * 3
    return x[None, None], g[None, None]


def solution(mesh):
    in_specs = (
        P("layer", "plan", None, None),
        P("layer", "plan", None, None),
        P("layer", "plan", None, None),
        P("plan", None),
        P("layer", "plan", None, None),
        P("layer", "plan", None),
        P("layer", "plan", None),
    )
    out_specs = (P("layer", "plan", None, None), P("layer", "plan", None, None))
    return jax.shard_map(shards, mesh=mesh, in_specs=in_specs, out_specs=out_specs, check_vma=False)
```

```python
import jax
import jax.numpy as jnp
from jax import lax
from jax.experimental import pallas as pl
from jax.experimental.pallas import tpu as pltpu
from jax.sharding import PartitionSpec as P

FACE = 128
JR = 32
ROUNDS = 6
ITERS = 4
LANES = 128
HALF = 3
JW = 2 * LANES
STRIP = 32
CHUNKS = 8
NAMES = 16
SQUARE, CURVATURE = HALF * JR, HALF * JR + 1
F32 = jnp.float32
BF16 = jnp.bfloat16

VMEM = pl.BlockSpec(memory_space=pltpu.VMEM)
SMEM = pl.BlockSpec(memory_space=pltpu.SMEM)
HBM = pl.BlockSpec(memory_space=pltpu.HBM)


def shape(*dims, dtype=F32):
    return jax.ShapeDtypeStruct(dims, dtype)


def call(body, name, outs, specs, limit, flops=0, traffic=0, scratch=()):
    return pl.pallas_call(
        body,
        name=name,
        out_shape=outs,
        in_specs=specs,
        scratch_shapes=scratch,
        out_specs=jax.tree.map(lambda _: VMEM, outs),
        compiler_params=pltpu.CompilerParams(vmem_limit_bytes=limit * 2**20),
        cost_estimate=pl.CostEstimate(flops=flops, bytes_accessed=traffic, transcendentals=0),
    )


def pieces(value, count):
    parts = []
    for _ in range(count):
        part = value.astype(BF16).astype(F32)
        parts.append(part)
        value = value - part
    return parts


def lane_sum(value):
    return jnp.sum(value, axis=1, keepdims=True)


def dense(field, high_ref, low_ref, columns=slice(None), arrive=None):
    lhs = jnp.concatenate(pieces(field, 2), axis=0).astype(BF16)
    total = 0.0
    for half_ref in (high_ref, low_ref):
        chunks = 1 if arrive is None else CHUNKS
        depth = field.shape[1] // chunks
        for chunk in range(chunks):
            if chunks > 1 and half_ref is low_ref:
                arrive(chunk)
            at = slice(chunk * depth, (chunk + 1) * depth)
            total = total + jnp.dot(lhs[:, at], half_ref[at, columns], preferred_element_type=F32)
    return total[:8] + total[8:]


def pick(field, onehot, *extra):
    lhs = jnp.concatenate(pieces(field, 3) + list(extra), axis=0).astype(BF16)
    out = jnp.dot(lhs, onehot, preferred_element_type=F32)
    return [out[:8] + out[8:16] + out[16:24]] + [
        out[24 + 8 * i : 32 + 8 * i] for i in range(len(extra))
    ]


def spread(jumps, onehot):
    lhs = jnp.concatenate(pieces(jumps, 3), axis=0).astype(BF16)
    out = lax.dot_general(lhs, onehot, (((1,), (1,)), ((), ())), preferred_element_type=F32)
    return out[:8] + out[8:16] + out[16:24]


def half_of(in_ref, table_ref, plan):
    place = lax.broadcasted_iota(jnp.int32, (8, LANES), 1) // JR
    total = jnp.zeros((8, LANES), F32)
    for r in range(HALF):
        total = jnp.where(place == r, in_ref[table_ref[0, HALF * plan + r]], total)
    return total


def stream_dense(field, block_ref, rows_ref, sems, high_ref, low_ref):
    lhs = jnp.concatenate(pieces(field, 2), axis=0).astype(BF16)
    depth = rows_ref.shape[0] // CHUNKS
    total = jnp.zeros((lhs.shape[0], rows_ref.shape[1]), F32)
    for chunk in range(CHUNKS):
        at = slice(chunk * depth, (chunk + 1) * depth)
        chunk_copy(block_ref, rows_ref, sems, chunk).wait()
        for first in range(at.start, at.stop, STRIP):
            strip = slice(first, first + STRIP)
            rows = rows_ref[strip, :]
            high = rows.astype(BF16)
            high_ref[strip, :] = high
            low_ref[strip, :] = (rows - high.astype(F32)).astype(BF16)
        total = total + jnp.dot(lhs[:, at], high_ref[at, :], preferred_element_type=F32)
        total = total + jnp.dot(lhs[:, at], low_ref[at, :], preferred_element_type=F32)
    return total[:8] + total[8:]


def chunk_copy(source_ref, target_ref, sems, chunk):
    depth = source_ref.shape[0] // CHUNKS
    at = pl.ds(chunk * depth, depth)
    return pltpu.make_async_copy(source_ref.at[at, :], target_ref.at[at, :], sems.at[chunk])


def prepare(block_ref, x_hbm, load_hbm, contact_hbm, rows_hbm, partners_hbm, counts_hbm,
            onehot_ref, valid_ref, own_ref, hown_ref, h_ref, out_ref, first_ref, last_ref, high_ref,
            held_ref, low_ref, x_ref, load_ref, contact_ref, rows_ref, partners_ref, counts_ref,
            sems, more_sems):
    small = [
        pltpu.make_async_copy(source, target, more_sems.at[i])
        for i, (source, target) in enumerate((
            (rows_hbm, rows_ref), (counts_hbm, counts_ref), (x_hbm, x_ref),
            (contact_hbm, contact_ref), (partners_hbm, partners_ref), (load_hbm, load_ref),
        ))
    ]
    for copy in small:
        copy.start()
    for chunk in range(CHUNKS):
        chunk_copy(block_ref, held_ref, sems, chunk).start()
    for copy in small:
        copy.wait()
    x = x_ref[...]
    width = x.shape[1]
    spare = [jnp.full((1, LANES - HALF * JR), -1, jnp.int32)]
    rows = [rows_ref[r] for r in range(ROUNDS)]
    rows = jnp.concatenate(rows[:HALF] + spare + rows[HALF:] + spare, axis=1)
    hit = lax.broadcasted_iota(jnp.int32, (width, JW), 0) == rows
    onehot_ref[...] = jnp.where(hit, 1.0, 0.0).astype(BF16)
    lane = lax.broadcasted_iota(jnp.int32, (8, JW), 1)
    valid = jnp.zeros((8, JW), F32)
    for r in range(ROUNDS):
        start = r // HALF * LANES + r % HALF * JR
        inside = (lane >= start) & (lane < start + counts_ref[0, r])
        valid = jnp.where(inside, 1.0, valid)
    valid_ref[...] = valid
    contact = jnp.broadcast_to(jnp.where(contact_ref[...] == 1, 1.0, 0.0), x.shape)
    own, own_contact = pick(x, onehot_ref[...], contact)
    own_ref[...] = jnp.concatenate([own, own_contact], axis=0)
    position = lax.broadcasted_iota(jnp.int32, x.shape, 1)
    edge = (position < FACE) | (position >= width - FACE)
    h = spread(valid * own, onehot_ref[...]) + jnp.where(edge, x, 0.0) - load_ref[...]
    h = h + stream_dense(x, block_ref, held_ref, sems, high_ref, low_ref)
    h_ref[...] = h
    (hown,) = pick(h, onehot_ref[...])
    hown_ref[...] = hown
    out_ref[...] = jnp.zeros_like(out_ref)
    place = lax.broadcasted_iota(jnp.int32, (8, LANES), 1) // JR
    for r in range(ROUNDS):
        group, slot = divmod(r, HALF)
        at = slice(group * LANES, (group + 1) * LANES)
        parcel = jnp.zeros((8, LANES), F32)
        for i, jump in enumerate((own, hown, own_contact)):
            block = pltpu.roll(jump[:, at], (i * JR) % LANES, 1) if i else jump[:, at]
            parcel = jnp.where(place == (slot + i) % (LANES // JR), block, parcel)
        out_ref[partners_ref[0, r]] = parcel
    both = jnp.concatenate([x, h, contact], axis=0)
    first_ref[...] = both[:, :FACE]
    last_ref[...] = both[:, width - FACE :]


def first_gradient(partners_ref, where_ref, block_ref, high_ref, x_ref, h_ref, own_ref, hown_ref, in_ref,
                   below_in, above_in, valid_ref, onehot_ref,
                   g_ref, gown_ref, far_ref, gfar_ref, below_ref, gbelow_ref, above_ref, gabove_ref,
                   all_ref, masks_ref, low_ref, held_ref, sems):
    for chunk in range(CHUNKS):
        chunk_copy(block_ref, held_ref, sems, chunk).start()

    def arrive(chunk):
        chunk_copy(block_ref, held_ref, sems, chunk).wait()
        depth = held_ref.shape[0] // CHUNKS
        for first in range(chunk * depth, (chunk + 1) * depth, STRIP):
            strip = slice(first, first + STRIP)
            rest = held_ref[strip, :] - high_ref[strip, :].astype(F32)
            low_ref[strip, :] = rest.astype(BF16)

    width = x_ref.shape[1]
    place = lax.broadcasted_iota(jnp.int32, (8, LANES), 1) // JR
    parts = [[jnp.zeros((8, LANES), F32)] * 2 for _ in range(3)]
    for r in range(ROUNDS):
        group, slot = divmod(r, HALF)
        parcel = in_ref[partners_ref[0, r]]
        for i in range(3):
            block = pltpu.roll(parcel, LANES - i * JR, 1) if i else parcel
            parts[i][group] = jnp.where(place == slot, block, parts[i][group])
    far, hfar, far_contact = (jnp.concatenate(part, axis=1) for part in parts)
    valid = valid_ref[...]
    own = own_ref[:8]
    far_ref[...] = jnp.concatenate([far, far_contact], axis=0)
    gown = hown_ref[...] - valid * far
    gfar = hfar - valid * own
    gown_ref[...] = gown
    gfar_ref[...] = gfar
    below, above = below_in[...], above_in[...]
    below_ref[...] = jnp.concatenate([below[:8], below[16:]], axis=0)
    above_ref[...] = jnp.concatenate([above[:8], above[16:]], axis=0)
    layer, layers, core = where_ref[0, 0], where_ref[0, 1], lax.rem(where_ref[0, 2], 2)
    member = lax.broadcasted_iota(jnp.int32, (masks_ref.shape[1], LANES), 0)
    masks_ref[0] = jnp.where(member == 2 * (layer + 1) + core, 1.0, 0.0)
    masks_ref[1] = jnp.where(member == 2 * layer + 1 - core, 1.0, 0.0)
    masks_ref[2] = jnp.where(member >= 0, core, 0).astype(F32)
    masks_ref[3] = jnp.where(member >= 0, where_ref[0, 2], 0).astype(F32)
    gbelow = jnp.where(layer > 0, below[8:16] - x_ref[:, :FACE], 0.0)
    gabove = jnp.where(layer < layers - 1, above[8:16] - x_ref[:, width - FACE :], 0.0)
    gbelow_ref[...] = gbelow
    gabove_ref[...] = gabove
    h = h_ref[...] - spread(valid * far, onehot_ref[...])
    first = h[:, :FACE] - below[:8]
    last = h[:, width - FACE :] - above[:8]
    g = jnp.concatenate([first, h[:, FACE : width - FACE], last], axis=1)
    g_ref[...] = g
    jumps = valid * gown * (gown - gfar)
    terms = first * (first - gbelow) + last * (last - gabove) + jumps[:, :LANES] + jumps[:, LANES:]
    square = lane_sum(g * g)
    image = dense(g, high_ref, low_ref, arrive=arrive)
    curvature = lane_sum(terms) + lane_sum(g * image)
    lane = lax.broadcasted_iota(jnp.int32, (8, LANES), 1)
    row = lax.broadcasted_iota(jnp.int32, (8, LANES), 0)
    line = jnp.where(lane == row, square, 0.0) + jnp.where(lane == row + 8, curvature, 0.0)
    line = jnp.sum(line, axis=0, keepdims=True)
    short = lax.broadcasted_iota(jnp.int32, (1, LANES), 1)
    for r in range(ROUNDS):
        name = jnp.full((1, LANES), partners_ref[0, r], jnp.int32).astype(F32)
        line = jnp.where(short == NAMES + r, name, line)
    all_ref[...] = jnp.broadcast_to(line, all_ref.shape)


def local_sums(g, high_ref, low_ref):
    width = g.shape[1]
    first, last = g[:, :FACE], g[:, width - FACE :]
    square = lane_sum(g * g)
    curvature = lane_sum(g * dense(g, high_ref, low_ref)) + lane_sum(first * first + last * last)
    lane = lax.broadcasted_iota(jnp.int32, (8, LANES), 1)
    return jnp.where(lane == SQUARE, square, jnp.where(lane == CURVATURE, curvature, 0.0))


def add_pairs(sums_ref, g_ref, gown_ref, valid_ref, below_ref, out_ref):
    own = valid_ref[...] * gown_ref[...]
    squares = own * own
    pairs = g_ref[:, :FACE] * below_ref[...]
    terms = squares[:, :LANES] + squares[:, LANES:] - 2.0 * pairs
    lane = lax.broadcasted_iota(jnp.int32, (8, LANES), 1)
    out_ref[...] = sums_ref[...] + jnp.where(lane == CURVATURE, lane_sum(terms), 0.0)


def announce(sums_ref, keep_ref, swapped_ref, out_ref):
    parcel = jnp.concatenate([keep_ref[...] + sums_ref[...], swapped_ref[...]], axis=0)
    out_ref[...] = jnp.broadcast_to(parcel[None], out_ref.shape)


def layer_sums(table_ref, in_ref, g_ref, out_ref, *gfar_refs):
    plan = table_ref[0, HALF * in_ref.shape[0]]
    core = lax.rem(plan, 2)
    for gfar_ref in gfar_refs:
        gfar_ref[...] = half_of(in_ref, table_ref, plan)
    products = sums = jnp.zeros((8, LANES), F32)
    for p in range(in_ref.shape[0]):
        near = in_ref[p + core if p % 2 == 0 else p - core]
        sums = sums + near
        products = products + near * half_of(in_ref, table_ref, p)
    lane = lax.broadcasted_iota(jnp.int32, (8, LANES), 1)
    sums = sums - jnp.where(lane == CURVATURE, lane_sum(products), 0.0)
    if gfar_refs:
        sibling = half_of(in_ref, table_ref, plan + 1 - 2 * core)
        sums = jnp.concatenate([jnp.where(lane < SQUARE, sibling, sums), g_ref[:, :FACE]], axis=1)
    out_ref[...] = jnp.broadcast_to(sums[None], out_ref.shape)


def step_of(in_ref):
    total = in_ref[0, :, :LANES]
    for member in range(1, in_ref.shape[0]):
        total = total + in_ref[member, :, :LANES]
    square = total[:, SQUARE : SQUARE + 1]
    curvature = total[:, CURVATURE : CURVATURE + 1]
    return (square + 1e-6) / (curvature + 1e-6)


def moved(x, g, step, contact):
    out = x - step * g
    return jnp.where(contact == 1, jnp.maximum(out, 0.0), out)


def first_step(in_ref):
    line = jnp.sum(in_ref[...], axis=0, keepdims=True)
    line = jnp.broadcast_to(line, (8, LANES))
    lane = lax.broadcasted_iota(jnp.int32, (8, LANES), 1)
    row = lax.broadcasted_iota(jnp.int32, (8, LANES), 0)
    square = lane_sum(jnp.where(lane == row, line, 0.0))
    curvature = lane_sum(jnp.where(lane == row + 8, line, 0.0))
    return (square + 1e-6) / (curvature + 1e-6)


def chosen(in_ref, mask, columns):
    total = jnp.zeros((8, LANES), F32)
    for member in range(in_ref.shape[0]):
        total = jnp.where(mask[member : member + 1] == 1.0, in_ref[member, :, columns], total)
    return total


def first_face(in_ref, gabove_ref, *refs):
    face_by(first_step(in_ref), gabove_ref[...], *refs)


def next_face(in_ref, masks_ref, *refs):
    face_by(step_of(in_ref), chosen(in_ref, masks_ref[0], slice(LANES, None)), *refs)


def face_by(step, gabove, x_ref, g_ref, contact_ref, load_ref, above_ref, high_ref, low_ref,
            x_out, last_out, step_out, *above_outs):
    x = moved(x_ref[...], g_ref[...], step, contact_ref[...])
    x_out[...] = x
    step_out[...] = jnp.broadcast_to(step, step_out.shape)
    above = moved(above_ref[:8], gabove, step, above_ref[8:])
    for above_out in above_outs:
        above_out[...] = jnp.concatenate([above, above_ref[8:]], axis=0)
    at = slice(x.shape[1] - FACE, x.shape[1])
    last_out[...] = dense(x, high_ref, low_ref, at) - load_ref[:, at] + (x[:, at] - above)


def first_rest(in_ref, masks_ref, gfar_ref, *refs):
    *refs, table_ref = refs
    plans = in_ref.shape[0] * 2 // masks_ref.shape[1]
    lines = in_ref[pl.ds(0, plans, stride=in_ref.shape[0] // plans), :]
    even = masks_ref[2, :1] == 0.0
    names = jnp.where(
        even, pltpu.roll(lines, LANES - NAMES, 1), pltpu.roll(lines, LANES - NAMES - HALF, 1)
    ).astype(jnp.int32)
    names = jnp.where(even, names, names + 1 - 2 * (names & 1)).astype(F32)
    lane = lax.broadcasted_iota(jnp.int32, (plans, LANES), 1)
    plan = lax.broadcasted_iota(jnp.int32, (plans, LANES), 0)
    table = jnp.zeros((plans, LANES), F32)
    for r in range(HALF):
        table = jnp.where(lane == HALF * plan + r, names[:, r : r + 1], table)
    table = jnp.sum(table, axis=0, keepdims=True)
    table = jnp.where(lane[:1] == HALF * plans, masks_ref[3, :1], table)
    table_ref[...] = table.astype(jnp.int32)
    rest_by(gfar_ref[...], masks_ref, *refs)


def next_rest(in_ref, masks_ref, half_ref, *refs):
    lane = lax.broadcasted_iota(jnp.int32, (8, LANES), 1)
    other = chosen(in_ref, masks_ref[1], slice(LANES))
    half, other = half_ref[...], jnp.where(lane < SQUARE, other, 0.0)
    even = masks_ref[2, :1] == 0.0
    rest_by(
        jnp.concatenate([jnp.where(even, half, other), jnp.where(even, other, half)], axis=1),
        masks_ref, *refs,
    )


def rest_by(gfar, masks_ref, step_ref, x_ref, last_ref, load_ref, own_ref, gown_ref, far_ref,
            below_ref, gbelow_ref, valid_ref, onehot_ref, high_ref, low_ref,
            g_out, gown_out, sums_out, keep_out, give_out, *halo_outs):
    step, x = step_ref[:, :1], x_ref[...]
    inner = x.shape[1] - FACE
    halo = []
    for held_ref, slope in ((own_ref, gown_ref[...]), (far_ref, gfar), (below_ref, gbelow_ref[...])):
        halo.append(moved(held_ref[:8], slope, step, held_ref[8:]))
    for held_ref, value, held_out in zip((own_ref, far_ref, below_ref), halo, halo_outs):
        held_out[...] = jnp.concatenate([value, held_ref[8:]], axis=0)
    own, far, below = halo
    onehot = onehot_ref[...]
    jumps = spread(valid_ref[...] * (own - far), onehot)
    total = dense(x, high_ref, low_ref, slice(inner)) + jumps[:, :inner] - load_ref[:, :inner]
    head = total[:, :FACE] + (x[:, :FACE] - below)
    g = jnp.concatenate([head, total[:, FACE:], last_ref[...]], axis=1)
    g_out[...] = g
    gown = pick(g, onehot)[0]
    gown_out[...] = gown
    jumps = valid_ref[...] * gown
    even = masks_ref[2, :1] == 0.0
    keep_out[...] = jnp.where(even, jumps[:, :LANES], jumps[:, LANES:])
    give_out[...] = jnp.where(even, jumps[:, LANES:], jumps[:, :LANES])
    sums_out[...] = local_sums(g, high_ref, low_ref)


def finish(in_ref, x_ref, g_ref, contact_ref, x_out, g_out):
    g = g_ref[...]
    g_out[...] = g
    x_out[...] = moved(x_ref[...], g, step_of(in_ref), contact_ref[...])


def swap(outgoing, axis, groups=None):
    return lax.all_to_all(
        outgoing, axis, split_axis=0, concat_axis=0, tiled=True, axis_index_groups=groups
    )


def lift(face, step):
    layers = lax.axis_size("layer")
    return lax.ppermute(
        face, "layer", [(i, i + step) for i in range(layers) if 0 <= i + step < layers]
    )


def shards(dual_block, start, load, partners, jump_rows, counts, contact):
    block, x, target = dual_block[0, 0], start[0, 0], load[0, 0]
    rows, amounts, flags = jump_rows.reshape(ROUNDS, 1, JR), counts[0], contact[0]
    loads, width = x.shape
    plans, layers = lax.axis_size("plan"), lax.axis_size("layer")
    field, jump, face = shape(loads, width), shape(loads, JW), shape(loads, FACE)
    jump2, face2, face3 = shape(2 * loads, JW), shape(2 * loads, FACE), shape(3 * loads, FACE)
    flops = 4 * 16 * width * width
    position = jnp.stack([lax.axis_index("layer"), layers, lax.axis_index("plan")])
    position = position.astype(jnp.int32).reshape(1, 3)
    amounts, position = lax.optimization_barrier((amounts, position))
    cores = [list(range(core, plans, 2)) for core in range(2)]
    columns = [
        [(chip + core) * layers + layer for layer in range(layers) for core in range(2)]
        for chip in range(0, plans, 2)
    ]
    half_shape = shape(width, width, dtype=BF16)
    held = pltpu.VMEM((width, width), F32)
    chunk_sems = pltpu.SemaphoreType.DMA((CHUNKS,))

    onehot, valid, own, hown, h, out, first, last, high = call(
        prepare, "prepare",
        (shape(width, JW, dtype=BF16), jump, jump2, jump, field, shape(plans, loads, LANES), face3, face3,
         half_shape),
        [HBM] * 7, 16, flops, 4 * width * width,
        [
            held, pltpu.VMEM((width, width), BF16), pltpu.VMEM(x.shape, F32), pltpu.VMEM(target.shape, F32),
            pltpu.VMEM(flags.shape, jnp.int32), pltpu.VMEM(rows.shape, jnp.int32),
            pltpu.SMEM(partners.shape, jnp.int32), pltpu.SMEM(amounts.shape, jnp.int32),
            chunk_sems, pltpu.SemaphoreType.DMA((6,)),
        ],
    )(*(pltpu.with_memory_space_constraint(a, pltpu.HBM) for a in (block, x, target, flags, rows, partners, amounts)))
    incoming = swap(out, "plan")
    below, above = lift(last, 1), lift(first, -1)
    g, gown, far, gfar, below, gbelow, above, gabove, out, masks, low = call(
        first_gradient, "first_gradient",
        (field, jump, jump2, jump, face2, face, face2, face,
         shape(plans * layers, LANES), shape(4, 2 * layers, LANES), half_shape),
        [SMEM] * 2 + [HBM] + [VMEM] * 10, 12, flops, 4 * width * width, [held, chunk_sems],
    )(partners, position, pltpu.with_memory_space_constraint(block, pltpu.HBM), high, x, h, own, hown, incoming, below, above, valid, onehot)
    incoming = swap(out, ("plan", "layer"))

    early = (field, face, face, face2)
    x, last, step, above = call(
        first_face, "first_face", early, [VMEM] * 9, 12, flops // 8, width * width // 2,
    )(incoming, gabove, x, g, flags, target, above, high, low)
    late = (field, jump, face, face, face, jump2, jump2, face2)
    below_next = lift(last, 1)
    g, gown, sums, keep, give, own, far, below, table = call(
        first_rest, "first_rest", late + (shape(1, LANES, dtype=jnp.int32),),
        [VMEM] * 16, 12, 2 * flops, 8 * width * width,
    )(incoming, masks, gfar, step, x, last, target, own, gown, far, below, gbelow, valid, onehot, high, low)

    for iteration in range(1, ITERS):
        gbelow = below_next
        sums = call(add_pairs, "add_pairs", face, [VMEM] * 5, 8)(sums, g, gown, valid, gbelow)
        swapped = lax.ppermute(give, "plan", [(p, p ^ 1) for p in range(plans)])
        out = call(announce, "announce", shape(plans // 2, 2 * loads, LANES), [VMEM] * 3, 8)(
            sums, keep, swapped
        )
        everyone = swap(out, "plan", cores).reshape(plans, loads, LANES)
        ending = iteration == ITERS - 1
        parcel = shape(2 * layers, loads, LANES if ending else LANES + FACE)
        out, *half = call(
            layer_sums, "layer_sums", (parcel,) + (() if ending else (shape(loads, LANES),)),
            [SMEM] + [VMEM] * 2, 8,
        )(table, everyone, g)
        incoming = swap(out, ("plan", "layer"), columns)
        if ending:
            x, g = call(finish, "finish", (field, field), [VMEM] * 4, 8)(incoming, x, g, flags)
            break
        x, last, step, *above = call(
            next_face, "next_face", early[:3] if iteration == ITERS - 2 else early, [VMEM] * 9, 12, flops // 8, width * width // 2,
        )(incoming, masks, x, g, flags, target, above, high, low)
        below_next = lift(last, 1)
        g, gown, sums, keep, give, *halo = call(
            next_rest, "next_rest", late[:5] if iteration == ITERS - 2 else late,
            [VMEM] * 16, 12, 2 * flops, 8 * width * width,
        )(incoming, masks, *half, step, x, last, target, own, gown, far, below, gbelow,
          valid, onehot, high, low)
        (above,), (own, far, below) = above or (None,), halo or (None,) * 3
    return x[None, None], g[None, None]


def solution(mesh):
    in_specs = (
        P("layer", "plan", None, None),
        P("layer", "plan", None, None),
        P("layer", "plan", None, None),
        P("plan", None),
        P("layer", "plan", None, None),
        P("layer", "plan", None),
        P("layer", "plan", None),
    )
    out_specs = (P("layer", "plan", None, None), P("layer", "plan", None, None))
    return jax.shard_map(shards, mesh=mesh, in_specs=in_specs, out_specs=out_specs, check_vma=False)
```
